32 devices in a mesh: fsdp: 4 (over y, x), ctx: 8 (over z, core).
Axes of the slice: x: 2, y: 2, z: 4, core: 2. Of those that a mesh axis runs over, the one named last changes fastest.
Arguments:
- tokens: bfloat16 [8, 1024, 2048], P('fsdp', 'ctx'), may hold values from -6 to 6
- cotangent: bfloat16 [8, 1024, 2048], P('fsdp', 'ctx'), may hold values from -6 to 6
- lengths: int32 [8], P('fsdp'), may hold values from 256 to 1024, as said below
- buckets: int32 [2047], replicated, may hold values from 0 to 31, as said below
- norm1_gain: float32 [2048], P(('fsdp', 'ctx')), may hold values from 0.25 to 1.75
- rel_bias: float32 [1024], P(('fsdp', 'ctx')), may hold values from -4 to 4
- w_query: float32 [2048, 2048], P(('fsdp', 'ctx')), may hold values from -0.0625 to 0.0625
- w_key: float32 [2048, 2048], P(('fsdp', 'ctx')), may hold values from -0.0625 to 0.0625
- w_value: float32 [2048, 2048], P(('fsdp', 'ctx')), may hold values from -0.125 to 0.125
- w_attn_out: float32 [2048, 2048], P(('fsdp', 'ctx')), may hold values from -0.5 to 0.5
- norm2_gain: float32 [2048], P(('fsdp', 'ctx')), may hold values from 0.25 to 1.75
- w_gate: float32 [2048, 5120], P(('fsdp', 'ctx')), may hold values from -0.125 to 0.125
- w_up: float32 [2048, 5120], P(('fsdp', 'ctx')), may hold values from -0.125 to 0.125
- w_down: float32 [5120, 2048], P(('fsdp', 'ctx')), may hold values from -0.078125 to 0.078125
Outputs:
- out: bfloat16 [8, 1024, 2048], P('fsdp', 'ctx')
- grad_tokens: bfloat16 [8, 1024, 2048], P('fsdp', 'ctx')
- grad_norm1_gain: float32 [2048], P(('fsdp', 'ctx'))
- grad_rel_bias: float32 [1024], P(('fsdp', 'ctx'))
- grad_w_query: float32 [2048, 2048], P(('fsdp', 'ctx'))
- grad_w_key: float32 [2048, 2048], P(('fsdp', 'ctx'))
- grad_w_value: float32 [2048, 2048], P(('fsdp', 'ctx'))
- grad_w_attn_out: float32 [2048, 2048], P(('fsdp', 'ctx'))
- grad_norm2_gain: float32 [2048], P(('fsdp', 'ctx'))
- grad_w_gate: float32 [2048, 5120], P(('fsdp', 'ctx'))
- grad_w_up: float32 [2048, 5120], P(('fsdp', 'ctx'))
- grad_w_down: float32 [5120, 2048], P(('fsdp', 'ctx'))
The draws below stay inside these ranges and needn't reach their ends.
Inputs may be any that keep to these rules, and one draw needn't show every extreme that they name: `lengths`: of the 2 sequences of one fsdp index, one has all 1024 slots valid. `buckets`: entry r + 1023 is the bucket of r = key slot minus query slot: 0 for r = 0, -r for -8 < r < 0, 16 + r for 0 < r < 8; for |r| >= 8 it does not fall as |r| grows and lies in 8 to 15 for negative r, 24 to 31 for positive r.
All inputs are finite; a program needn't handle non-finite values.
Results may differ from the reference program's by a relative error of at most 0.018.
The reference program's roundings to bfloat16 on the way count: a program that leaves them out, or rounds other values in their place, can miss the bound.
Values may be sent and summed in bfloat16 or wider, within the bound.
A program may use at most 512 MiB of HBM per device.

```python
import math
import jax
import jax.numpy as jnp
from jax import lax

D = 2048
H = 32
NB = 32
FF = 5120
SEQS = 2
HD = 2048
LENGTH = 1024
SEQUENCES = 8


def draw_lengths(key, part):
    key = jax.random.fold_in(key, 5)
    pick_key, drawn_key = jax.random.split(key)
    groups = SEQUENCES // SEQS
    chosen = jax.random.randint(pick_key, (groups, 1), 0, SEQS)
    drawn_len = jax.random.randint(drawn_key, (groups, SEQS), LENGTH // 4, LENGTH + 1)
    slot_ids = jnp.arange(SEQS, dtype=jnp.int32)[None, :]
    return jnp.where(slot_ids == chosen, LENGTH, drawn_len).reshape(SEQUENCES).astype(jnp.int32)


def draw_buckets(key, part):
    key = jax.random.fold_in(key, 9)
    offsets = jnp.arange(2 * LENGTH - 1, dtype=jnp.int32) - (LENGTH - 1)
    distance = jnp.abs(offsets)
    cut_points = jnp.sort(jax.random.randint(key, (7,), 8, LENGTH))
    far_bucket = 8 + jnp.sum((distance[:, None] >= cut_points[None, :]).astype(jnp.int32), axis=1)
    base_bucket = jnp.where(distance < 8, distance, far_bucket)
    return jnp.where(offsets > 0, base_bucket + NB // 2, base_bucket).astype(jnp.int32)


def levels(rng, dims, pieces, smallest, high):
    def one(dim, shards_of):
        heights = jax.random.uniform(jax.random.fold_in(jax.random.fold_in(rng, 6), dim), (shards_of,), jnp.float32, smallest / len(pieces), high / len(pieces))
        return jnp.repeat(jnp.exp(heights), dims[dim] // shards_of).reshape((-1,) + (1,) * (len(dims) - dim - 1))

    gain = one(*pieces[0])
    for cut in pieces[1:]:
        gain = gain * one(*cut)
    return gain


def centred(key, extent, spread, reach, pieces=(), held_as=jnp.bfloat16):
    values = spread * jax.random.normal(key, extent, jnp.float32)
    if pieces:
        values = values * levels(key, extent, pieces, -0.22, 0.18)
    return jnp.clip(values, -reach, reach).astype(held_as)


def setup_inputs(seed: int = 0) -> dict:
    streams_of = jax.random.split(jax.random.key(seed), 15)
    return {
        "tokens": centred(streams_of[0], (SEQUENCES, LENGTH, D), 1.0, 6.0, ((0, 4), (1, 8))),
        "cotangent": centred(streams_of[1], (SEQUENCES, LENGTH, D), 1.0, 6.0, ((0, 4), (1, 8))),
        "lengths": draw_lengths(jax.random.fold_in(streams_of[14], 71), 0),
        "buckets": draw_buckets(jax.random.fold_in(streams_of[14], 71), 0),
        "norm1_gain": jnp.clip(1.0 + 0.15 * jax.random.normal(streams_of[4], (D,), jnp.float32), 0.25, 1.75),
        "rel_bias": centred(streams_of[5], (H * NB,), 1.0, 4.0, ((0, 32),), jnp.float32),
        "w_query": centred(streams_of[6], (D, HD), (4 * D) ** -0.5, 0.0625, ((0, 32),), jnp.float32),
        "w_key": centred(streams_of[7], (D, HD), (4 * D) ** -0.5, 0.0625, ((0, 32),), jnp.float32),
        "w_value": centred(streams_of[8], (D, HD), D ** -0.5, 0.125, ((0, 32),), jnp.float32),
        "w_attn_out": centred(streams_of[9], (HD, D), (HD // 16) ** -0.5, 0.5, ((0, 32),), jnp.float32),
        "norm2_gain": jnp.clip(1.0 + 0.15 * jax.random.normal(streams_of[10], (D,), jnp.float32), 0.25, 1.75),
        "w_gate": centred(streams_of[11], (D, FF), D ** -0.5, 0.125, ((0, 32),), jnp.float32),
        "w_up": centred(streams_of[12], (D, FF), D ** -0.5, 0.125, ((0, 32),), jnp.float32),
        "w_down": centred(streams_of[13], (FF, D), FF ** -0.5, 0.078125, ((0, 32),), jnp.float32),
    }


@jax.custom_vjp
def low(v):
    return lax.optimization_barrier(v.astype(jnp.bfloat16)).astype(jnp.float32)

@jax.custom_vjp
def low_back(v):
    return v

def low_keep(v):
    return (low(v), None)

def low_pass(kept, grad):
    return (grad,)

def back_keep(v):
    return (v, None)

def back_low(kept, grad):
    return (low(grad),)
low.defvjp(low_keep, low_pass)
low_back.defvjp(back_keep, back_low)
EPSILON = 1e-06
MASKED = -1e+30
HIGHEST = lax.Precision.HIGHEST

def rounded_both(values):
    return low_back(low(values))

def matmul(left, right):
    return jnp.dot(left, right, precision=HIGHEST)

def rms_scale(values):
    return lax.rsqrt(lax.optimization_barrier(jnp.mean(values * values, axis=1, keepdims=True)) + EPSILON)

def layer(params, inputs, valid_len, buckets):
    gain_one, bias_flat, query_weight, key_weight, value_weight, attn_weight, gain_two, gate_weight, up_weight, down_weight = tuple((low(master) for master in params))
    seq_len = inputs.shape[0]
    positions = jnp.arange(seq_len, dtype=jnp.int32)
    valid = positions < valid_len
    scale_one = rms_scale(inputs)
    normed = low(inputs * scale_one * gain_one)
    head_dim = query_weight.shape[1] // H
    query_heads = rounded_both(matmul(normed, query_weight)).reshape(seq_len, H, head_dim)
    key_heads = rounded_both(matmul(normed, key_weight)).reshape(seq_len, H, head_dim)
    value_heads = rounded_both(matmul(normed, value_weight)).reshape(seq_len, H, head_dim)
    by_offset = bias_flat.reshape(H, NB)[:, buckets]
    query_block = math.gcd(512, seq_len)

    def attend_block(start):
        query_part = lax.dynamic_slice_in_dim(query_heads, start, query_block, 0)
        row_pos = start + jnp.arange(query_block, dtype=jnp.int32)
        offset = positions[None, :] - row_pos[:, None] + (seq_len - 1)
        scores = jnp.einsum('ihd,jhd->hij', query_part, key_heads, precision=HIGHEST) + by_offset[:, offset]
        scores = low_back(scores)
        scores = jnp.where(valid[None, None, :], scores, MASKED)
        weights = low(jax.nn.softmax(scores, axis=-1))
        return jnp.einsum('hij,jhd->ihd', weights, value_heads, precision=HIGHEST)
    starts = jnp.arange(seq_len // query_block, dtype=jnp.int32) * query_block
    attended = lax.map(jax.checkpoint(attend_block), starts).reshape(seq_len, -1)
    attended = rounded_both(attended)
    hidden_one = inputs + low_back(matmul(attended, attn_weight))
    scale_two = rms_scale(hidden_one)
    normed_two = low(hidden_one * scale_two * gain_two)
    gate_act = low_back(matmul(normed_two, gate_weight))
    upward = low_back(matmul(normed_two, up_weight))
    hidden_ff = low(jax.nn.gelu(gate_act, approximate=True) * upward)
    result = hidden_one + low_back(matmul(hidden_ff, down_weight))
    return result * valid[:, None].astype(result.dtype)

def reference(tokens, cotangent, lengths, buckets, norm1_gain, rel_bias, w_query, w_key, w_value, w_attn_out, norm2_gain, w_gate, w_up, w_down):
    masters = (norm1_gain, rel_bias, w_query, w_key, w_value, w_attn_out, norm2_gain, w_gate, w_up, w_down)

    def per_sequence(totals, item):
        inputs, upstream, valid_len = item

        def forward(params, values):
            return layer(params, values, valid_len, buckets)
        result, pullback = jax.vjp(forward, masters, inputs.astype(jnp.float32))
        grad_params, grad_inputs = pullback(upstream.astype(jnp.float32))
        totals = jax.tree.map(jnp.add, totals, grad_params)
        return (totals, (result.astype(jnp.bfloat16), grad_inputs.astype(jnp.bfloat16)))
    zero_grads = jax.tree.map(jnp.zeros_like, masters)
    totals, (outputs, grad_tokens) = lax.scan(per_sequence, zero_grads, (tokens, cotangent, lengths))
    return (outputs, grad_tokens, totals[0], totals[1], totals[2], totals[3], totals[4], totals[5], totals[6], totals[7], totals[8], totals[9])
```

```python
import functools, math
import jax, jax.numpy as jnp
from jax import lax
from jax.experimental import pallas as pl
from jax.experimental.pallas import tpu as pltpu

MASKED = -1e30
NT = (((1,), (1,)), ((), ()))
NN = (((1,), (0,)), ((), ()))


def dotf(a, b, dims=NN):
    return lax.dot_general(a, b, dims, preferred_element_type=jnp.float32)


def head_mask(width, head_dim, h):
    lane = lax.broadcasted_iota(jnp.int32, (1, width), 1)
    return (lane // head_dim == h).astype(jnp.float32).astype(jnp.bfloat16)


def fill_skew(bias_ref, skew_ref, heads, block, length):
    for h in range(heads):
        rows = jnp.broadcast_to(bias_ref[h : h + 1, :], (block, 2 * length))
        rolled = pltpu.roll(rows, 2 * length - (block - 1), 1, stride=1, stride_axis=0)
        skew_ref[h] = rolled[:, : 2 * length - block]


def attn_fwd_kernel(
    heads, head_dim, block, length, lens_ref, q_ref, k_ref, v_ref, bias_ref, out_ref, lse_ref,
    skew_ref, kt_ref,
):
    seq, blk = pl.program_id(0), pl.program_id(1)
    width = heads * head_dim

    @pl.when((seq == 0) & (blk == 0))
    def _():
        fill_skew(bias_ref, skew_ref, heads, block, length)

    @pl.when(blk == 0)
    def _():
        kt_ref[...] = k_ref[...].T

    valid_len = lens_ref[seq]
    key_pos = lax.broadcasted_iota(jnp.int32, (1, length), 1)
    key_mask = jnp.where(key_pos < valid_len, 0.0, MASKED)
    start = pl.multiple_of(length - block - blk * block, block)
    lane = lax.broadcasted_iota(jnp.int32, (block, 128), 1)
    out = jnp.zeros((block, width), jnp.float32)
    lse_all = jnp.zeros((block, 128), jnp.float32)
    for h in range(heads):
        mask = head_mask(width, head_dim, h)
        scores = dotf(q_ref[...] * mask, kt_ref[...])
        scores = scores + skew_ref[h, :, pl.ds(start, length)] + key_mask
        peak = jnp.max(scores, axis=1, keepdims=True)
        probs = jnp.exp(scores - peak)
        mass = jnp.sum(probs, axis=1, keepdims=True)
        probs = (probs * (1.0 / mass)).astype(jnp.bfloat16)
        out = out + dotf(probs, v_ref[...] * mask)
        lse_all = jnp.where(lane == h, peak + jnp.log(mass), lse_all)
    out_ref[...] = out.astype(jnp.bfloat16)
    lse_ref[...] = lse_all


def attn_fwd(qkv, offset_bias, lens, heads, head_dim, seqs, block=256):
    rows, width3 = qkv.shape
    width = width3 // 3
    length = rows // seqs
    block = min(block, length)
    blocks = length // block
    return pl.pallas_call(
        functools.partial(attn_fwd_kernel, heads, head_dim, block, length),
        grid_spec=pltpu.PrefetchScalarGridSpec(
            num_scalar_prefetch=1,
            grid=(seqs, blocks),
            in_specs=[
                pl.BlockSpec((block, width), lambda s, i, lens: (s * blocks + i, 0)),
                pl.BlockSpec((length, width), lambda s, i, lens: (s, 1)),
                pl.BlockSpec((length, width), lambda s, i, lens: (s, 2)),
                pl.BlockSpec((heads, 2 * length), lambda s, i, lens: (0, 0)),
            ],
            out_specs=[
                pl.BlockSpec((block, width), lambda s, i, lens: (s * blocks + i, 0)),
                pl.BlockSpec((block, 128), lambda s, i, lens: (s * blocks + i, 0)),
            ],
            scratch_shapes=[
                pltpu.VMEM((heads, block, 2 * length - block), jnp.float32),
                pltpu.VMEM((width, length), jnp.bfloat16),
            ],
        ),
        out_shape=[
            jax.ShapeDtypeStruct((rows, width), jnp.bfloat16),
            jax.ShapeDtypeStruct((rows, 128), jnp.float32),
        ],
        compiler_params=pltpu.CompilerParams(
            dimension_semantics=("arbitrary", "arbitrary"), vmem_limit_bytes=56 * 1024 * 1024
        ),
        name="attn_fwd",
    )(lens, qkv, qkv, qkv, offset_bias)


def attn_bwd_kernel(
    heads, head_dim, block, length, lens_ref, q_ref, k_ref, v_ref, g_ref, lse_ref, bias_ref,
    dq_ref, dk_ref, dv_ref, dbias_ref, skew_ref, kt_ref, vt_ref, acc_ref, dkt_ref, dvt_ref,
):
    seq, blk = pl.program_id(0), pl.program_id(1)
    last_seq, last_blk = pl.num_programs(0) - 1, pl.num_programs(1) - 1
    width = heads * head_dim

    @pl.when((seq == 0) & (blk == 0))
    def _():
        fill_skew(bias_ref, skew_ref, heads, block, length)
        acc_ref[...] = jnp.zeros_like(acc_ref)

    @pl.when(blk == 0)
    def _():
        kt_ref[...] = k_ref[...].T
        vt_ref[...] = v_ref[...].T
        dkt_ref[...] = jnp.zeros_like(dkt_ref)
        dvt_ref[...] = jnp.zeros_like(dvt_ref)

    valid_len = lens_ref[seq]
    key_pos = lax.broadcasted_iota(jnp.int32, (1, length), 1)
    key_mask = jnp.where(key_pos < valid_len, 0.0, MASKED)
    start = pl.multiple_of(length - block - blk * block, block)
    q_t = q_ref[...].T
    g_t = g_ref[...].T
    dq = jnp.zeros((block, width), jnp.float32)
    row = lax.broadcasted_iota(jnp.int32, (width, 1), 0)
    for h in range(heads):
        mask = head_mask(width, head_dim, h)
        rmask = (row // head_dim == h).astype(jnp.float32).astype(jnp.bfloat16)
        scores = dotf(q_ref[...] * mask, kt_ref[...])
        scores = scores + skew_ref[h, :, pl.ds(start, length)] + key_mask
        probs = jnp.exp(scores - lse_ref[:, h : h + 1])
        grad_probs = dotf(g_ref[...] * mask, vt_ref[...])
        delta = jnp.sum(probs * grad_probs, axis=1, keepdims=True)
        ds = (probs * (grad_probs - delta)).astype(jnp.bfloat16)
        dq = dq + dotf(ds, k_ref[...] * mask)
        acc_ref[h, :, pl.ds(start, length)] += ds.astype(jnp.float32)
        dkt_ref[...] += dotf(q_t * rmask, ds)
        dvt_ref[...] += dotf(g_t * rmask, probs.astype(jnp.bfloat16))
    dq_ref[...] = dq.astype(jnp.bfloat16)

    @pl.when(blk == last_blk)
    def _():
        dk_ref[...] = dkt_ref[...].astype(jnp.bfloat16).T
        dv_ref[...] = dvt_ref[...].astype(jnp.bfloat16).T

    @pl.when((seq == last_seq) & (blk == last_blk))
    def _():
        for h in range(heads):
            part = jnp.concatenate(
                [acc_ref[h], jnp.zeros((block, block), jnp.float32)], axis=1
            )
            n = block
            while n > 8:
                n //= 2
                part = pltpu.roll(part[:n], n, 1) + part[n:]
            total = jnp.zeros((1, 2 * length), jnp.float32)
            for i in range(n):
                total = total + (pltpu.roll(part, n - 1 - i, 1) if i < n - 1 else part)[i : i + 1]
            dbias_ref[h : h + 1, :] = total


def attn_bwd(qkv, grad, lse, offset_bias, lens, heads, head_dim, seqs, block=256):
    rows, width3 = qkv.shape
    width = width3 // 3
    length = rows // seqs
    block = min(block, length)
    blocks = length // block
    return pl.pallas_call(
        functools.partial(attn_bwd_kernel, heads, head_dim, block, length),
        grid_spec=pltpu.PrefetchScalarGridSpec(
            num_scalar_prefetch=1,
            grid=(seqs, blocks),
            in_specs=[
                pl.BlockSpec((block, width), lambda s, i, lens: (s * blocks + i, 0)),
                pl.BlockSpec((length, width), lambda s, i, lens: (s, 1)),
                pl.BlockSpec((length, width), lambda s, i, lens: (s, 2)),
                pl.BlockSpec((block, width), lambda s, i, lens: (s * blocks + i, 0)),
                pl.BlockSpec((block, 128), lambda s, i, lens: (s * blocks + i, 0)),
                pl.BlockSpec((heads, 2 * length), lambda s, i, lens: (0, 0)),
            ],
            out_specs=[
                pl.BlockSpec((block, width), lambda s, i, lens: (s * blocks + i, 0)),
                pl.BlockSpec((length, width), lambda s, i, lens: (s, 0)),
                pl.BlockSpec((length, width), lambda s, i, lens: (s, 0)),
                pl.BlockSpec((heads, 2 * length), lambda s, i, lens: (0, 0)),
            ],
            scratch_shapes=[
                pltpu.VMEM((heads, block, 2 * length - block), jnp.float32),
                pltpu.VMEM((width, length), jnp.bfloat16),
                pltpu.VMEM((width, length), jnp.bfloat16),
                pltpu.VMEM((heads, block, 2 * length - block), jnp.float32),
                pltpu.VMEM((width, length), jnp.float32),
                pltpu.VMEM((width, length), jnp.float32),
            ],
        ),
        out_shape=[
            jax.ShapeDtypeStruct((rows, width), jnp.bfloat16),
            jax.ShapeDtypeStruct((rows, width), jnp.bfloat16),
            jax.ShapeDtypeStruct((rows, width), jnp.bfloat16),
            jax.ShapeDtypeStruct((heads, 2 * length), jnp.float32),
        ],
        compiler_params=pltpu.CompilerParams(
            dimension_semantics=("arbitrary", "arbitrary"), vmem_limit_bytes=60 * 1024 * 1024
        ),
        name="attn_bwd",
    )(lens, qkv, qkv, qkv, grad, lse, offset_bias)


from jax.sharding import Mesh
from jax.sharding import PartitionSpec as P

H = 32
EPSILON = 1e-06
HIGHEST = lax.Precision.HIGHEST
BF = jnp.bfloat16
F32 = jnp.float32
TP = ("fsdp", "core")
ALL = ("fsdp", "z", "core")


def rms_scale(values):
    return lax.rsqrt(jnp.mean(values * values, axis=1, keepdims=True) + EPSILON)


def norm_back(grad_normed, values, row_scale, gain_row):
    weighted = grad_normed * gain_row
    inner_mean = jnp.mean(weighted * values, axis=1, keepdims=True)
    return row_scale * (weighted - values * row_scale * row_scale * inner_mean)


def gelu_tanh(values):
    return jax.nn.gelu(values, approximate=True)


def swap_planes(x):
    f, z = lax.axis_size("fsdp"), lax.axis_size("z")
    pairs = [(i * z + j, j * f + i) for i in range(f) for j in range(z)]
    return lax.ppermute(x, ("fsdp", "z"), pairs)


def gather_rows(x, seqs):
    b = x.shape[0] // seqs
    full = lax.all_gather(x.reshape(seqs, b, -1), TP, axis=1, tiled=True)
    return full.reshape(-1, x.shape[1])


def scatter_rows(x, seqs):
    part = lax.psum_scatter(
        x.reshape(seqs, x.shape[0] // seqs, -1), TP, scatter_dimension=1, tiled=True
    )
    return part.reshape(-1, x.shape[1])


class Layout:
    def __init__(self, per_device, head_dim):
        self.f, self.z, self.c = (lax.axis_size(a) for a in ALL)
        self.natural = per_device % head_dim == 0
        self.per_device = per_device

    def split(self, w):
        rows, cols = w.shape
        if self.natural:
            w = w.reshape(rows, self.f, self.z, self.c, self.per_device)
            w = w.transpose(1, 3, 0, 2, 4)
        else:
            w = w.reshape(rows, self.f, self.c, -1).transpose(1, 2, 0, 3)
        return w.reshape(self.f * self.c, rows, -1)

    def join(self, w):
        devices, rows, cols = w.shape
        if self.natural:
            w = w.reshape(self.f, self.c, rows, self.z, self.per_device)
            w = w.transpose(2, 0, 3, 1, 4)
        else:
            w = w.reshape(self.f, self.c, rows, cols).transpose(2, 0, 1, 3)
        return w.reshape(rows, -1)

    def gather(self, w):
        if self.natural:
            return lax.all_gather(w, "z", axis=0, tiled=True)
        both = lax.all_gather(w, ("z", "core"), axis=0, tiled=True)
        size = both.shape[0] // self.c
        return lax.dynamic_slice_in_dim(both, lax.axis_index("core") * size, size, 0)

    def scatter(self, g):
        if self.natural:
            return lax.psum_scatter(g, "z", scatter_dimension=0, tiled=True)
        size = g.shape[0]
        both = jnp.zeros((size * self.c, g.shape[1]), g.dtype)
        both = lax.dynamic_update_slice_in_dim(both, g, lax.axis_index("core") * size, 0)
        return lax.psum_scatter(both, ("z", "core"), scatter_dimension=0, tiled=True)


def spread(pieces):
    f, z, c = (lax.axis_size(a) for a in ALL)
    devices, rows, cols = pieces.shape
    got = lax.all_to_all(pieces, TP, split_axis=0, concat_axis=0, tiled=True)
    return got.reshape(f, c * rows, cols)


def over_z(got):
    f, cr, cols = got.shape
    full = lax.all_gather(got, "z", axis=1, tiled=True)
    return full.reshape(-1, cols)


def reduce_z(grad):
    f, z = lax.axis_size("fsdp"), lax.axis_size("z")
    return lax.psum_scatter(
        grad.reshape(f, grad.shape[0] // f, -1), "z", scatter_dimension=1, tiled=True
    )


def unspread(part):
    f, cr, cols = part.shape
    c = lax.axis_size("core")
    return lax.all_to_all(
        part.reshape(f * c, cr // c, cols), TP, split_axis=0, concat_axis=0, tiled=True
    )


def shards(
    tokens, cotangent, lengths, buckets, norm1_gain, rel_bias,
    w_query, w_key, w_value, w_attn_out, norm2_gain, w_gate, w_up, w_down,
):
    fs, zs, cs = (lax.axis_size(a) for a in ALL)
    seqs, block_len, width = tokens.shape
    rows = seqs * block_len
    length = block_len * fs * cs
    head_dim = w_query.shape[1] // H
    heads = H // (fs * cs)
    buckets_n = rel_bias.shape[0] * fs * zs * cs // H
    head_cols = Layout(w_attn_out.shape[0], head_dim)
    ff_cols = Layout(w_down.shape[0], w_down.shape[0])

    small = lax.all_gather(
        jnp.concatenate([norm1_gain, norm2_gain, rel_bias]).astype(BF), ALL, axis=0
    )
    g = norm1_gain.shape[0]
    gain_one = small[:, :g].reshape(1, -1).astype(F32)
    gain_two = small[:, g : 2 * g].reshape(1, -1).astype(F32)
    table = small[:, 2 * g :].reshape(1, -1).astype(F32).reshape(H, buckets_n)
    plane_index = lax.axis_index("fsdp") * cs + lax.axis_index("core")
    table = head_cols.split(jnp.repeat(table.T, head_dim, axis=1))[:, :, ::head_dim]
    table = lax.dynamic_index_in_dim(table, plane_index, 0, keepdims=False).T
    one_hot = (buckets[:, None] == jnp.arange(buckets_n, dtype=jnp.int32)[None, :]).astype(F32)
    one_hot = jnp.pad(one_hot, ((0, 1), (0, 0)))
    offset_bias = jnp.dot(table, one_hot.T, precision=HIGHEST)

    lens = swap_planes(lengths)
    x_in = swap_planes(tokens)
    cot = swap_planes(cotangent)

    qkv_pieces = jnp.concatenate(
        [head_cols.split(w.astype(BF)) for w in (w_query, w_key, w_value)], axis=2
    )
    ff_pieces = jnp.concatenate([ff_cols.split(w.astype(BF)) for w in (w_gate, w_up)], axis=2)
    w_qkv = over_z(spread(qkv_pieces))
    w_o = head_cols.gather(w_attn_out.astype(BF))
    w_gu = over_z(spread(ff_pieces))
    w_d = ff_cols.gather(w_down.astype(BF))
    ff = w_d.shape[0]

    positions = plane_index * block_len + jnp.arange(block_len, dtype=jnp.int32)
    valid = (positions[None, :] < lens[:, None]).astype(F32).reshape(rows, 1)

    x = x_in.reshape(rows, width).astype(F32)
    scale_one = rms_scale(x)
    normed = gather_rows((x * scale_one * gain_one).astype(BF), seqs)
    grad_rows = cot.reshape(rows, width).astype(F32) * valid
    grad_branch = gather_rows(grad_rows.astype(BF), seqs)

    qkv = jnp.dot(normed, w_qkv, preferred_element_type=F32).astype(BF)
    attended, lse = attn_fwd(qkv, offset_bias, lens, heads, head_dim, seqs)
    attn_sum = scatter_rows(jnp.dot(attended, w_o, preferred_element_type=F32).astype(BF), seqs)
    hidden_one = x + attn_sum.astype(F32)
    scale_two = rms_scale(hidden_one)
    normed_two = gather_rows((hidden_one * scale_two * gain_two).astype(BF), seqs)

    gate = jnp.dot(normed_two, w_gu[:, :ff], preferred_element_type=F32)
    upward = jnp.dot(normed_two, w_gu[:, ff:], preferred_element_type=F32)
    activated, gelu_pull = jax.vjp(gelu_tanh, gate)
    hidden_ff = (activated * upward).astype(BF)
    out_part = jnp.dot(hidden_ff, w_d, preferred_element_type=F32).astype(BF)
    grad_hidden = jnp.einsum("rd,fd->rf", grad_branch, w_d, preferred_element_type=F32)
    grad_gate = gelu_pull(grad_hidden * upward)[0].astype(BF)
    grad_up = (grad_hidden * activated).astype(BF)
    grad_gu = jnp.concatenate([grad_gate, grad_up], axis=1)
    grad_n2_part = jnp.einsum("rf,df->rd", grad_gu, w_gu, preferred_element_type=F32).astype(BF)
    grad_normed_two = scatter_rows(grad_n2_part, seqs).astype(F32)
    gain_two_part = jnp.sum(grad_normed_two * hidden_one * scale_two, axis=0)
    grad_hidden_one = grad_rows + norm_back(grad_normed_two, hidden_one, scale_two, gain_two)
    grad_attn = gather_rows(grad_hidden_one.astype(BF), seqs)

    result = hidden_one + scatter_rows(out_part, seqs).astype(F32)
    output = swap_planes((result * valid).astype(BF).reshape(seqs, block_len, width))

    grad_w_down = jnp.einsum("rf,rd->fd", hidden_ff, grad_branch, preferred_element_type=F32)
    grad_w_gu = jnp.einsum("rd,rf->df", normed_two, grad_gu, preferred_element_type=F32)
    sum_down = ff_cols.scatter(grad_w_down.astype(BF))
    sum_gu = reduce_z(grad_w_gu.astype(BF))

    grad_attended = jnp.einsum("rd,kd->rk", grad_attn, w_o, preferred_element_type=F32).astype(BF)
    grad_w_o = jnp.einsum("rk,rd->kd", attended, grad_attn, preferred_element_type=F32)
    sum_o = head_cols.scatter(grad_w_o.astype(BF))
    dq, dk, dv, grad_offset = attn_bwd(
        qkv, grad_attended, lse, offset_bias, lens, heads, head_dim, seqs
    )
    dqkv = jnp.concatenate([dq, dk, dv], axis=1)
    grad_w_qkv = jnp.einsum("rd,rk->dk", normed, dqkv, preferred_element_type=F32)
    sum_qkv = reduce_z(grad_w_qkv.astype(BF))
    grad_n_part = jnp.einsum("rk,dk->rd", dqkv, w_qkv, preferred_element_type=F32).astype(BF)
    grad_normed = scatter_rows(grad_n_part, seqs).astype(F32)
    gain_one_part = jnp.sum(grad_normed * x * scale_one, axis=0)
    grad_x = grad_hidden_one + norm_back(grad_normed, x, scale_one, gain_one)
    grad_tokens = swap_planes(grad_x.astype(BF).reshape(seqs, block_len, width))

    grad_table = jnp.dot(grad_offset, one_hot, precision=HIGHEST)
    bias_all = jnp.zeros((fs * cs, heads, buckets_n), F32)
    bias_all = lax.dynamic_update_index_in_dim(bias_all, grad_table, plane_index, 0)
    bias_all = jnp.repeat(bias_all.transpose(0, 2, 1), head_dim, axis=2)
    bias_all = head_cols.join(bias_all)[:, ::head_dim].T.reshape(fs * zs * cs, -1)
    small_grad = jnp.concatenate(
        [
            gain_one_part.reshape(fs * zs * cs, -1),
            gain_two_part.reshape(fs * zs * cs, -1),
            bias_all,
        ],
        axis=1,
    )
    small_grad = lax.psum_scatter(small_grad, ALL, scatter_dimension=0, tiled=True)[0]

    got_gu = unspread(sum_gu)
    got_qkv = unspread(sum_qkv)
    hw = heads * head_dim
    grads_qkv = [
        head_cols.join(got_qkv[:, :, i * hw : (i + 1) * hw]).astype(F32) for i in range(3)
    ]
    grads_gu = [ff_cols.join(got_gu[:, :, i * ff : (i + 1) * ff]).astype(F32) for i in range(2)]
    return (
        output,
        grad_tokens,
        small_grad[:g],
        small_grad[2 * g :],
        grads_qkv[0],
        grads_qkv[1],
        grads_qkv[2],
        sum_o.astype(F32),
        small_grad[g : 2 * g],
        grads_gu[0],
        grads_gu[1],
        sum_down.astype(F32),
    )


def solution(mesh):
    fs, ctx = mesh.shape["fsdp"], mesh.shape["ctx"]
    mesh3 = Mesh(mesh.devices.reshape(fs, ctx // 2, 2), ALL)
    act = P("fsdp", ("z", "core"), None)
    vec, mat = P(ALL), P(ALL, None)
    in_specs = (act, act, P("fsdp"), P(), vec, vec, mat, mat, mat, mat, vec, mat, mat, mat)
    out_specs = (act, act, vec, vec, mat, mat, mat, mat, vec, mat, mat, mat)
    return jax.shard_map(shards, mesh=mesh3, in_specs=in_specs, out_specs=out_specs, check_vma=False)
```

```python
import functools, math
import jax, jax.numpy as jnp
from jax import lax
from jax.experimental import pallas as pl
from jax.experimental.pallas import tpu as pltpu

MASKED = -1e30
NT = (((1,), (1,)), ((), ()))
NN = (((1,), (0,)), ((), ()))


def dotf(a, b, dims=NN):
    return lax.dot_general(a, b, dims, preferred_element_type=jnp.float32)


def head_mask(width, head_dim, h):
    lane = lax.broadcasted_iota(jnp.int32, (1, width), 1)
    return (lane // head_dim == h).astype(jnp.float32).astype(jnp.bfloat16)


def fill_skew(bias_ref, skew_ref, heads, block, length):
    for h in range(heads):
        rows = jnp.broadcast_to(bias_ref[h : h + 1, :], (block, 2 * length))
        rolled = pltpu.roll(rows, 2 * length - (block - 1), 1, stride=1, stride_axis=0)
        skew_ref[h] = rolled[:, : 2 * length - block]


def attn_fwd_kernel(
    heads, head_dim, block, length, lens_ref, q_ref, k_ref, v_ref, bias_ref, out_ref, lse_ref,
    skew_ref, kt_ref,
):
    seq, blk = pl.program_id(0), pl.program_id(1)
    width = heads * head_dim

    @pl.when((seq == 0) & (blk == 0))
    def _():
        fill_skew(bias_ref, skew_ref, heads, block, length)

    @pl.when(blk == 0)
    def _():
        kt_ref[...] = k_ref[...].T

    valid_len = lens_ref[seq]
    key_pos = lax.broadcasted_iota(jnp.int32, (1, length), 1)
    key_mask = jnp.where(key_pos < valid_len, 0.0, MASKED)
    start = pl.multiple_of(length - block - blk * block, block)
    lane = lax.broadcasted_iota(jnp.int32, (block, 128), 1)
    out = jnp.zeros((block, width), jnp.float32)
    lse_all = jnp.zeros((block, 128), jnp.float32)
    for h in range(heads):
        mask = head_mask(width, head_dim, h)
        scores = dotf(q_ref[...] * mask, kt_ref[...])
        scores = scores + skew_ref[h, :, pl.ds(start, length)] + key_mask
        peak = jnp.max(scores, axis=1, keepdims=True)
        probs = jnp.exp(scores - peak)
        mass = jnp.sum(probs, axis=1, keepdims=True)
        probs = (probs * (1.0 / mass)).astype(jnp.bfloat16)
        out = out + dotf(probs, v_ref[...] * mask)
        lse_all = jnp.where(lane == h, peak + jnp.log(mass), lse_all)
    out_ref[...] = out.astype(jnp.bfloat16)
    lse_ref[...] = lse_all


def attn_fwd(qkv, offset_bias, lens, heads, head_dim, seqs, block=256):
    rows, width3 = qkv.shape
    width = width3 // 3
    length = rows // seqs
    block = min(block, length)
    blocks = length // block
    return pl.pallas_call(
        functools.partial(attn_fwd_kernel, heads, head_dim, block, length),
        grid_spec=pltpu.PrefetchScalarGridSpec(
            num_scalar_prefetch=1,
            grid=(seqs, blocks),
            in_specs=[
                pl.BlockSpec((block, width), lambda s, i, lens: (s * blocks + i, 0)),
                pl.BlockSpec((length, width), lambda s, i, lens: (s, 1)),
                pl.BlockSpec((length, width), lambda s, i, lens: (s, 2)),
                pl.BlockSpec((heads, 2 * length), lambda s, i, lens: (0, 0)),
            ],
            out_specs=[
                pl.BlockSpec((block, width), lambda s, i, lens: (s * blocks + i, 0)),
                pl.BlockSpec((block, 128), lambda s, i, lens: (s * blocks + i, 0)),
            ],
            scratch_shapes=[
                pltpu.VMEM((heads, block, 2 * length - block), jnp.float32),
                pltpu.VMEM((width, length), jnp.bfloat16),
            ],
        ),
        out_shape=[
            jax.ShapeDtypeStruct((rows, width), jnp.bfloat16),
            jax.ShapeDtypeStruct((rows, 128), jnp.float32),
        ],
        compiler_params=pltpu.CompilerParams(
            dimension_semantics=("arbitrary", "arbitrary"), vmem_limit_bytes=56 * 1024 * 1024
        ),
        cost_estimate=estimate(26),
        name="attn_fwd",
    )(lens, qkv, qkv, qkv, offset_bias)


def attn_bwd_kernel(
    heads, head_dim, block, length, seqs, fs, lens_ref, q_ref, k_ref, v_ref, g_ref, lse_ref, bias_ref,
    *refs,
):
    seq, blk = pl.program_id(0), pl.program_id(1)
    blocks = length // block
    last_seq, last_blk = seqs - 1, blocks - 1
    if fs:
        a_ref, w_ref, dq_ref, dk_ref, dv_ref, dbias_ref, sum_ref = refs[:7]
        refs = refs[7:]
        plane = Plane(fs)

        def partial(slot, cols):
            return dotf(a_ref[:, slot].reshape(-1, a_ref.shape[3]), w_ref[:, cols])

        actions = [plane.barrier] + scatter_actions(
            plane, partial, 256, sum_ref.shape[2], sum_ref, refs[6:]
        )
        grid_step = seq * blocks + blk
        steps = seqs * blocks
        for step in range(steps):
            todo = actions[len(actions) * step // steps : len(actions) * (step + 1) // steps]

            @pl.when(grid_step == step)
            def _(todo=todo):
                for action in todo:
                    action()

    else:
        dq_ref, dk_ref, dv_ref, dbias_ref = refs[:4]
        refs = refs[4:]
    skew_ref, kt_ref, vt_ref, acc_ref, dkt_ref, dvt_ref = refs[:6]
    width = heads * head_dim

    @pl.when((seq == 0) & (blk == 0))
    def _():
        fill_skew(bias_ref, skew_ref, heads, block, length)
        acc_ref[...] = jnp.zeros_like(acc_ref)

    @pl.when(blk == 0)
    def _():
        kt_ref[...] = k_ref[...].T
        vt_ref[...] = v_ref[...].T
        dkt_ref[...] = jnp.zeros_like(dkt_ref)
        dvt_ref[...] = jnp.zeros_like(dvt_ref)

    valid_len = lens_ref[seq]
    key_pos = lax.broadcasted_iota(jnp.int32, (1, length), 1)
    key_mask = jnp.where(key_pos < valid_len, 0.0, MASKED)
    start = pl.multiple_of(length - block - blk * block, block)
    q_t = q_ref[...].T
    g_t = g_ref[...].T
    dq = jnp.zeros((block, width), jnp.float32)
    row = lax.broadcasted_iota(jnp.int32, (width, 1), 0)
    for h in range(heads):
        mask = head_mask(width, head_dim, h)
        rmask = (row // head_dim == h).astype(jnp.float32).astype(jnp.bfloat16)
        scores = dotf(q_ref[...] * mask, kt_ref[...])
        scores = scores + skew_ref[h, :, pl.ds(start, length)] + key_mask
        probs = jnp.exp(scores - lse_ref[:, h : h + 1])
        grad_probs = dotf(g_ref[...] * mask, vt_ref[...])
        delta = jnp.sum(probs * grad_probs, axis=1, keepdims=True)
        ds = (probs * (grad_probs - delta)).astype(jnp.bfloat16)
        dq = dq + dotf(ds, k_ref[...] * mask)
        acc_ref[h, :, pl.ds(start, length)] += ds.astype(jnp.float32)
        dkt_ref[...] += dotf(q_t * rmask, ds)
        dvt_ref[...] += dotf(g_t * rmask, probs.astype(jnp.bfloat16))
    dq_ref[...] = dq.astype(jnp.bfloat16)

    @pl.when(blk == last_blk)
    def _():
        dk_ref[...] = dkt_ref[...].astype(jnp.bfloat16).T
        dv_ref[...] = dvt_ref[...].astype(jnp.bfloat16).T

    @pl.when((seq == last_seq) & (blk == last_blk))
    def _():
        for h in range(heads):
            part = jnp.concatenate(
                [acc_ref[h], jnp.zeros((block, block), jnp.float32)], axis=1
            )
            n = block
            while n > 8:
                n //= 2
                part = pltpu.roll(part[:n], n, 1) + part[n:]
            total = jnp.zeros((1, 2 * length), jnp.float32)
            for i in range(n):
                total = total + (pltpu.roll(part, n - 1 - i, 1) if i < n - 1 else part)[i : i + 1]
            dbias_ref[h : h + 1, :] = total


def attn_bwd(
    qkv, grad, lse, offset_bias, lens, heads, head_dim, seqs, block=256, product=None,
    collective_id=None,
):
    rows, width3 = qkv.shape
    width = width3 // 3
    length = rows // seqs
    block = min(block, length)
    blocks = length // block
    in_specs = [
        pl.BlockSpec(memory_space=pltpu.SMEM),
        pl.BlockSpec((block, width), lambda s, i: (s * blocks + i, 0)),
        pl.BlockSpec((length, width), lambda s, i: (s, 1)),
        pl.BlockSpec((length, width), lambda s, i: (s, 2)),
        pl.BlockSpec((block, width), lambda s, i: (s * blocks + i, 0)),
        pl.BlockSpec((block, 128), lambda s, i: (s * blocks + i, 0)),
        pl.BlockSpec((heads, 2 * length), lambda s, i: (0, 0)),
    ]
    out_specs = [
        pl.BlockSpec((block, width), lambda s, i: (s * blocks + i, 0)),
        pl.BlockSpec((length, width), lambda s, i: (s, 0)),
        pl.BlockSpec((length, width), lambda s, i: (s, 0)),
        pl.BlockSpec((heads, 2 * length), lambda s, i: (0, 0)),
    ]
    out_shape = [
        jax.ShapeDtypeStruct((rows, width), jnp.bfloat16),
        jax.ShapeDtypeStruct((rows, width), jnp.bfloat16),
        jax.ShapeDtypeStruct((rows, width), jnp.bfloat16),
        jax.ShapeDtypeStruct((heads, 2 * length), jnp.float32),
    ]
    scratch = [
        pltpu.VMEM((heads, block, 2 * length - block), jnp.float32),
        pltpu.VMEM((width, length), jnp.bfloat16),
        pltpu.VMEM((width, length), jnp.bfloat16),
        pltpu.VMEM((heads, block, 2 * length - block), jnp.float32),
        pltpu.VMEM((width, length), jnp.float32),
        pltpu.VMEM((width, length), jnp.float32),
    ]
    args = [lens, qkv, qkv, qkv, grad, lse, offset_bias]
    fs = 0
    if product is not None:
        fs = lax.axis_size("fsdp")
        a, w = product
        a = a.reshape(seqs, 2 * fs, -1, a.shape[1])
        args += [a, w]
        in_specs += [vmem(), vmem()]
        out_specs.append(vmem())
        out_shape.append(jax.ShapeDtypeStruct((seqs, a.shape[2], w.shape[1]), jnp.float32))
        scratch += scatter_scratch(fs, a.shape[2], w.shape[1])
    out = pl.pallas_call(
        functools.partial(attn_bwd_kernel, heads, head_dim, block, length, seqs, fs),
        grid=(seqs, blocks),
        in_specs=in_specs,
        out_specs=out_specs,
        out_shape=out_shape,
        scratch_shapes=scratch,
        compiler_params=pltpu.CompilerParams(
            dimension_semantics=("arbitrary", "arbitrary"), vmem_limit_bytes=62 * 1024 * 1024,
            collective_id=collective_id, has_side_effects=fs > 0,
        ),
        cost_estimate=estimate(50),
        name="attn_bwd",
    )(*args)
    if product is not None:
        out = list(out[:4]) + [out[4].reshape(-1, w.shape[1])]
    return out

MESH_ID = pl.DeviceIdType.MESH
MIB = 1024 * 1024


def remote_copy(src, dst, send_sem, recv_sem, device):
    return pltpu.make_async_remote_copy(
        src_ref=src, dst_ref=dst, send_sem=send_sem, recv_sem=recv_sem, device_id=device,
        device_id_type=MESH_ID,
    )


def landed(ref, sem):
    pltpu.make_async_copy(ref, ref, sem).wait()


def estimate(us):
    return pl.CostEstimate(flops=int(us * 1.1e9), bytes_accessed=int(us * 1e6), transcendentals=0)


def flip(f, bits):
    k = 1
    while k <= bits:
        if bits & k:
            f = f + (1 - 2 * (lax.rem(lax.div(f, k), 2))) * k
        k *= 2
    return f


class Plane:
    def __init__(self, fs):
        self.fs = fs
        self.f, self.z, self.c = (lax.axis_index(a) for a in ("fsdp", "z", "core"))
        self.bits = [1 << i for i in range(fs.bit_length() - 1)]
        self.orders = [self.bits, self.bits[::-1]]
        self.steps = len(self.bits)

    def peer(self, bit):
        return (flip(self.f, bit), self.z, self.c)

    def mate(self):
        return (self.f, self.z, 1 - self.c)

    def slot(self, rel, other=False):
        c = 1 - self.c if other else self.c
        return flip(self.f, rel) * 2 + c

    def barrier(self):
        bar = pltpu.get_barrier_semaphore()
        for dev in [self.mate()] + [self.peer(b) for b in self.bits]:
            pl.semaphore_signal(bar, inc=1, device_id=dev, device_id_type=MESH_ID)
        pl.semaphore_wait(bar, 1 + self.steps)


def gather_sems(fs):
    steps = fs.bit_length() - 1
    return [
        pltpu.SemaphoreType.DMA((2, steps, fs)),
        pltpu.SemaphoreType.DMA((2, fs)),
        pltpu.SemaphoreType.DMA((2, fs)),
        pltpu.SemaphoreType.DMA((2, fs)),
    ]


def run_gather(plane, x_ref, buf_ref, sems, consume):
    send, recv, mate_send, mate_recv = sems
    started = []

    def remote(*args):
        started.append(remote_copy(*args))
        started[-1].start()

    def source(p, rel):
        return x_ref.at[p] if rel == 0 else buf_ref.at[p, plane.slot(rel)]

    def to_mate(p, rel):
        remote(
            source(p, rel), buf_ref.at[p, plane.slot(rel)], mate_send.at[p, rel],
            mate_recv.at[p, rel], plane.mate(),
        )

    def to_peer(p, step, rel):
        bit = plane.orders[p][step]
        remote(
            source(p, rel), buf_ref.at[p, plane.slot(rel)], send.at[p, step, rel],
            recv.at[p, rel ^ bit], plane.peer(bit),
        )

    for step in range(plane.steps):
        for p in range(2):
            to_peer(p, step, 0)
        if step == 0:
            for p in range(2):
                to_mate(p, 0)
    for p in range(2):
        consume(p, plane.slot(0), x_ref.at[p])

    def arrived(p, rel):
        landed(buf_ref.at[p, plane.slot(rel)], recv.at[p, rel])

    def mate_arrived(p, rel):
        ref = buf_ref.at[p, plane.slot(rel, True)]
        landed(ref, mate_recv.at[p, rel])
        consume(p, plane.slot(rel, True), ref)

    have = [[0], [0]]
    pending = [(0, 0), (1, 0)]
    for step in range(plane.steps):
        fresh = []
        for i in range(len(have[0])):
            for p in range(2):
                rel = have[p][i] ^ plane.orders[p][step]
                fresh.append((p, rel))
        for p, rel in pending:
            mate_arrived(p, rel)
        for p, rel in fresh:
            arrived(p, rel)
            to_mate(p, rel)
            for later in range(step + 1, plane.steps):
                to_peer(p, later, rel)
            consume(p, plane.slot(rel), buf_ref.at[p, plane.slot(rel)])
        for p in range(2):
            have[p] = have[p] + [rel for q, rel in fresh if q == p]
        pending = fresh
    for p, rel in pending:
        mate_arrived(p, rel)
    for cp in started:
        cp.wait_send()


def scatter_scratch(fs, b, width):
    return [
        pltpu.VMEM((2, fs, b, width), jnp.bfloat16),
        pltpu.VMEM((2, fs, b, width), jnp.bfloat16),
        pltpu.VMEM((2, fs // 2, b, width), jnp.float32),
        pltpu.VMEM((2, fs, b, width), jnp.bfloat16),
        pltpu.VMEM((2, fs - 1, b, width), jnp.bfloat16),
        pltpu.SemaphoreType.DMA((fs,)),
        pltpu.SemaphoreType.DMA((fs,)),
        pltpu.SemaphoreType.DMA((2, fs)),
        pltpu.SemaphoreType.DMA((2, fs - 1)),
    ]


def scatter_actions(plane, partial, tile, width, out_ref, scratch):
    give, got, total, outbox, inbox, give_sem, got_sem, send, recv = scratch
    b = out_ref.shape[1]
    rels = sorted(range(plane.fs), key=lambda r: (-bin(r).count("1"), r))
    tiles = width // tile

    def each_tile(body):
        def one(j, carry):
            body(pl.ds(pl.multiple_of(j * tile, tile), tile))
            return carry

        lax.fori_loop(0, tiles, one, 0)

    def leaves(p, rel):
        for step, bit in enumerate(plane.orders[p]):
            if rel & bit:
                return step
        return plane.steps

    def place(p, step, rel):
        kept = [r for r in range(plane.fs) if leaves(p, r) > step]
        return plane.fs - 2 * len(kept) + kept.index(rel)

    def held(p, rel):
        return [r for r in range(plane.fs) if leaves(p, r) > 0].index(rel)

    def to_peer(p, rel):
        step = leaves(p, rel)
        bit = plane.orders[p][step]
        at = place(p, step, rel ^ bit)
        return remote_copy(
            outbox.at[p, rel], inbox.at[p, at], send.at[p, rel], recv.at[p, at], plane.peer(bit)
        )

    def to_mate(rel):
        return remote_copy(
            give.at[:, rel], got.at[:, rel], give_sem.at[rel], got_sem.at[rel], plane.mate()
        )

    def give_part(rel):
        theirs = plane.slot(rel, True)

        def body(cols):
            part = partial(theirs, cols).astype(jnp.bfloat16)
            give[0, rel, :, cols] = part[:b]
            give[1, rel, :, cols] = part[b:]

        each_tile(body)
        to_mate(rel).start()

    def own_part(rel):
        mine = plane.slot(rel)
        landed(got.at[:, rel], got_sem.at[rel])

        def body(cols):
            part = partial(mine, cols)
            for p in range(2):
                here = part[p * b : (p + 1) * b] + got[p, rel, :, cols].astype(jnp.float32)
                if leaves(p, rel) == 0:
                    outbox[p, rel, :, cols] = here.astype(jnp.bfloat16)
                else:
                    total[p, held(p, rel), :, cols] = here

        each_tile(body)
        for p in range(2):
            if leaves(p, rel) == 0:
                to_peer(p, rel).start()

    def add_part(step, rel, p):
        at = place(p, step, rel)
        landed(inbox.at[p, at], recv.at[p, at])
        sends = leaves(p, rel) == step + 1

        def body(cols):
            here = total[p, held(p, rel), :, cols] + inbox[p, at, :, cols].astype(jnp.float32)
            if step + 1 == plane.steps:
                out_ref[p, :, cols] = here
            elif sends:
                outbox[p, rel, :, cols] = here.astype(jnp.bfloat16)
            else:
                total[p, held(p, rel), :, cols] = here

        each_tile(body)
        if sends and step + 1 < plane.steps:
            to_peer(p, rel).start()

    def close():
        for rel in rels:
            to_mate(rel).wait_send()
            for p in range(2):
                if leaves(p, rel) < plane.steps:
                    to_peer(p, rel).wait_send()

    actions = [functools.partial(give_part, rels[0])]
    for i, rel in enumerate(rels):
        if i + 1 < len(rels):
            actions.append(functools.partial(give_part, rels[i + 1]))
        actions.append(functools.partial(own_part, rel))
    for step in range(plane.steps):
        for rel in rels:
            for p in range(2):
                if leaves(p, rel) > step:
                    actions.append(functools.partial(add_part, step, rel, p))
    return actions + [close]


def vmem():
    return pl.BlockSpec(memory_space=pltpu.VMEM)


def anywhere():
    return pl.BlockSpec(memory_space=pl.ANY)


def plane_params(collective_id, limit=58):
    return pltpu.CompilerParams(
        collective_id=collective_id, has_side_effects=True, vmem_limit_bytes=limit * MIB
    )


def gather_kernel(fs, x_ref, out_ref, *sems):
    plane = Plane(fs)
    plane.barrier()
    own_sem = sems[4]
    own = pltpu.make_async_copy(x_ref, out_ref.at[:, plane.slot(0)], own_sem)
    own.start()
    run_gather(plane, x_ref, out_ref, sems[:4], lambda p, slot, ref: None)
    own.wait()


def plane_gather(x, seqs, collective_id):
    fs = lax.axis_size("fsdp")
    x = x.reshape(seqs, -1, x.shape[1])
    _, b, width = x.shape
    full = pl.pallas_call(
        functools.partial(gather_kernel, fs),
        out_shape=jax.ShapeDtypeStruct((seqs, 2 * fs, b, width), x.dtype),
        in_specs=[vmem()],
        out_specs=anywhere(),
        scratch_shapes=gather_sems(fs) + [pltpu.SemaphoreType.DMA],
        compiler_params=plane_params(collective_id),
        cost_estimate=estimate(45),
        name="plane_gather",
    )(x)
    return full.reshape(-1, width)


def gather_dot_kernel(fs, dims, tile, x_ref, w_ref, full_ref, y_ref, buf_ref, *sems):
    plane = Plane(fs)
    plane.barrier()
    keep_sem = sems[4]
    columns = y_ref.shape[3]
    kept = []

    def consume(p, slot, ref):
        cp = pltpu.make_async_copy(ref, full_ref.at[p, slot], keep_sem.at[len(kept)])
        cp.start()
        kept.append(cp)

        def one(j, carry):
            cols = pl.ds(pl.multiple_of(j * tile, tile), tile)
            w = w_ref[:, cols] if dims == NN else w_ref[cols, :]
            y_ref[p, slot, :, cols] = dotf(ref[...], w, dims).astype(y_ref.dtype)
            return carry

        lax.fori_loop(0, columns // tile, one, 0)

    run_gather(plane, x_ref, buf_ref, sems[:4], consume)
    for cp in kept:
        cp.wait()


def plane_gather_dot(x, w, dims, seqs, collective_id):
    fs = lax.axis_size("fsdp")
    x = x.reshape(seqs, -1, x.shape[1])
    _, b, width = x.shape
    columns = w.shape[1] if dims == NN else w.shape[0]
    tile = math.gcd(columns, 256)
    full, y = pl.pallas_call(
        functools.partial(gather_dot_kernel, fs, dims, tile),
        out_shape=[
            jax.ShapeDtypeStruct((seqs, 2 * fs, b, width), x.dtype),
            jax.ShapeDtypeStruct((seqs, 2 * fs, b, columns), jnp.bfloat16),
        ],
        in_specs=[vmem(), vmem()],
        out_specs=[anywhere(), vmem()],
        scratch_shapes=[pltpu.VMEM((seqs, 2 * fs, b, width), x.dtype)]
        + gather_sems(fs)
        + [pltpu.SemaphoreType.DMA((seqs * 2 * fs,))],
        compiler_params=plane_params(collective_id),
        cost_estimate=estimate(45),
        name="plane_gather_dot",
    )(x, w)
    return full.reshape(-1, width), y.reshape(-1, columns)


class Swap:
    def __init__(self, x_ref, out_ref, scratch):
        self.x_ref, self.out_ref = x_ref, out_ref
        self.relay, self.d_sem, self.in_send, self.in_recv, self.on_send, self.on_recv = scratch
        self.f, self.z, self.c = (lax.axis_index(a) for a in ("fsdp", "z", "core"))
        self.zs = self.relay.shape[0]

    @staticmethod
    def scratch(zs, b, width):
        dma = pltpu.SemaphoreType.DMA
        return [
            pltpu.VMEM((zs, b, width), jnp.bfloat16), dma((2,)), dma, dma((zs,)), dma((zs,)), dma
        ]

    def straight(self):
        return remote_copy(
            self.x_ref.at[0], self.out_ref.at[0], self.d_sem.at[0], self.d_sem.at[1],
            (self.z, self.f, self.c),
        )

    def inward(self):
        return remote_copy(
            self.x_ref.at[1], self.relay.at[self.f], self.in_send, self.in_recv.at[self.f],
            (self.z, self.z, self.c),
        )

    def onward(self, source):
        return remote_copy(
            self.relay.at[source], self.out_ref.at[1], self.on_send.at[source], self.on_recv,
            (self.f, source, self.c),
        )

    def own(self):
        return pltpu.make_async_copy(self.x_ref, self.out_ref, self.d_sem.at[0])

    def start(self):
        @pl.when(self.f != self.z)
        def _():
            self.inward().start()
            self.straight().start()

        @pl.when(self.f == self.z)
        def _():
            self.own().start()

    def hand_on(self):
        @pl.when(self.f == self.z)
        def _():
            for source in range(self.zs):

                @pl.when(source != self.z)
                def _(source=source):
                    landed(self.relay.at[source], self.in_recv.at[source])
                    self.onward(source).start()

    def close(self):
        @pl.when(self.f == self.z)
        def _():
            for source in range(self.zs):

                @pl.when(source != self.z)
                def _(source=source):
                    self.onward(source).wait_send()

            self.own().wait()

        @pl.when(self.f != self.z)
        def _():
            self.inward().wait_send()
            self.straight().wait_send()
            landed(self.out_ref.at[0], self.d_sem.at[1])
            landed(self.out_ref.at[1], self.on_recv)


class Everyone:
    def __init__(self, sizes):
        self.fs, self.zs, self.cs = sizes
        self.n = math.prod(sizes)
        f, z, c = (lax.axis_index(a) for a in ("fsdp", "z", "core"))
        self.me = (f * self.zs + z) * self.cs + c

    def place(self, index):
        zs, cs = self.zs, self.cs
        return (lax.div(index, zs * cs), lax.rem(lax.div(index, cs), zs), lax.rem(index, cs))

    def other(self, d):
        return lax.rem(self.me + d, self.n)

    def barrier(self):
        bar = pltpu.get_barrier_semaphore()

        def greet(d, carry):
            pl.semaphore_signal(
                bar, inc=1, device_id=self.place(self.other(d)), device_id_type=MESH_ID
            )
            return carry

        lax.fori_loop(1, self.n, greet, 0)
        pl.semaphore_wait(bar, self.n - 1)

    def copy(self, d, x_ref, spread_out, slots, send, recv):
        src = x_ref.at[self.other(d)] if spread_out else x_ref.at[0]
        return remote_copy(
            src, slots.at[self.me], send.at[d], recv.at[d], self.place(self.other(d))
        )

    def begin(self, x_ref, spread_out, slots, send, recv, own_sem):
        def one(d, carry):
            self.copy(d, x_ref, spread_out, slots, send, recv).start()
            return carry

        lax.fori_loop(1, self.n, one, 0)
        src = x_ref.at[self.me] if spread_out else x_ref.at[0]
        own = pltpu.make_async_copy(src, slots.at[self.me], own_sem)
        own.start()
        own.wait()

    def finish(self, x_ref, spread_out, slots, send, recv):
        def one(d, carry):
            landed(slots.at[lax.rem(self.me + self.n - d, self.n)], recv.at[d])
            self.copy(d, x_ref, spread_out, slots, send, recv).wait_send()
            return carry

        lax.fori_loop(1, self.n, one, 0)


def dot_scatter_kernel(fs, zs, dims, tile, swaps, a_ref, w_ref, *refs):
    plane = Plane(fs)
    if swaps:
        Everyone((fs, zs, 2)).barrier()
        swap = Swap(refs[0], refs[2], refs[3:9])
        out_ref, scratch = refs[1], refs[9:]
    else:
        plane.barrier()
        out_ref, scratch = refs[0], refs[1:]

    def partial(slot, cols):
        a = a_ref[:, slot].reshape(-1, a_ref.shape[3])
        return dotf(a, w_ref[:, cols] if dims == NN else w_ref[cols, :], dims)

    actions = scatter_actions(plane, partial, tile, out_ref.shape[2], out_ref, scratch)
    if swaps:
        swap.start()
    for i, action in enumerate(actions):
        action()
        if swaps and i == 2 * fs:
            swap.hand_on()
    if swaps:
        swap.close()


def plane_dot_scatter(a, w, dims, seqs, collective_id, swapped=None):
    fs, zs = lax.axis_size("fsdp"), lax.axis_size("z")
    a = a.reshape(seqs, 2 * fs, -1, a.shape[1])
    b = a.shape[2]
    width = w.shape[1] if dims == NN else w.shape[0]
    out_shape = [jax.ShapeDtypeStruct((seqs, b, width), jnp.float32)]
    args, scratch = [a, w], scatter_scratch(fs, b, width)
    if swapped is not None:
        out_shape.append(jax.ShapeDtypeStruct(swapped.shape, swapped.dtype))
        args.append(swapped)
        scratch = Swap.scratch(zs, b, width) + scratch
    out = pl.pallas_call(
        functools.partial(dot_scatter_kernel, fs, zs, dims, 256, swapped is not None),
        out_shape=out_shape,
        in_specs=[vmem()] * len(args),
        out_specs=[vmem()] + [anywhere()] * (len(args) - 2),
        scratch_shapes=scratch,
        compiler_params=plane_params(collective_id),
        cost_estimate=estimate(45),
        name="plane_dot_scatter",
    )(*args)
    rows = out[0].reshape(-1, width)
    return rows if swapped is None else (rows, out[1])


GELU_C = math.sqrt(2.0 / math.pi)


def gather_ffn_kernel(fs, x_ref, g_ref, wgu_ref, wd_ref, full_ref, h_ref, ggu_ref, buf_ref, *sems):
    plane = Plane(fs)
    plane.barrier()
    keep_sem = sems[4]
    ff = wd_ref.shape[0]
    kept = []

    def consume(p, slot, ref):
        cp = pltpu.make_async_copy(ref, full_ref.at[p, slot], keep_sem.at[len(kept)])
        cp.start()
        kept.append(cp)
        gate = dotf(ref[...], wgu_ref[:, :ff])
        up = dotf(ref[...], wgu_ref[:, ff:])
        grad_hidden = dotf(g_ref[p, slot], wd_ref[...], NT)
        square = gate * gate
        tanh = jnp.tanh(GELU_C * gate * (1.0 + 0.044715 * square))
        half = 0.5 * (1.0 + tanh)
        act = gate * half
        slope = half + (0.5 * GELU_C) * gate * (1.0 - tanh * tanh) * (1.0 + 0.134145 * square)
        h_ref[p, slot] = (act * up).astype(jnp.bfloat16)
        ggu_ref[p, slot, :, :ff] = (grad_hidden * up * slope).astype(jnp.bfloat16)
        ggu_ref[p, slot, :, ff:] = (grad_hidden * act).astype(jnp.bfloat16)

    run_gather(plane, x_ref, buf_ref, sems[:4], consume)
    for cp in kept:
        cp.wait()


def plane_gather_ffn(x, grad, w_gu, w_d, seqs, collective_id):
    fs = lax.axis_size("fsdp")
    x = x.reshape(seqs, -1, x.shape[1])
    _, b, width = x.shape
    ff = w_d.shape[0]
    lead = (seqs, 2 * fs, b)
    full, h, ggu = pl.pallas_call(
        functools.partial(gather_ffn_kernel, fs),
        out_shape=[
            jax.ShapeDtypeStruct(lead + (width,), x.dtype),
            jax.ShapeDtypeStruct(lead + (ff,), jnp.bfloat16),
            jax.ShapeDtypeStruct(lead + (2 * ff,), jnp.bfloat16),
        ],
        in_specs=[vmem()] * 4,
        out_specs=[anywhere(), vmem(), vmem()],
        scratch_shapes=[pltpu.VMEM(lead + (width,), x.dtype)]
        + gather_sems(fs)
        + [pltpu.SemaphoreType.DMA((seqs * 2 * fs,))],
        compiler_params=plane_params(collective_id),
        cost_estimate=estimate(45),
        name="plane_gather_ffn",
    )(x, grad.reshape(lead + (width,)), w_gu, w_d)
    return full.reshape(-1, width), h.reshape(-1, ff), ggu.reshape(-1, 2 * ff)

def start_kernel(
    sizes, small_ref, qkv_ref, gu_ref, tok_ref, cot_ref, o_ref, d_ref,
    small_out, wqkv_ref, ggu_ref, x_ref, g_ref, o_out, d_out,
    slots, s_send, s_recv, own_sem, q_send, q_recv, g_send, g_recv, line_send, line_recv,
    *swap_scratch,
):
    fs, zs, cs = sizes
    f, z, c = (lax.axis_index(a) for a in ("fsdp", "z", "core"))
    me = f * cs + c
    devices = fs * cs
    rows = qkv_ref.shape[1]
    everyone = Everyone(sizes)
    everyone.barrier()
    everyone.begin(small_ref, False, slots, s_send, s_recv, own_sem.at[0])
    half = len(swap_scratch) // 2
    swaps = [
        Swap(tok_ref, x_ref, swap_scratch[:half]), Swap(cot_ref, g_ref, swap_scratch[half:])
    ]

    def block(out_ref, index, lead):
        at = pl.ds(pl.multiple_of(lax.rem(index, cs) * rows, rows), rows)
        if lead is None:
            return out_ref.at[lax.div(index, cs), at]
        return out_ref.at[lax.div(index, cs), lead, at]

    def spread_copy(d, src_ref, out_ref, lead, send, recv):
        to = lax.rem(me + d, devices)
        return remote_copy(
            src_ref.at[to], block(out_ref, me, lead), send.at[d], recv.at[d],
            (lax.div(to, cs), z, lax.rem(to, cs)),
        )

    own_qkv = pltpu.make_async_copy(qkv_ref.at[me], block(wqkv_ref, me, z), own_sem.at[1])
    own_gu = pltpu.make_async_copy(gu_ref.at[me], block(ggu_ref, me, None), own_sem.at[2])
    later = [
        pltpu.make_async_copy(o_ref, o_out, own_sem.at[3]),
        pltpu.make_async_copy(d_ref, d_out, own_sem.at[4]),
    ]
    for copy in later:
        copy.start()
    own_qkv.start()
    for d in range(1, devices):
        spread_copy(d, qkv_ref, wqkv_ref, z, q_send, q_recv).start()
    own_gu.start()

    swaps[0].start()
    own_qkv.wait()
    for d in range(1, devices):
        landed(block(wqkv_ref, lax.rem(me + devices - d, devices), z), q_recv.at[d])

    def line(step, way):
        source = lax.rem(z - way * step + zs, zs)
        to = lax.rem(z + way + zs, zs)
        k = 0 if way > 0 else 1
        ref = wqkv_ref.at[:, source]
        return remote_copy(ref, ref, line_send.at[k, step], line_recv.at[k, step], (f, to, c))

    def sends(step, way):
        if way > 0:
            return (z >= step) & (z < zs - 1)
        return (z < zs - step) & (z > 0)

    def arrives(step, way):
        return (z > step) if way > 0 else (z < zs - 1 - step)

    def arrive(step, way):
        k = 0 if way > 0 else 1
        source = lax.rem(z - way * (step + 1) + zs, zs)
        landed(wqkv_ref.at[:, source], line_recv.at[k, step])

    for step in range(zs - 1):
        for way in (1, -1):

            @pl.when(sends(step, way))
            def _(step=step, way=way):
                line(step, way).start()

        if step == 1:
            swaps[1].start()
        if step == 0:
            for d in range(1, devices):
                spread_copy(d, gu_ref, ggu_ref, None, g_send, g_recv).start()
        for way in (1, -1):

            @pl.when(arrives(step, way))
            def _(step=step, way=way):
                arrive(step, way)

        if step < 2:
            swaps[step].hand_on()

    everyone.finish(small_ref, False, slots, s_send, s_recv)
    small_out[...] = slots[...]
    own_gu.wait()
    for copy in later:
        copy.wait()
    for d in range(1, devices):
        landed(block(ggu_ref, lax.rem(me + devices - d, devices), None), g_recv.at[d])
    for d in range(1, devices):
        spread_copy(d, qkv_ref, wqkv_ref, z, q_send, q_recv).wait_send()
        spread_copy(d, gu_ref, ggu_ref, None, g_send, g_recv).wait_send()
    for step in range(zs - 1):
        for way in (1, -1):

            @pl.when(sends(step, way))
            def _(step=step, way=way):
                line(step, way).wait_send()

    for swap in swaps:
        swap.close()


def start(small, qkv_pieces, gu_pieces, tokens, cotangent, own_o, own_d, collective_id):
    sizes = tuple(lax.axis_size(a) for a in ("fsdp", "z", "core"))
    fs, zs, cs = sizes
    n = math.prod(sizes)
    devices, rows, qkv_cols = qkv_pieces.shape
    dma = pltpu.SemaphoreType.DMA
    return pl.pallas_call(
        functools.partial(start_kernel, sizes),
        out_shape=[
            jax.ShapeDtypeStruct((n, 8, 128), jnp.float32),
            jax.ShapeDtypeStruct((fs, zs, cs * rows, qkv_cols), jnp.bfloat16),
            jax.ShapeDtypeStruct((fs, cs * rows, gu_pieces.shape[2]), jnp.bfloat16),
            jax.ShapeDtypeStruct(tokens.shape, tokens.dtype),
            jax.ShapeDtypeStruct(cotangent.shape, cotangent.dtype),
            jax.ShapeDtypeStruct(own_o.shape, own_o.dtype),
            jax.ShapeDtypeStruct(own_d.shape, own_d.dtype),
        ],
        in_specs=[vmem()] * 7,
        out_specs=[vmem()] + [anywhere()] * 6,
        scratch_shapes=[
            pltpu.VMEM((n, 8, 128), jnp.float32),
            dma((n,)), dma((n,)), dma((5,)),
            dma((devices,)), dma((devices,)), dma((devices,)), dma((devices,)),
            dma((2, zs)), dma((2, zs)),
        ]
        + Swap.scratch(zs, *tokens.shape[1:]) * 2,
        compiler_params=plane_params(collective_id),
        cost_estimate=estimate(120),
        name="start",
    )(small, qkv_pieces, gu_pieces, tokens, cotangent, own_o, own_d)


def finish_kernel(
    sizes, small_ref, g_ref, small_out, out_ref, slots, send, recv, own_sem, *swap_scratch
):
    everyone = Everyone(sizes)
    everyone.barrier()
    everyone.begin(small_ref, True, slots, send, recv, own_sem)
    swap = Swap(g_ref, out_ref, swap_scratch)
    swap.start()
    swap.hand_on()
    everyone.finish(small_ref, True, slots, send, recv)
    small_out[...] = jnp.sum(slots[...], axis=0)
    swap.close()


def finish(small, grad, collective_id):
    sizes = tuple(lax.axis_size(a) for a in ("fsdp", "z", "core"))
    n = math.prod(sizes)
    dma = pltpu.SemaphoreType.DMA
    return pl.pallas_call(
        functools.partial(finish_kernel, sizes),
        out_shape=[
            jax.ShapeDtypeStruct((8, 128), small.dtype),
            jax.ShapeDtypeStruct(grad.shape, grad.dtype),
        ],
        in_specs=[vmem(), vmem()],
        out_specs=[vmem(), anywhere()],
        scratch_shapes=[pltpu.VMEM((n, 8, 128), small.dtype), dma((n,)), dma((n,)), dma]
        + Swap.scratch(sizes[1], *grad.shape[1:]),
        compiler_params=plane_params(collective_id),
        cost_estimate=estimate(45),
        name="finish",
    )(small, grad)


def to_tiles(x):
    return jnp.pad(x, ((0, 0), (0, 1024 - x.shape[1]))).reshape(-1, 8, 128)

from jax.sharding import Mesh
from jax.sharding import PartitionSpec as P

H = 32
EPSILON = 1e-06
HIGHEST = lax.Precision.HIGHEST
BF = jnp.bfloat16
F32 = jnp.float32
TP = ("fsdp", "core")
ALL = ("fsdp", "z", "core")


def rms_scale(values):
    return lax.rsqrt(jnp.mean(values * values, axis=1, keepdims=True) + EPSILON)


def norm_back(grad_normed, values, row_scale, gain_row):
    weighted = grad_normed * gain_row
    inner_mean = jnp.mean(weighted * values, axis=1, keepdims=True)
    return row_scale * (weighted - values * row_scale * row_scale * inner_mean)


class Layout:
    def __init__(self, per_device, head_dim):
        self.f, self.z, self.c = (lax.axis_size(a) for a in ALL)
        self.natural = per_device % head_dim == 0
        self.per_device = per_device

    def split(self, w):
        rows, cols = w.shape
        if self.natural:
            w = w.reshape(rows, self.f, self.z, self.c, self.per_device)
            w = w.transpose(1, 3, 0, 2, 4)
        else:
            w = w.reshape(rows, self.f, self.c, -1).transpose(1, 2, 0, 3)
        return w.reshape(self.f * self.c, rows, -1)

    def join(self, w):
        devices, rows, cols = w.shape
        if self.natural:
            w = w.reshape(self.f, self.c, rows, self.z, self.per_device)
            w = w.transpose(2, 0, 3, 1, 4)
        else:
            w = w.reshape(self.f, self.c, rows, cols).transpose(2, 0, 1, 3)
        return w.reshape(rows, -1)

    def gather(self, w):
        if self.natural:
            return lax.all_gather(w, "z", axis=0, tiled=True)
        both = lax.all_gather(w, ("z", "core"), axis=0, tiled=True)
        size = both.shape[0] // self.c
        return lax.dynamic_slice_in_dim(both, lax.axis_index("core") * size, size, 0)

    def scatter(self, g):
        if self.natural:
            return lax.psum_scatter(g, "z", scatter_dimension=0, tiled=True)
        size = g.shape[0]
        both = jnp.zeros((size * self.c, g.shape[1]), g.dtype)
        both = lax.dynamic_update_slice_in_dim(both, g, lax.axis_index("core") * size, 0)
        return lax.psum_scatter(both, ("z", "core"), scatter_dimension=0, tiled=True)


def over_z(got):
    f, cr, cols = got.shape
    full = lax.all_gather(got, "z", axis=1, tiled=True)
    return full.reshape(-1, cols)


def reduce_z(grad):
    f, z = lax.axis_size("fsdp"), lax.axis_size("z")
    return lax.psum_scatter(
        grad.reshape(f, grad.shape[0] // f, -1), "z", scatter_dimension=1, tiled=True
    )


def unspread(part):
    f, cr, cols = part.shape
    c = lax.axis_size("core")
    return lax.all_to_all(
        part.reshape(f * c, cr // c, cols), TP, split_axis=0, concat_axis=0, tiled=True
    )


def shards(
    tokens, cotangent, lengths, buckets, norm1_gain, rel_bias,
    w_query, w_key, w_value, w_attn_out, norm2_gain, w_gate, w_up, w_down,
):
    fs, zs, cs = (lax.axis_size(a) for a in ALL)
    seqs, block_len, width = tokens.shape
    rows = seqs * block_len
    length = block_len * fs * cs
    head_dim = w_query.shape[1] // H
    heads = H // (fs * cs)
    buckets_n = rel_bias.shape[0] * fs * zs * cs // H
    head_cols = Layout(w_attn_out.shape[0], head_dim)
    ff_cols = Layout(w_down.shape[0], w_down.shape[0])

    own_small = jnp.concatenate([norm1_gain, norm2_gain, rel_bias]).astype(BF).astype(F32)
    own_small = jnp.concatenate([own_small, lengths.astype(F32)])
    qkv_pieces = jnp.concatenate(
        [head_cols.split(w.astype(BF)) for w in (w_query, w_key, w_value)], axis=2
    )
    ff_pieces = jnp.concatenate([ff_cols.split(w.astype(BF)) for w in (w_gate, w_up)], axis=2)
    small, w_qkv, got_gu, x_in, cot, own_o, own_d = start(
        to_tiles(own_small[None]), qkv_pieces, ff_pieces, tokens, cotangent,
        w_attn_out.astype(BF), w_down.astype(BF), 9,
    )
    w_qkv = w_qkv.reshape(width, -1)
    w_o = head_cols.gather(own_o)
    w_gu = over_z(got_gu)
    w_d = ff_cols.gather(own_d)
    small = small.reshape(-1, 1024)[:, : own_small.shape[0]]
    lens = lax.dynamic_index_in_dim(
        small[:, -seqs:], lax.axis_index("z") * zs * cs, 0, keepdims=False
    ).astype(jnp.int32)
    g = norm1_gain.shape[0]
    gain_one = small[:, :g].reshape(1, -1).astype(F32)
    gain_two = small[:, g : 2 * g].reshape(1, -1).astype(F32)
    table = small[:, 2 * g : -seqs].reshape(1, -1).astype(F32).reshape(H, buckets_n)
    plane_index = lax.axis_index("fsdp") * cs + lax.axis_index("core")
    table = head_cols.split(jnp.repeat(table.T, head_dim, axis=1))[:, :, ::head_dim]
    table = lax.dynamic_index_in_dim(table, plane_index, 0, keepdims=False).T
    one_hot = (buckets[:, None] == jnp.arange(buckets_n, dtype=jnp.int32)[None, :]).astype(F32)
    one_hot = jnp.pad(one_hot, ((0, 1), (0, 0)))
    offset_bias = jnp.dot(table, one_hot.T, precision=HIGHEST)

    ff = w_d.shape[0]

    positions = plane_index * block_len + jnp.arange(block_len, dtype=jnp.int32)
    valid = (positions[None, :] < lens[:, None]).astype(F32).reshape(rows, 1)

    x = x_in.reshape(rows, width).astype(F32)
    scale_one = rms_scale(x)
    grad_rows = cot.reshape(rows, width).astype(F32) * valid
    grad_branch = plane_gather(grad_rows.astype(BF), seqs, 1)

    normed, qkv = plane_gather_dot((x * scale_one * gain_one).astype(BF), w_qkv, NN, seqs, 2)
    attended, lse = attn_fwd(qkv, offset_bias, lens, heads, head_dim, seqs)
    hidden_one = x + plane_dot_scatter(attended, w_o, NN, seqs, 3)
    scale_two = rms_scale(hidden_one)
    normed_two, hidden_ff, grad_gu = plane_gather_ffn(
        (hidden_one * scale_two * gain_two).astype(BF), grad_branch, w_gu, w_d, seqs, 4
    )
    grad_w_down = jnp.einsum("rf,rd->fd", hidden_ff, grad_branch, preferred_element_type=F32)
    grad_w_gu = jnp.einsum("rd,rf->df", normed_two, grad_gu, preferred_element_type=F32)
    grad_w_down, grad_gu = lax.optimization_barrier((grad_w_down.astype(BF), grad_gu))
    sum_down = ff_cols.scatter(grad_w_down)
    grad_w_gu, grad_gu = lax.optimization_barrier((grad_w_gu.astype(BF), grad_gu))
    grad_normed_two = plane_dot_scatter(grad_gu, w_gu, NT, seqs, 5)
    grad_w_gu, grad_normed_two, sum_down = lax.optimization_barrier(
        (grad_w_gu, grad_normed_two, sum_down)
    )
    sum_gu = reduce_z(grad_w_gu)
    gain_two_part = jnp.sum(grad_normed_two * hidden_one * scale_two, axis=0)
    grad_hidden_one = grad_rows + norm_back(grad_normed_two, hidden_one, scale_two, gain_two)
    grad_attn, grad_attended = plane_gather_dot(grad_hidden_one.astype(BF), w_o, NT, seqs, 6)


    grad_w_o = jnp.einsum("rk,rd->kd", attended, grad_attn, preferred_element_type=F32)
    grad_w_o, grad_attended = lax.optimization_barrier((grad_w_o.astype(BF), grad_attended))
    if fs <= 4:
        dq, dk, dv, grad_offset, ff_sum = attn_bwd(
            qkv, grad_attended, lse, offset_bias, lens, heads, head_dim, seqs,
            product=(hidden_ff, w_d), collective_id=7,
        )
    else:
        ff_sum = plane_dot_scatter(hidden_ff, w_d, NN, seqs, 7)
        dq, dk, dv, grad_offset = attn_bwd(
            qkv, grad_attended, lse, offset_bias, lens, heads, head_dim, seqs
        )
    result = ((hidden_one + ff_sum) * valid).astype(BF).reshape(seqs, block_len, width)
    dqkv = jnp.concatenate([dq, dk, dv], axis=1)
    grad_w_qkv = jnp.einsum("rd,rk->dk", normed, dqkv, preferred_element_type=F32)
    grad_w_qkv, dqkv = lax.optimization_barrier((grad_w_qkv.astype(BF), dqkv))
    grad_w_qkv, grad_w_o, sum_gu = lax.optimization_barrier((grad_w_qkv, grad_w_o, sum_gu))
    sum_qkv = reduce_z(grad_w_qkv)
    sum_o = head_cols.scatter(grad_w_o)
    grad_normed, output = plane_dot_scatter(dqkv, w_qkv, NT, seqs, 8, swapped=result)
    gain_one_part = jnp.sum(grad_normed * x * scale_one, axis=0)
    grad_x = grad_hidden_one + norm_back(grad_normed, x, scale_one, gain_one)

    grad_table = jnp.dot(grad_offset, one_hot, precision=HIGHEST)
    bias_all = jnp.zeros((fs * cs, heads, buckets_n), F32)
    bias_all = lax.dynamic_update_index_in_dim(bias_all, grad_table, plane_index, 0)
    bias_all = jnp.repeat(bias_all.transpose(0, 2, 1), head_dim, axis=2)
    bias_all = head_cols.join(bias_all)[:, ::head_dim].T.reshape(fs * zs * cs, -1)
    small_grad = jnp.concatenate(
        [
            gain_one_part.reshape(fs * zs * cs, -1),
            gain_two_part.reshape(fs * zs * cs, -1),
            bias_all,
        ],
        axis=1,
    )
    small_sum, grad_tokens = finish(
        to_tiles(small_grad), grad_x.astype(BF).reshape(seqs, block_len, width), 10
    )
    small_grad = small_sum.reshape(-1)[: small_grad.shape[1]]

    got_gu = unspread(sum_gu)
    got_qkv = unspread(sum_qkv)
    hw = heads * head_dim
    grads_qkv = [
        head_cols.join(got_qkv[:, :, i * hw : (i + 1) * hw]).astype(F32) for i in range(3)
    ]
    grads_gu = [ff_cols.join(got_gu[:, :, i * ff : (i + 1) * ff]).astype(F32) for i in range(2)]
    return (
        output,
        grad_tokens,
        small_grad[:g],
        small_grad[2 * g :],
        grads_qkv[0],
        grads_qkv[1],
        grads_qkv[2],
        sum_o.astype(F32),
        small_grad[g : 2 * g],
        grads_gu[0],
        grads_gu[1],
        sum_down.astype(F32),
    )


def solution(mesh):
    fs, ctx = mesh.shape["fsdp"], mesh.shape["ctx"]
    mesh3 = Mesh(mesh.devices.reshape(fs, ctx // 2, 2), ALL)
    act = P("fsdp", ("z", "core"), None)
    vec, mat = P(ALL), P(ALL, None)
    in_specs = (act, act, P("fsdp"), P(), vec, vec, mat, mat, mat, mat, vec, mat, mat, mat)
    out_specs = (act, act, vec, vec, mat, mat, mat, mat, vec, mat, mat, mat)
    return jax.shard_map(shards, mesh=mesh3, in_specs=in_specs, out_specs=out_specs, check_vma=False)
```

```python
import functools, math
import jax, jax.numpy as jnp
from jax import lax
from jax.experimental import pallas as pl
from jax.experimental.pallas import tpu as pltpu

MASKED = -1e30
NT = (((1,), (1,)), ((), ()))
NN = (((1,), (0,)), ((), ()))


def dotf(a, b, dims=NN):
    return lax.dot_general(a, b, dims, preferred_element_type=jnp.float32)


def head_mask(width, head_dim, h):
    lane = lax.broadcasted_iota(jnp.int32, (1, width), 1)
    return (lane // head_dim == h).astype(jnp.float32).astype(jnp.bfloat16)


def fill_skew(bias_ref, skew_ref, heads, block, length):
    for h in range(heads):
        rows = jnp.broadcast_to(bias_ref[h : h + 1, :], (block, 2 * length))
        rolled = pltpu.roll(rows, 2 * length - (block - 1), 1, stride=1, stride_axis=0)
        skew_ref[h] = rolled[:, : 2 * length - block]


def attn_fwd_kernel(
    heads, head_dim, block, length, lens_ref, q_ref, k_ref, v_ref, bias_ref, out_ref, lse_ref,
    skew_ref, kt_ref,
):
    seq, blk = pl.program_id(0), pl.program_id(1)
    width = heads * head_dim

    @pl.when((seq == 0) & (blk == 0))
    def _():
        fill_skew(bias_ref, skew_ref, heads, block, length)

    @pl.when(blk == 0)
    def _():
        kt_ref[...] = k_ref[...].T

    valid_len = lens_ref[seq]
    key_pos = lax.broadcasted_iota(jnp.int32, (1, length), 1)
    key_mask = jnp.where(key_pos < valid_len, 0.0, MASKED)
    start = pl.multiple_of(length - block - blk * block, block)
    lane = lax.broadcasted_iota(jnp.int32, (block, 128), 1)
    out = jnp.zeros((block, width), jnp.float32)
    lse_all = jnp.zeros((block, 128), jnp.float32)
    for h in range(heads):
        mask = head_mask(width, head_dim, h)
        scores = dotf(q_ref[...] * mask, kt_ref[...])
        scores = scores + skew_ref[h, :, pl.ds(start, length)] + key_mask
        peak = jnp.max(scores, axis=1, keepdims=True)
        probs = jnp.exp(scores - peak)
        mass = jnp.sum(probs, axis=1, keepdims=True)
        probs = (probs * (1.0 / mass)).astype(jnp.bfloat16)
        out = out + dotf(probs, v_ref[...] * mask)
        lse_all = jnp.where(lane == h, peak + jnp.log(mass), lse_all)
    out_ref[...] = out.astype(jnp.bfloat16)
    lse_ref[...] = lse_all


def attn_fwd(qkv, offset_bias, lens, heads, head_dim, seqs, block=256):
    rows, width3 = qkv.shape
    width = width3 // 3
    length = rows // seqs
    block = min(block, length)
    blocks = length // block
    return pl.pallas_call(
        functools.partial(attn_fwd_kernel, heads, head_dim, block, length),
        grid_spec=pltpu.PrefetchScalarGridSpec(
            num_scalar_prefetch=1,
            grid=(seqs, blocks),
            in_specs=[
                pl.BlockSpec((block, width), lambda s, i, lens: (s * blocks + i, 0)),
                pl.BlockSpec((length, width), lambda s, i, lens: (s, 1)),
                pl.BlockSpec((length, width), lambda s, i, lens: (s, 2)),
                pl.BlockSpec((heads, 2 * length), lambda s, i, lens: (0, 0)),
            ],
            out_specs=[
                pl.BlockSpec((block, width), lambda s, i, lens: (s * blocks + i, 0)),
                pl.BlockSpec((block, 128), lambda s, i, lens: (s * blocks + i, 0)),
            ],
            scratch_shapes=[
                pltpu.VMEM((heads, block, 2 * length - block), jnp.float32),
                pltpu.VMEM((width, length), jnp.bfloat16),
            ],
        ),
        out_shape=[
            jax.ShapeDtypeStruct((rows, width), jnp.bfloat16),
            jax.ShapeDtypeStruct((rows, 128), jnp.float32),
        ],
        compiler_params=pltpu.CompilerParams(
            dimension_semantics=("arbitrary", "arbitrary"), vmem_limit_bytes=56 * 1024 * 1024
        ),
        cost_estimate=estimate(26),
        name="attn_fwd",
    )(lens, qkv, qkv, qkv, offset_bias)


def attn_bwd_kernel(
    heads, head_dim, block, length, seqs, fs, lens_ref, q_ref, k_ref, v_ref, g_ref, lse_ref,
    bias_ref, *refs,
):
    seq, blk = pl.program_id(0), pl.program_id(1)
    blocks = length // block
    last_seq, last_blk = seqs - 1, blocks - 1
    grid_step = seq * blocks + blk
    steps = seqs * blocks
    if fs:
        x_ref, wg_ref, gu_ref, dq_ref, dk_ref, dv_ref, dbias_ref = refs[:7]
        out_ref, sum_ref, got_ref = refs[7:10]
        refs = refs[10:]
        column = Column(wg_ref, sum_ref, refs[6:9])
        back = Back((fs, 1, 2), gu_ref, got_ref, refs[9:12])
        swap = Swap(x_ref, out_ref, refs[12:])

        def begin():
            plane_and_column_greet()
            swap.start()
            column.start()
            back.start()

        todo = {0: begin, steps // 2: swap.hand_on}
        for step, action in todo.items():
            pl.when(grid_step == step)(action)
    else:
        dq_ref, dk_ref, dv_ref, dbias_ref = refs[:4]
        refs = refs[4:]
    skew_ref, kt_ref, vt_ref, acc_ref, dkt_ref, dvt_ref = refs[:6]
    width = heads * head_dim

    @pl.when((seq == 0) & (blk == 0))
    def _():
        fill_skew(bias_ref, skew_ref, heads, block, length)
        acc_ref[...] = jnp.zeros_like(acc_ref)

    @pl.when(blk == 0)
    def _():
        kt_ref[...] = k_ref[...].T
        vt_ref[...] = v_ref[...].T
        dkt_ref[...] = jnp.zeros_like(dkt_ref)
        dvt_ref[...] = jnp.zeros_like(dvt_ref)

    valid_len = lens_ref[seq]
    key_pos = lax.broadcasted_iota(jnp.int32, (1, length), 1)
    key_mask = jnp.where(key_pos < valid_len, 0.0, MASKED)
    start = pl.multiple_of(length - block - blk * block, block)
    q_t = q_ref[...].T
    g_t = g_ref[...].T
    dq = jnp.zeros((block, width), jnp.float32)
    row = lax.broadcasted_iota(jnp.int32, (width, 1), 0)
    for h in range(heads):
        mask = head_mask(width, head_dim, h)
        rmask = (row // head_dim == h).astype(jnp.float32).astype(jnp.bfloat16)
        scores = dotf(q_ref[...] * mask, kt_ref[...])
        scores = scores + skew_ref[h, :, pl.ds(start, length)] + key_mask
        probs = jnp.exp(scores - lse_ref[:, h : h + 1])
        grad_probs = dotf(g_ref[...] * mask, vt_ref[...])
        delta = jnp.sum(probs * grad_probs, axis=1, keepdims=True)
        ds = (probs * (grad_probs - delta)).astype(jnp.bfloat16)
        dq = dq + dotf(ds, k_ref[...] * mask)
        acc_ref[h, :, pl.ds(start, length)] += ds.astype(jnp.float32)
        dkt_ref[...] += dotf(q_t * rmask, ds)
        dvt_ref[...] += dotf(g_t * rmask, probs.astype(jnp.bfloat16))
    dq_ref[...] = dq.astype(jnp.bfloat16)

    @pl.when(blk == last_blk)
    def _():
        dk_ref[...] = dkt_ref[...].astype(jnp.bfloat16).T
        dv_ref[...] = dvt_ref[...].astype(jnp.bfloat16).T

    @pl.when((seq == last_seq) & (blk == last_blk))
    def _():
        for h in range(heads):
            part = jnp.concatenate(
                [acc_ref[h], jnp.zeros((block, block), jnp.float32)], axis=1
            )
            n = block
            while n > 8:
                n //= 2
                part = pltpu.roll(part[:n], n, 1) + part[n:]
            total = jnp.zeros((1, 2 * length), jnp.float32)
            for i in range(n):
                total = total + (pltpu.roll(part, n - 1 - i, 1) if i < n - 1 else part)[i : i + 1]
            dbias_ref[h : h + 1, :] = total

    if fs:

        @pl.when(grid_step == steps - 1)
        def _():
            column.close()
            back.arrived()
            back.close()
            swap.close()


def attn_bwd(
    qkv, grad, lse, offset_bias, lens, heads, head_dim, seqs, block=256, swapped=None,
    column=None, spread=None, collective_id=None,
):
    rows, width3 = qkv.shape
    width = width3 // 3
    length = rows // seqs
    block = min(block, length)
    blocks = length // block
    in_specs = [
        pl.BlockSpec(memory_space=pltpu.SMEM),
        pl.BlockSpec((block, width), lambda s, i: (s * blocks + i, 0)),
        pl.BlockSpec((length, width), lambda s, i: (s, 1)),
        pl.BlockSpec((length, width), lambda s, i: (s, 2)),
        pl.BlockSpec((block, width), lambda s, i: (s * blocks + i, 0)),
        pl.BlockSpec((block, 128), lambda s, i: (s * blocks + i, 0)),
        pl.BlockSpec((heads, 2 * length), lambda s, i: (0, 0)),
    ]
    out_specs = [
        pl.BlockSpec((block, width), lambda s, i: (s * blocks + i, 0)),
        pl.BlockSpec((length, width), lambda s, i: (s, 0)),
        pl.BlockSpec((length, width), lambda s, i: (s, 0)),
        pl.BlockSpec((heads, 2 * length), lambda s, i: (0, 0)),
    ]
    out_shape = [
        jax.ShapeDtypeStruct((rows, width), jnp.bfloat16),
        jax.ShapeDtypeStruct((rows, width), jnp.bfloat16),
        jax.ShapeDtypeStruct((rows, width), jnp.bfloat16),
        jax.ShapeDtypeStruct((heads, 2 * length), jnp.float32),
    ]
    scratch = [
        pltpu.VMEM((heads, block, 2 * length - block), jnp.float32),
        pltpu.VMEM((width, length), jnp.bfloat16),
        pltpu.VMEM((width, length), jnp.bfloat16),
        pltpu.VMEM((heads, block, 2 * length - block), jnp.float32),
        pltpu.VMEM((width, length), jnp.float32),
        pltpu.VMEM((width, length), jnp.float32),
    ]
    args = [lens, qkv, qkv, qkv, grad, lse, offset_bias]
    fs = 0
    if swapped is not None:
        fs, zs = lax.axis_size("fsdp"), lax.axis_size("z")
        column = column.reshape(zs, -1, column.shape[1])
        spread = spread.reshape(2 * fs, -1, spread.shape[2])
        args += [swapped, column, spread]
        in_specs += [vmem()] * 3
        out_specs += [anywhere(), vmem(), anywhere()]
        out_shape += [
            jax.ShapeDtypeStruct(swapped.shape, swapped.dtype),
            jax.ShapeDtypeStruct(column.shape[1:], jnp.float32),
            jax.ShapeDtypeStruct(spread.shape, spread.dtype),
        ]
        scratch += Column.scratch(column) + Back.scratch(2 * fs)
        scratch += Swap.scratch(fs, *swapped.shape)
    return pl.pallas_call(
        functools.partial(attn_bwd_kernel, heads, head_dim, block, length, seqs, fs),
        grid=(seqs, blocks),
        in_specs=in_specs,
        out_specs=out_specs,
        out_shape=out_shape,
        scratch_shapes=scratch,
        compiler_params=pltpu.CompilerParams(
            dimension_semantics=("arbitrary", "arbitrary"), vmem_limit_bytes=62 * 1024 * 1024,
            collective_id=collective_id, has_side_effects=fs > 0,
        ),
        cost_estimate=estimate(50),
        name="attn_bwd",
    )(*args)

MESH_ID = pl.DeviceIdType.MESH
MIB = 1024 * 1024


def remote_copy(src, dst, send_sem, recv_sem, device):
    return pltpu.make_async_remote_copy(
        src_ref=src, dst_ref=dst, send_sem=send_sem, recv_sem=recv_sem, device_id=device,
        device_id_type=MESH_ID,
    )


def landed(ref, sem):
    pltpu.make_async_copy(ref, ref, sem).wait()


def estimate(us):
    return pl.CostEstimate(flops=int(us * 0.02 * 1.1e9), bytes_accessed=int(us * 1e5), transcendentals=0)


def flip(f, bits):
    k = 1
    while k <= bits:
        if bits & k:
            f = f + (1 - 2 * (lax.rem(lax.div(f, k), 2))) * k
        k *= 2
    return f


class Plane:
    def __init__(self, fs):
        self.fs = fs
        self.f, self.z, self.c = (lax.axis_index(a) for a in ("fsdp", "z", "core"))
        self.bits = [1 << i for i in range(fs.bit_length() - 1)]
        self.orders = [self.bits, self.bits[::-1]]
        self.steps = len(self.bits)

    def peer(self, bit):
        return (flip(self.f, bit), self.z, self.c)

    def mate(self):
        return (self.f, self.z, 1 - self.c)

    def slot(self, rel, other=False):
        c = 1 - self.c if other else self.c
        return flip(self.f, rel) * 2 + c

    def barrier(self):
        bar = pltpu.get_barrier_semaphore()
        for dev in [self.mate()] + [self.peer(b) for b in self.bits]:
            pl.semaphore_signal(bar, inc=1, device_id=dev, device_id_type=MESH_ID)
        pl.semaphore_wait(bar, 1 + self.steps)


def gather_sems(fs):
    steps = fs.bit_length() - 1
    return [
        pltpu.SemaphoreType.DMA((2, steps, fs)),
        pltpu.SemaphoreType.DMA((2, fs)),
        pltpu.SemaphoreType.DMA((2, fs)),
        pltpu.SemaphoreType.DMA((2, fs)),
    ]


def run_gather(plane, x_ref, buf_ref, sems, consume):
    send, recv, mate_send, mate_recv = sems
    started = []

    def remote(*args):
        copy = remote_copy(*args)
        copy.start()
        started.append(copy)
        return copy

    def source(p, rel):
        return x_ref.at[p] if rel == 0 else buf_ref.at[p, plane.slot(rel)]

    def to_mate(p, rel):
        remote(
            source(p, rel), buf_ref.at[p, plane.slot(rel)], mate_send.at[p, rel],
            mate_recv.at[p, rel], plane.mate(),
        )

    def to_peer(p, step, rel):
        bit = plane.orders[p][step]
        return remote(
            source(p, rel), buf_ref.at[p, plane.slot(rel)], send.at[p, step, rel],
            recv.at[p, rel ^ bit], plane.peer(bit),
        )

    def finish(pairs):
        for p, rel in pairs:
            landed(buf_ref.at[p, plane.slot(rel, True)], mate_recv.at[p, rel])
            if consume is not None:
                consume(p, flip(plane.f, rel) * 2)

    first = [to_peer(p, 0, 0) for p in range(2)]
    for p in range(2):
        to_mate(p, 0)
    if consume is not None:
        for p in range(2):
            buf_ref[p, plane.slot(0)] = x_ref[p]
    have = [[0], [0]]
    pending = [(0, 0), (1, 0)]
    for step in range(plane.steps):
        for i in range(len(have[0])):
            finish(pending)
            if i == 0 and step + 1 < plane.steps:
                for copy in first:
                    copy.wait_send()
                    started[:] = [other for other in started if other is not copy]
                first = [to_peer(p, step + 1, 0) for p in range(2)]
            pending = [(p, have[p][i] ^ plane.orders[p][step]) for p in range(2)]
            for p, rel in pending:
                landed(buf_ref.at[p, plane.slot(rel)], recv.at[p, rel])
                to_mate(p, rel)
                for later in range(step + 1, plane.steps):
                    to_peer(p, later, rel)
        for p in range(2):
            have[p] = have[p] + [rel ^ plane.orders[p][step] for rel in have[p]]
    finish(pending)
    for copy in started:
        copy.wait_send()


def scatter_scratch(fs, b, width):
    return [
        pltpu.VMEM((2, fs, b, width), jnp.bfloat16),
        pltpu.VMEM((2, fs, b, width), jnp.bfloat16),
        pltpu.VMEM((2, fs // 2, b, width), jnp.float32),
        pltpu.VMEM((2, fs, b, width), jnp.bfloat16),
        pltpu.VMEM((2, fs - 1, b, width), jnp.bfloat16),
        pltpu.SemaphoreType.DMA((fs,)),
        pltpu.SemaphoreType.DMA((fs,)),
        pltpu.SemaphoreType.DMA((2, fs)),
        pltpu.SemaphoreType.DMA((2, fs - 1)),
    ]


def scatter_actions(plane, partial, tile, width, out_ref, scratch):
    give, got, total, outbox, inbox, give_sem, got_sem, send, recv = scratch
    b = out_ref.shape[1]
    rels = sorted(range(plane.fs), key=lambda r: (-bin(r).count("1"), r))
    tiles = width // tile

    def each_tile(body):
        def one(j, carry):
            body(pl.ds(pl.multiple_of(j * tile, tile), tile))
            return carry

        lax.fori_loop(0, tiles, one, 0)

    def leaves(p, rel):
        for step, bit in enumerate(plane.orders[p]):
            if rel & bit:
                return step
        return plane.steps

    def place(p, step, rel):
        kept = [r for r in range(plane.fs) if leaves(p, r) > step]
        return plane.fs - 2 * len(kept) + kept.index(rel)

    def held(p, rel):
        return [r for r in range(plane.fs) if leaves(p, r) > 0].index(rel)

    def to_peer(p, rel):
        step = leaves(p, rel)
        bit = plane.orders[p][step]
        at = place(p, step, rel ^ bit)
        return remote_copy(
            outbox.at[p, rel], inbox.at[p, at], send.at[p, rel], recv.at[p, at], plane.peer(bit)
        )

    def to_mate(rel):
        return remote_copy(
            give.at[:, rel], got.at[:, rel], give_sem.at[rel], got_sem.at[rel], plane.mate()
        )

    def give_part(rel):
        theirs = plane.slot(rel, True)

        def body(cols):
            part = partial(theirs, cols).astype(jnp.bfloat16)
            give[0, rel, :, cols] = part[:b]
            give[1, rel, :, cols] = part[b:]

        each_tile(body)
        to_mate(rel).start()

    def own_part(rel):
        mine = plane.slot(rel)
        landed(got.at[:, rel], got_sem.at[rel])

        def body(cols):
            part = partial(mine, cols)
            for p in range(2):
                here = part[p * b : (p + 1) * b] + got[p, rel, :, cols].astype(jnp.float32)
                if leaves(p, rel) == 0:
                    outbox[p, rel, :, cols] = here.astype(jnp.bfloat16)
                else:
                    total[p, held(p, rel), :, cols] = here

        each_tile(body)
        for p in range(2):
            if leaves(p, rel) == 0:
                to_peer(p, rel).start()

    def add_part(step, rel, p):
        at = place(p, step, rel)
        landed(inbox.at[p, at], recv.at[p, at])
        sends = leaves(p, rel) == step + 1

        def body(cols):
            here = total[p, held(p, rel), :, cols] + inbox[p, at, :, cols].astype(jnp.float32)
            if step + 1 == plane.steps:
                out_ref[p, :, cols] = here
            elif sends:
                outbox[p, rel, :, cols] = here.astype(jnp.bfloat16)
            else:
                total[p, held(p, rel), :, cols] = here

        each_tile(body)
        if sends and step + 1 < plane.steps:
            to_peer(p, rel).start()

    def close():
        for rel in rels:
            to_mate(rel).wait_send()
            for p in range(2):
                if leaves(p, rel) < plane.steps:
                    to_peer(p, rel).wait_send()

    actions = [functools.partial(give_part, rels[0])]
    for i, rel in enumerate(rels):
        if i + 1 < len(rels):
            actions.append(functools.partial(give_part, rels[i + 1]))
        actions.append(functools.partial(own_part, rel))
    for step in range(plane.steps):
        for rel in rels:
            for p in range(2):
                if leaves(p, rel) > step:
                    actions.append(functools.partial(add_part, step, rel, p))
    return actions + [close]


def vmem():
    return pl.BlockSpec(memory_space=pltpu.VMEM)


def anywhere():
    return pl.BlockSpec(memory_space=pl.ANY)


def plane_params(collective_id, limit=58):
    return pltpu.CompilerParams(
        collective_id=collective_id, has_side_effects=True, vmem_limit_bytes=limit * MIB
    )


def gather_dot_kernel(fs, dims, tile, other, x_ref, w_ref, *refs):
    plane = Plane(fs)
    plane.barrier()
    if other:
        o_ref, full_ref, y_ref, wg_ref, buf_ref, acc_ref = refs[:6]
        sems = refs[6:]
        acc_ref[...] = jnp.zeros_like(acc_ref)
    else:
        full_ref, y_ref, buf_ref = refs[:3]
        sems = refs[3:]
    keep_sem = sems[4]
    b, width = buf_ref.shape[2:]
    columns = y_ref.shape[3]
    kept = []

    def consume(p, slot):
        two = pl.ds(slot, 2)
        cp = pltpu.make_async_copy(
            buf_ref.at[p, two], full_ref.at[p, two], keep_sem.at[len(kept)]
        )
        cp.start()
        kept.append(cp)

        def product(cols):
            w = w_ref[:, cols] if dims == NN else w_ref[cols, :]
            y = dotf(buf_ref[p, two].reshape(2 * b, width), w, dims)
            y_ref[p, two, :, cols] = y.astype(y_ref.dtype).reshape(2, b, tile)

        def one(j, carry):
            product(pl.ds(pl.multiple_of(j * tile, tile), tile))
            return carry

        if tile == columns:
            product(slice(None))
        else:
            lax.fori_loop(0, columns // tile, one, 0)
        if other:
            o_t = o_ref[p, two].reshape(2 * b, -1).T

            def grad(j, carry):
                cols = pl.ds(pl.multiple_of(j * 256, 256), 256)
                acc_ref[:, cols] += dotf(o_t, buf_ref[p, two, :, cols].reshape(2 * b, 256))
                return carry

            lax.fori_loop(0, width // 256, grad, 0)

    run_gather(plane, x_ref, buf_ref, sems[:4], consume)
    if other:
        wg_ref[...] = acc_ref[...].astype(wg_ref.dtype)
    for cp in kept:
        cp.wait()


def plane_gather_dot(x, w, dims, seqs, collective_id, other=None, dtype=jnp.bfloat16):
    fs = lax.axis_size("fsdp")
    x = x.reshape(seqs, -1, x.shape[1])
    _, b, width = x.shape
    columns = w.shape[1] if dims == NN else w.shape[0]
    tile = next((t for t in (256, 128) if columns % t == 0), columns)
    lead = (seqs, 2 * fs, b)
    out_shape = [
        jax.ShapeDtypeStruct(lead + (width,), x.dtype),
        jax.ShapeDtypeStruct(lead + (columns,), dtype),
    ]
    args, scratch = [x, w], [pltpu.VMEM(lead + (width,), x.dtype)]
    if other is not None:
        args.append(other.reshape(lead + (-1,)))
        out_shape.append(jax.ShapeDtypeStruct((other.shape[1], width), jnp.bfloat16))
        scratch.append(pltpu.VMEM((other.shape[1], width), jnp.float32))
    out = pl.pallas_call(
        functools.partial(gather_dot_kernel, fs, dims, tile, other is not None),
        out_shape=out_shape,
        in_specs=[vmem()] * len(args),
        out_specs=[anywhere()] + [vmem()] * (len(out_shape) - 1),
        scratch_shapes=scratch + gather_sems(fs) + [pltpu.SemaphoreType.DMA((seqs * fs,))],
        compiler_params=plane_params(collective_id),
        cost_estimate=estimate(45),
        name="plane_gather_dot",
    )(*args)
    return (out[0].reshape(-1, width), out[1].reshape(-1, columns)) + tuple(out[2:])


class Swap:
    def __init__(self, x_ref, out_ref, scratch):
        self.x_ref, self.out_ref = x_ref, out_ref
        self.relay, self.own_sem, self.in_send, self.in_recv, self.on_send, self.on_recv = scratch
        self.f, self.z, self.c = (lax.axis_index(a) for a in ("fsdp", "z", "core"))
        self.fs, self.size = self.relay.shape[:2]

    @staticmethod
    def scratch(fs, rows, width):
        dma = pltpu.SemaphoreType.DMA
        return [
            pltpu.VMEM((fs, rows // fs, width), jnp.bfloat16), dma,
            dma((fs,)), dma((fs,)), dma((fs,)), dma((fs,)),
        ]

    def column(self, d):
        return lax.rem(self.f + d, self.fs)

    def part(self, ref, k):
        return ref.at[pl.ds(pl.multiple_of(k * self.size, self.size), self.size)]

    def straight(self):
        return remote_copy(
            self.part(self.x_ref, self.f), self.part(self.out_ref, self.f), self.in_send.at[0],
            self.on_recv.at[self.f], (self.z, self.f, self.c),
        )

    def inward(self, d):
        k = self.column(d)
        return remote_copy(
            self.part(self.x_ref, k), self.relay.at[d], self.in_send.at[d],
            self.in_recv.at[d], (k, self.z, self.c),
        )

    def onward(self, d):
        source = self.column(self.fs - d)
        return remote_copy(
            self.relay.at[d], self.part(self.out_ref, self.f), self.on_send.at[d],
            self.on_recv.at[self.f], (self.z, source, self.c),
        )

    def own(self):
        return pltpu.make_async_copy(self.x_ref, self.out_ref, self.own_sem)

    def start_inward(self):
        @pl.when(self.f != self.z)
        def _():
            for d in range(1, self.fs):
                self.inward(d).start()

    def start_straight(self):
        @pl.when(self.f != self.z)
        def _():
            self.straight().start()

        @pl.when(self.f == self.z)
        def _():
            self.own().start()

    def start(self):
        self.start_inward()
        self.start_straight()

    def relayed(self, body):
        for d in range(1, self.fs):

            @pl.when(self.column(self.fs - d) != self.z)
            def _(d=d):
                body(d)

    def hand_on(self):
        def one(d):
            landed(self.relay.at[d], self.in_recv.at[d])
            self.onward(d).start()

        self.relayed(one)

    def close(self):
        self.relayed(lambda d: self.onward(d).wait_send())

        @pl.when(self.f == self.z)
        def _():
            self.own().wait()

        @pl.when(self.f != self.z)
        def _():
            self.straight().wait_send()
            for d in range(1, self.fs):
                self.inward(d).wait_send()
            for k in range(self.fs):
                landed(self.part(self.out_ref, k), self.on_recv.at[k])


def plane_and_column_greet():
    fs, zs, cs = (lax.axis_size(a) for a in ("fsdp", "z", "core"))
    f, z, c = (lax.axis_index(a) for a in ("fsdp", "z", "core"))
    bar = pltpu.get_barrier_semaphore()
    places = [(lax.rem(f + df, fs), z, lax.rem(c + dc, cs)) for df in range(fs) for dc in range(cs)]
    places = places[1:] + [(f, lax.rem(z + dz, zs), c) for dz in range(1, zs)]
    places += [
        (lax.rem(f + df, fs), lax.rem(z + dz, zs), c) for df in range(1, fs) for dz in range(1, zs)
    ]
    for place in places:
        pl.semaphore_signal(bar, inc=1, device_id=place, device_id_type=MESH_ID)
    pl.semaphore_wait(bar, len(places))


class Column:
    def __init__(self, x_ref, sum_ref, scratch):
        self.x_ref, self.sum_ref = x_ref, sum_ref
        self.inbox, self.send, self.recv = scratch
        self.f, self.z, self.c = (lax.axis_index(a) for a in ("fsdp", "z", "core"))
        self.zs = x_ref.shape[0]

    @staticmethod
    def scratch(x):
        dma = pltpu.SemaphoreType.DMA
        return [pltpu.VMEM(x.shape, x.dtype), dma((x.shape[0],)), dma((x.shape[0],))]

    def copy(self, d):
        to = lax.rem(self.z + d, self.zs)
        return remote_copy(
            self.x_ref.at[to], self.inbox.at[d], self.send.at[d], self.recv.at[d],
            (self.f, to, self.c),
        )

    def start(self):
        for d in range(1, self.zs):
            self.copy(d).start()

    def close(self):
        for d in range(1, self.zs):
            self.copy(d).wait_send()
            landed(self.inbox.at[d], self.recv.at[d])
        total = self.x_ref[self.z].astype(jnp.float32)
        for d in range(1, self.zs):
            total = total + self.inbox[d].astype(jnp.float32)
        self.sum_ref[...] = total


class Back:
    def __init__(self, sizes, src_ref, got_ref, scratch):
        fs, zs, self.cs = sizes
        self.src_ref, self.got_ref = src_ref, got_ref
        self.send, self.recv, self.own_sem = scratch
        self.z = lax.axis_index("z")
        self.devices = fs * self.cs
        self.me = lax.axis_index("fsdp") * self.cs + lax.axis_index("core")

    @staticmethod
    def scratch(devices):
        dma = pltpu.SemaphoreType.DMA
        return [dma((devices,)), dma((devices,)), dma]

    def copy(self, d):
        to = lax.rem(self.me + d, self.devices)
        return remote_copy(
            self.src_ref.at[to], self.got_ref.at[self.me], self.send.at[d], self.recv.at[d],
            (lax.div(to, self.cs), self.z, lax.rem(to, self.cs)),
        )

    def own(self):
        return pltpu.make_async_copy(
            self.src_ref.at[self.me], self.got_ref.at[self.me], self.own_sem
        )

    def start(self):
        for d in range(1, self.devices):
            self.copy(d).start()
        self.own().start()

    def arrived(self):
        for d in range(1, self.devices):
            at = lax.rem(self.me + self.devices - d, self.devices)
            landed(self.got_ref.at[at], self.recv.at[d])
        self.own().wait()

    def close(self):
        for d in range(1, self.devices):
            self.copy(d).wait_send()


class Everyone:
    def __init__(self, sizes):
        self.fs, self.zs, self.cs = sizes
        self.n = math.prod(sizes)
        f, z, c = (lax.axis_index(a) for a in ("fsdp", "z", "core"))
        self.me = (f * self.zs + z) * self.cs + c

    def place(self, d):
        f, z, c = (lax.axis_index(a) for a in ("fsdp", "z", "core"))
        df, dz, dc = d // (self.zs * self.cs), d // self.cs % self.zs, d % self.cs
        return (lax.rem(f + df, self.fs), lax.rem(z + dz, self.zs), lax.rem(c + dc, self.cs))

    def index(self, place):
        return (place[0] * self.zs + place[1]) * self.cs + place[2]

    def back(self, d):
        f, z, c = (lax.axis_index(a) for a in ("fsdp", "z", "core"))
        df, dz, dc = d // (self.zs * self.cs), d // self.cs % self.zs, d % self.cs
        return self.index((
            lax.rem(f + self.fs - df, self.fs), lax.rem(z + self.zs - dz, self.zs),
            lax.rem(c + self.cs - dc, self.cs),
        ))

    def greet(self):
        bar = pltpu.get_barrier_semaphore()
        for d in range(1, self.n):
            pl.semaphore_signal(bar, inc=1, device_id=self.place(d), device_id_type=MESH_ID)

    def met(self):
        pl.semaphore_wait(pltpu.get_barrier_semaphore(), self.n - 1)

    def copy(self, d, x_ref, spread_out, slots, send, recv):
        to = self.place(d)
        src = x_ref.at[self.index(to)] if spread_out else x_ref.at[0]
        return remote_copy(src, slots.at[self.me], send.at[d], recv.at[d], to)

    def begin(self, x_ref, spread_out, slots, send, recv, own_sem):
        for d in range(1, self.n):
            self.copy(d, x_ref, spread_out, slots, send, recv).start()
        src = x_ref.at[self.me] if spread_out else x_ref.at[0]
        own = pltpu.make_async_copy(src, slots.at[self.me], own_sem)
        own.start()
        own.wait()

    def finish(self, x_ref, spread_out, slots, send, recv):
        for d in range(1, self.n):
            landed(slots.at[self.back(d)], recv.at[d])
        for d in range(1, self.n):
            self.copy(d, x_ref, spread_out, slots, send, recv).wait_send()


def dot_scatter_kernel(fs, dims, tile, beside, a_ref, w_ref, *refs):
    plane = Plane(fs)
    plane.barrier()
    if beside:
        l_hbm, r_hbm, out_ref, g_ref, l_ref, r_ref, l_sem, r_sem = refs[:8]
        scratch = refs[8:]
        loads = [
            pltpu.make_async_copy(l_hbm, l_ref, l_sem), pltpu.make_async_copy(r_hbm, r_ref, r_sem)
        ]
        for load in loads:
            load.start()
    else:
        out_ref, scratch = refs[0], refs[1:]

    def partial(slot, cols):
        a = a_ref[:, slot].reshape(-1, a_ref.shape[3])
        return dotf(a, w_ref[:, cols] if dims == NN else w_ref[cols, :], dims)

    actions = scatter_actions(plane, partial, tile, out_ref.shape[2], out_ref, scratch)
    first = 2 * fs
    for action in actions[:first]:
        action()
    if beside:
        for load in loads:
            load.wait()
        block = 256

        def one(i, carry):
            here = pl.ds(pl.multiple_of(i * block, block), block)
            g_ref[here, :] = dotf(l_ref[:, here].T, r_ref[...]).astype(g_ref.dtype)
            return carry

        steps = l_ref.shape[1] // block
        lax.fori_loop(0, steps // 2, one, 0)
    middle = first + len(actions[first:-1]) - 2
    for action in actions[first:middle]:
        action()
    if beside:
        lax.fori_loop(steps // 2, steps, one, 0)
    for action in actions[middle:]:
        action()


def plane_dot_scatter(a, w, dims, seqs, collective_id, beside=None):
    fs = lax.axis_size("fsdp")
    a = a.reshape(seqs, 2 * fs, -1, a.shape[1])
    b = a.shape[2]
    width = w.shape[1] if dims == NN else w.shape[0]
    out_shape = [jax.ShapeDtypeStruct((seqs, b, width), jnp.float32)]
    args = [a, w]
    scratch = scatter_scratch(fs, b, width)
    if beside is not None:
        l, r = beside
        args += [l, r]
        dma = pltpu.SemaphoreType.DMA
        scratch = [pltpu.VMEM(l.shape, l.dtype), pltpu.VMEM(r.shape, r.dtype), dma, dma] + scratch
        out_shape.append(jax.ShapeDtypeStruct((l.shape[1], r.shape[1]), jnp.bfloat16))
    out = pl.pallas_call(
        functools.partial(dot_scatter_kernel, fs, dims, 256, beside is not None),
        out_shape=out_shape,
        in_specs=[vmem()] * 2 + [anywhere()] * (len(args) - 2),
        out_specs=[vmem()] * len(out_shape),
        scratch_shapes=scratch,
        compiler_params=plane_params(collective_id, 62),
        cost_estimate=estimate(45),
        name="plane_dot_scatter",
    )(*args)
    rows = out[0].reshape(-1, width)
    return rows if beside is None else (rows, out[1])


GELU_C = math.sqrt(2.0 / math.pi)


def gather_ffn_kernel(
    fs, x_ref, gh_hbm, g_hbm, wgu_ref, full_ref, h_ref, ggu_ref, wg_ref,
    buf_ref, gh_ref, g_ref, acc_ref, *sems
):
    plane = Plane(fs)
    gh_sem, g_sem = sems[5:]
    loads = [
        pltpu.make_async_copy(gh_hbm, gh_ref, gh_sem), pltpu.make_async_copy(g_hbm, g_ref, g_sem)
    ]
    for load in loads:
        load.start()
    plane.barrier()
    keep_sem = sems[4]
    ff = h_ref.shape[3]
    b, width = buf_ref.shape[2:]
    kept = []

    def consume(p, slot):
        two = pl.ds(slot, 2)
        cp = pltpu.make_async_copy(
            buf_ref.at[p, two], full_ref.at[p, two], keep_sem.at[len(kept)]
        )
        cp.start()
        if not kept:
            for load in loads:
                load.wait()
            acc_ref[...] = jnp.zeros_like(acc_ref)
        kept.append(cp)
        rows = buf_ref[p, two].reshape(2 * b, width)
        gate = dotf(rows, wgu_ref[:, :ff])
        up = dotf(rows, wgu_ref[:, ff:])
        grad_hidden = gh_ref[p, two].reshape(2 * b, ff)
        square = gate * gate
        tanh = jnp.tanh(GELU_C * gate * (1.0 + 0.044715 * square))
        half = 0.5 * (1.0 + tanh)
        act = gate * half
        slope = half + (0.5 * GELU_C) * gate * (1.0 - tanh * tanh) * (1.0 + 0.134145 * square)
        hidden = (act * up).astype(jnp.bfloat16)

        def put(ref, cols, value):
            ref[p, two, :, cols] = value.astype(jnp.bfloat16).reshape(2, b, ff)

        put(h_ref, slice(0, ff), hidden)
        put(ggu_ref, slice(0, ff), grad_hidden * up * slope)
        put(ggu_ref, slice(ff, 2 * ff), grad_hidden * act)
        hidden_t = hidden.T

        def grad(j, carry):
            cols = pl.ds(pl.multiple_of(j * 256, 256), 256)
            acc_ref[:, cols] += dotf(hidden_t, g_ref[p, two, :, cols].reshape(2 * b, 256))
            return carry

        lax.fori_loop(0, width // 256, grad, 0)

    run_gather(plane, x_ref, buf_ref, sems[:4], consume)
    wg_ref[...] = acc_ref[...].astype(jnp.bfloat16)
    for cp in kept:
        cp.wait()


def plane_gather_ffn(x, grad_hidden, grad, w_gu, seqs, collective_id):
    fs = lax.axis_size("fsdp")
    x = x.reshape(seqs, -1, x.shape[1])
    _, b, width = x.shape
    ff = grad_hidden.shape[1]
    lead = (seqs, 2 * fs, b)
    dma = pltpu.SemaphoreType.DMA
    full, h, ggu, wg = pl.pallas_call(
        functools.partial(gather_ffn_kernel, fs),
        out_shape=[
            jax.ShapeDtypeStruct(lead + (width,), x.dtype),
            jax.ShapeDtypeStruct(lead + (ff,), jnp.bfloat16),
            jax.ShapeDtypeStruct(lead + (2 * ff,), jnp.bfloat16),
            jax.ShapeDtypeStruct((ff, width), jnp.bfloat16),
        ],
        in_specs=[vmem(), anywhere(), anywhere(), vmem()],
        out_specs=[anywhere(), vmem(), vmem(), vmem()],
        scratch_shapes=[
            pltpu.VMEM(lead + (width,), x.dtype),
            pltpu.VMEM(lead + (ff,), jnp.float32),
            pltpu.VMEM(lead + (width,), x.dtype),
            pltpu.VMEM((ff, width), jnp.float32),
        ]
        + gather_sems(fs)
        + [dma((seqs * fs,)), dma, dma],
        compiler_params=plane_params(collective_id, 62),
        cost_estimate=estimate(45),
        name="plane_gather_ffn",
    )(x, grad_hidden.reshape(lead + (ff,)), grad.reshape(lead + (width,)), w_gu)
    return full.reshape(-1, width), h.reshape(-1, ff), ggu.reshape(-1, 2 * ff), wg

def column_runs(sizes, per_device, total, natural):
    fs, zs, cs = sizes
    if not natural:
        size = total // (fs * cs)
        return [(t * size, t, 0, size) for t in range(fs * cs)]
    return [
        (((f * zs + z) * cs + c) * per_device, f * cs + c, z * per_device, per_device)
        for f in range(fs) for z in range(zs) for c in range(cs)
    ]


def start_kernel(
    sizes, runs, small_ref, q_ref, k_ref, v_ref, gate_ref, up_ref, tok_ref, cot_ref, o_ref, d_ref,
    small_out, wqkv_ref, ggu_ref, x_ref, g_ref, o_out, d_out,
    slots, qkv_ref, gu_ref, s_send, s_recv, own_sem, q_send, q_recv, g_send, g_recv,
    line_send, line_recv, *swap_scratch,
):
    fs, zs, cs = sizes
    f, z, c = (lax.axis_index(a) for a in ("fsdp", "z", "core"))
    me = f * cs + c
    devices = fs * cs
    rows = qkv_ref.shape[1]
    everyone = Everyone(sizes)
    everyone.greet()

    def split(pieces_ref, parts, run):
        size = pieces_ref.shape[2] // len(parts)
        for i, part in enumerate(parts):
            for at, device, start, count in run:
                here = part[:, at : at + count].astype(jnp.bfloat16)
                pieces_ref[device, :, i * size + start : i * size + start + count] = here

    split(qkv_ref, (q_ref, k_ref, v_ref), runs[1])
    half = len(swap_scratch) // 2
    swaps = [
        Swap(tok_ref, x_ref, swap_scratch[:half]), Swap(cot_ref, g_ref, swap_scratch[half:])
    ]
    everyone.met()
    everyone.begin(small_ref, False, slots, s_send, s_recv, own_sem.at[0])

    def block(out_ref, index, lead):
        at = pl.ds(pl.multiple_of(lax.rem(index, cs) * rows, rows), rows)
        if lead is None:
            return out_ref.at[lax.div(index, cs), at]
        return out_ref.at[lax.div(index, cs), lead, at]

    def spread_copy(d, src_ref, out_ref, lead, send, recv):
        to = lax.rem(me + d, devices)
        return remote_copy(
            src_ref.at[to], block(out_ref, me, lead), send.at[d], recv.at[d],
            (lax.div(to, cs), z, lax.rem(to, cs)),
        )

    own_qkv = pltpu.make_async_copy(qkv_ref.at[me], block(wqkv_ref, me, z), own_sem.at[1])
    own_gu = pltpu.make_async_copy(gu_ref.at[me], block(ggu_ref, me, None), own_sem.at[2])
    own_qkv.start()
    for d in range(1, devices):
        spread_copy(d, qkv_ref, wqkv_ref, z, q_send, q_recv).start()
    swaps[0].start()
    split(gu_ref, (gate_ref, up_ref), runs[0])
    own_gu.start()
    o_out[...] = o_ref[...].astype(jnp.bfloat16)
    d_out[...] = d_ref[...].astype(jnp.bfloat16)
    own_qkv.wait()
    for d in range(1, devices):
        landed(block(wqkv_ref, lax.rem(me + devices - d, devices), z), q_recv.at[d])

    def line(step, way):
        source = lax.rem(z - way * step + zs, zs)
        to = lax.rem(z + way + zs, zs)
        k = 0 if way > 0 else 1
        ref = wqkv_ref.at[:, source]
        return remote_copy(ref, ref, line_send.at[k, step], line_recv.at[k, step], (f, to, c))

    def sends(step, way):
        if way > 0:
            return (z >= step) & (z < zs - 1)
        return (z < zs - step) & (z > 0)

    def arrives(step, way):
        return (z > step) if way > 0 else (z < zs - 1 - step)

    def arrive(step, way):
        k = 0 if way > 0 else 1
        source = lax.rem(z - way * (step + 1) + zs, zs)
        landed(wqkv_ref.at[:, source], line_recv.at[k, step])

    for step in range(zs - 1):
        for way in (1, -1):

            @pl.when(sends(step, way))
            def _(step=step, way=way):
                line(step, way).start()

        if step == 0:
            swaps[1].start_inward()
            for d in range(1, devices):
                spread_copy(d, gu_ref, ggu_ref, None, g_send, g_recv).start()
        if step == 1:
            swaps[1].start_straight()
        for way in (1, -1):

            @pl.when(arrives(step, way))
            def _(step=step, way=way):
                arrive(step, way)

        if step < 2:
            swaps[step].hand_on()

    everyone.finish(small_ref, False, slots, s_send, s_recv)
    small_out[...] = slots[...]
    own_gu.wait()
    for d in range(1, devices):
        landed(block(ggu_ref, lax.rem(me + devices - d, devices), None), g_recv.at[d])
    for d in range(1, devices):
        spread_copy(d, qkv_ref, wqkv_ref, z, q_send, q_recv).wait_send()
        spread_copy(d, gu_ref, ggu_ref, None, g_send, g_recv).wait_send()
    for step in range(zs - 1):
        for way in (1, -1):

            @pl.when(sends(step, way))
            def _(step=step, way=way):
                line(step, way).wait_send()

    for swap in swaps:
        swap.close()


def start(small, qkv, gu, tokens, cotangent, own_o, own_d, runs, collective_id):
    sizes = tuple(lax.axis_size(a) for a in ("fsdp", "z", "core"))
    fs, zs, cs = sizes
    n = math.prod(sizes)
    devices = fs * cs
    rows = qkv[0].shape[0]
    qkv_cols = sum(w.shape[1] for w in qkv) // devices
    gu_cols = sum(w.shape[1] for w in gu) // devices
    dma = pltpu.SemaphoreType.DMA
    return pl.pallas_call(
        functools.partial(start_kernel, sizes, runs),
        out_shape=[
            jax.ShapeDtypeStruct((n, 8, 128), jnp.float32),
            jax.ShapeDtypeStruct((fs, zs, cs * rows, qkv_cols), jnp.bfloat16),
            jax.ShapeDtypeStruct((fs, cs * rows, gu_cols), jnp.bfloat16),
            jax.ShapeDtypeStruct(tokens.shape, tokens.dtype),
            jax.ShapeDtypeStruct(cotangent.shape, cotangent.dtype),
            jax.ShapeDtypeStruct(own_o.shape, jnp.bfloat16),
            jax.ShapeDtypeStruct(own_d.shape, jnp.bfloat16),
        ],
        in_specs=[vmem()] * 10,
        out_specs=[vmem()] + [anywhere()] * 4 + [vmem()] * 2,
        scratch_shapes=[
            pltpu.VMEM((n, 8, 128), jnp.float32),
            pltpu.VMEM((devices, rows, qkv_cols), jnp.bfloat16),
            pltpu.VMEM((devices, rows, gu_cols), jnp.bfloat16),
            dma((n,)), dma((n,)), dma((3,)),
            dma((devices,)), dma((devices,)), dma((devices,)), dma((devices,)),
            dma((2, zs)), dma((2, zs)),
        ]
        + Swap.scratch(fs, *tokens.shape) * 2,
        compiler_params=plane_params(collective_id),
        cost_estimate=estimate(120),
        name="start",
    )(small, *qkv, *gu, tokens, cotangent, own_o, own_d)


def finish_kernel(
    sizes, runs, small_ref, g_ref, qkv_ref, gu_ref, small_out, out_ref, gate_ref, up_ref,
    q_ref, k_ref, v_ref, slots, got_qkv, send, recv, own_sem, back_send, back_recv, back_sem,
    *swap_scratch
):
    everyone = Everyone(sizes)
    everyone.greet()
    back = Back(sizes, qkv_ref, got_qkv, (back_send, back_recv, back_sem))
    swap = Swap(g_ref, out_ref, swap_scratch)
    everyone.met()
    swap.start()
    everyone.begin(small_ref, True, slots, send, recv, own_sem)
    back.start()
    swap.hand_on()

    def join(got_ref, pieces, run):
        size = got_ref.shape[2] // len(pieces)
        for i, piece in enumerate(pieces):
            for to, device, start, count in run:
                part = got_ref[device, :, i * size + start : i * size + start + count]
                piece[:, to : to + count] = part.astype(jnp.float32)

    join(gu_ref, (gate_ref, up_ref), runs[0])
    back.arrived()
    join(got_qkv, (q_ref, k_ref, v_ref), runs[1])
    everyone.finish(small_ref, True, slots, send, recv)
    small_out[...] = jnp.sum(slots[...], axis=0)
    back.close()
    swap.close()


def finish(small, grad, sum_qkv, got_gu, runs, columns, collective_id):
    sizes = tuple(lax.axis_size(a) for a in ("fsdp", "z", "core"))
    fs, zs, cs = sizes
    n = math.prod(sizes)
    devices = fs * cs
    dma = pltpu.SemaphoreType.DMA
    sum_qkv = sum_qkv.reshape(devices, -1, sum_qkv.shape[2])
    wide = [jax.ShapeDtypeStruct((sum_qkv.shape[1], k), jnp.float32) for k in columns]
    return pl.pallas_call(
        functools.partial(finish_kernel, sizes, runs),
        out_shape=[
            jax.ShapeDtypeStruct((8, 128), small.dtype),
            jax.ShapeDtypeStruct(grad.shape, grad.dtype),
        ]
        + wide,
        in_specs=[vmem()] * 4,
        out_specs=[vmem(), anywhere()] + [vmem()] * len(wide),
        scratch_shapes=[
            pltpu.VMEM((n, 8, 128), small.dtype),
            pltpu.VMEM(sum_qkv.shape, jnp.bfloat16),
            dma((n,)), dma((n,)), dma,
        ]
        + Back.scratch(devices)
        + Swap.scratch(fs, *grad.shape),
        compiler_params=plane_params(collective_id),
        cost_estimate=estimate(45),
        name="finish",
    )(small, grad, sum_qkv, got_gu)


def to_tiles(x):
    return jnp.pad(x, ((0, 0), (0, 1024 - x.shape[1]))).reshape(-1, 8, 128)

from jax.sharding import Mesh
from jax.sharding import PartitionSpec as P

H = 32
EPSILON = 1e-06
HIGHEST = lax.Precision.HIGHEST
BF = jnp.bfloat16
F32 = jnp.float32
TP = ("fsdp", "core")
ALL = ("fsdp", "z", "core")


def rms_scale(values):
    return lax.rsqrt(jnp.mean(values * values, axis=1, keepdims=True) + EPSILON)


def norm_back(grad_normed, values, row_scale, gain_row):
    weighted = grad_normed * gain_row
    inner_mean = jnp.mean(weighted * values, axis=1, keepdims=True)
    return row_scale * (weighted - values * row_scale * row_scale * inner_mean)


class Layout:
    def __init__(self, per_device, head_dim):
        self.f, self.z, self.c = (lax.axis_size(a) for a in ALL)
        self.natural = per_device % head_dim == 0
        self.per_device = per_device

    def split(self, w):
        rows, cols = w.shape
        if self.natural:
            w = w.reshape(rows, self.f, self.z, self.c, self.per_device)
            w = w.transpose(1, 3, 0, 2, 4)
        else:
            w = w.reshape(rows, self.f, self.c, -1).transpose(1, 2, 0, 3)
        return w.reshape(self.f * self.c, rows, -1)

    def join(self, w):
        devices, rows, cols = w.shape
        if self.natural:
            w = w.reshape(self.f, self.c, rows, self.z, self.per_device)
            w = w.transpose(2, 0, 3, 1, 4)
        else:
            w = w.reshape(self.f, self.c, rows, cols).transpose(2, 0, 1, 3)
        return w.reshape(rows, -1)

    def gather(self, w):
        if self.natural:
            return lax.all_gather(w, "z", axis=0, tiled=True)
        both = lax.all_gather(w, ("z", "core"), axis=0, tiled=True)
        size = both.shape[0] // self.c
        return lax.dynamic_slice_in_dim(both, lax.axis_index("core") * size, size, 0)

    def whole(self, g):
        if self.natural:
            return g
        size = g.shape[0]
        both = jnp.zeros((size * self.c, g.shape[1]), g.dtype)
        both = lax.dynamic_update_slice_in_dim(both, g, lax.axis_index("core") * size, 0)
        both = lax.psum(both, "core").reshape(self.z, self.c, -1, g.shape[1])
        mine = lax.dynamic_index_in_dim(both, lax.axis_index("core"), 1, keepdims=False)
        return mine.reshape(-1, g.shape[1])

    def scatter(self, g):
        return lax.psum_scatter(g, "z", scatter_dimension=0, tiled=True)


def over_z(got):
    f, cr, cols = got.shape
    full = lax.all_gather(got, "z", axis=1, tiled=True)
    return full.reshape(-1, cols)


def reduce_z(grad):
    f, z = lax.axis_size("fsdp"), lax.axis_size("z")
    return lax.psum_scatter(
        grad.reshape(f, grad.shape[0] // f, -1), "z", scatter_dimension=1, tiled=True
    )


def shards(
    tokens, cotangent, lengths, buckets, norm1_gain, rel_bias,
    w_query, w_key, w_value, w_attn_out, norm2_gain, w_gate, w_up, w_down,
):
    fs, zs, cs = (lax.axis_size(a) for a in ALL)
    seqs, block_len, width = tokens.shape
    rows = seqs * block_len
    length = block_len * fs * cs
    head_dim = w_query.shape[1] // H
    heads = H // (fs * cs)
    buckets_n = rel_bias.shape[0] * fs * zs * cs // H
    head_cols = Layout(w_attn_out.shape[0], head_dim)
    ff_cols = Layout(w_down.shape[0], w_down.shape[0])

    own_small = jnp.concatenate([norm1_gain, norm2_gain, rel_bias]).astype(BF).astype(F32)
    own_small = jnp.concatenate([own_small, lengths.astype(F32)])
    sizes = (fs, zs, cs)
    runs = (
        column_runs(sizes, ff_cols.per_device, w_gate.shape[1], True),
        column_runs(sizes, head_cols.per_device, w_query.shape[1], head_cols.natural),
    )
    small, w_qkv, got_gu, x_in, cot, own_o, own_d = start(
        to_tiles(own_small[None]), (w_query, w_key, w_value), (w_gate, w_up),
        tokens.reshape(rows, width), cotangent.reshape(rows, width), w_attn_out, w_down, runs, 9,
    )
    w_qkv = w_qkv.reshape(width, -1)
    w_o = head_cols.gather(own_o)
    w_gu = over_z(got_gu)
    w_d = ff_cols.gather(own_d)
    small = small.reshape(-1, 1024)[:, : own_small.shape[0]]
    lens = lax.dynamic_index_in_dim(
        small[:, -seqs:], lax.axis_index("z") * zs * cs, 0, keepdims=False
    ).astype(jnp.int32)
    g = norm1_gain.shape[0]
    gain_one = small[:, :g].reshape(1, -1).astype(F32)
    gain_two = small[:, g : 2 * g].reshape(1, -1).astype(F32)
    table = small[:, 2 * g : -seqs].reshape(1, -1).astype(F32).reshape(H, buckets_n)
    plane_index = lax.axis_index("fsdp") * cs + lax.axis_index("core")
    table = head_cols.split(jnp.repeat(table.T, head_dim, axis=1))[:, :, ::head_dim]
    table = lax.dynamic_index_in_dim(table, plane_index, 0, keepdims=False).T
    one_hot = (buckets[:, None] == jnp.arange(buckets_n, dtype=jnp.int32)[None, :]).astype(F32)
    one_hot = jnp.pad(one_hot, ((0, 1), (0, 0)))
    offset_bias = jnp.dot(table, one_hot.T, precision=HIGHEST)

    ff = w_d.shape[0]

    positions = plane_index * block_len + jnp.arange(block_len, dtype=jnp.int32)
    valid = (positions[None, :] < lens[:, None]).astype(F32).reshape(rows, 1)

    x = x_in.reshape(rows, width).astype(F32)
    scale_one = rms_scale(x)
    grad_rows = cot.reshape(rows, width).astype(F32) * valid

    normed, qkv = plane_gather_dot((x * scale_one * gain_one).astype(BF), w_qkv, NN, seqs, 2)
    attended, lse = attn_fwd(qkv, offset_bias, lens, heads, head_dim, seqs)
    attn_sum = plane_dot_scatter(attended, w_o, NN, seqs, 3)
    branch = grad_rows.astype(BF)
    branch, attn_sum = lax.optimization_barrier((branch, attn_sum))
    grad_branch, grad_hidden = plane_gather_dot(branch, w_d, NT, seqs, 1, dtype=F32)
    hidden_one = x + attn_sum
    scale_two = rms_scale(hidden_one)
    normed_two, hidden_ff, grad_gu, grad_w_down = plane_gather_ffn(
        (hidden_one * scale_two * gain_two).astype(BF), grad_hidden, grad_branch, w_gu, seqs, 4
    )
    sum_down = ff_cols.scatter(grad_w_down)
    if fs <= 4:
        ff_sum, grad_w_gu = plane_dot_scatter(
            hidden_ff, w_d, NN, seqs, 7, beside=(normed_two, grad_gu)
        )
    else:
        ff_sum = plane_dot_scatter(hidden_ff, w_d, NN, seqs, 7)
        grad_w_gu = jnp.einsum("rd,rf->df", normed_two, grad_gu, preferred_element_type=F32)
        grad_w_gu = grad_w_gu.astype(BF)
    result = ((hidden_one + ff_sum) * valid).astype(BF)
    grad_w_gu, sum_down, grad_gu = lax.optimization_barrier((grad_w_gu, sum_down, grad_gu))
    sum_gu = reduce_z(grad_w_gu)
    grad_normed_two = plane_dot_scatter(grad_gu, w_gu, NT, seqs, 5)
    gain_two_part = jnp.sum(grad_normed_two * hidden_one * scale_two, axis=0)
    grad_hidden_one = grad_rows + norm_back(grad_normed_two, hidden_one, scale_two, gain_two)
    grad_attn, grad_attended, grad_w_o = plane_gather_dot(
        grad_hidden_one.astype(BF), w_o, NT, seqs, 6, other=attended
    )
    dq, dk, dv, grad_offset, output, sum_o, got_gu = attn_bwd(
        qkv, grad_attended, lse, offset_bias, lens, heads, head_dim, seqs,
        swapped=result, column=head_cols.whole(grad_w_o), spread=sum_gu, collective_id=11,
    )
    output = output.reshape(seqs, block_len, width)
    dqkv = jnp.concatenate([dq, dk, dv], axis=1)
    grad_w_qkv = jnp.einsum("rd,rk->dk", normed, dqkv, preferred_element_type=F32)
    grad_w_qkv, dqkv = lax.optimization_barrier((grad_w_qkv.astype(BF), dqkv))
    grad_w_qkv, sum_gu = lax.optimization_barrier((grad_w_qkv, sum_gu))
    sum_qkv = reduce_z(grad_w_qkv)
    grad_normed = plane_dot_scatter(dqkv, w_qkv, NT, seqs, 8)
    gain_one_part = jnp.sum(grad_normed * x * scale_one, axis=0)
    grad_x = grad_hidden_one + norm_back(grad_normed, x, scale_one, gain_one)

    grad_table = jnp.dot(grad_offset, one_hot, precision=HIGHEST)
    bias_all = jnp.zeros((fs * cs, heads, buckets_n), F32)
    bias_all = lax.dynamic_update_index_in_dim(bias_all, grad_table, plane_index, 0)
    bias_all = jnp.repeat(bias_all.transpose(0, 2, 1), head_dim, axis=2)
    bias_all = head_cols.join(bias_all)[:, ::head_dim].T.reshape(fs * zs * cs, -1)
    small_grad = jnp.concatenate(
        [
            gain_one_part.reshape(fs * zs * cs, -1),
            gain_two_part.reshape(fs * zs * cs, -1),
            bias_all,
        ],
        axis=1,
    )
    columns = (w_gate.shape[1],) * 2 + (w_query.shape[1],) * 3
    small_sum, grad_tokens, grad_gate_w, grad_up_w, grad_q_w, grad_k_w, grad_v_w = finish(
        to_tiles(small_grad), grad_x.astype(BF), sum_qkv, got_gu, runs, columns, 10
    )
    grad_tokens = grad_tokens.reshape(seqs, block_len, width)
    small_grad = small_sum.reshape(-1)[: small_grad.shape[1]]
    return (
        output,
        grad_tokens,
        small_grad[:g],
        small_grad[2 * g :],
        grad_q_w,
        grad_k_w,
        grad_v_w,
        sum_o,
        small_grad[g : 2 * g],
        grad_gate_w,
        grad_up_w,
        sum_down.astype(F32),
    )


def solution(mesh):
    fs, ctx = mesh.shape["fsdp"], mesh.shape["ctx"]
    mesh3 = Mesh(mesh.devices.reshape(fs, ctx // 2, 2), ALL)
    act = P("fsdp", ("z", "core"), None)
    vec, mat = P(ALL), P(ALL, None)
    in_specs = (act, act, P("fsdp"), P(), vec, vec, mat, mat, mat, mat, vec, mat, mat, mat)
    out_specs = (act, act, vec, vec, mat, mat, mat, mat, vec, mat, mat, mat)
    return jax.shard_map(shards, mesh=mesh3, in_specs=in_specs, out_specs=out_specs, check_vma=False)
```

```python
import functools, math
import jax, jax.numpy as jnp
from jax import lax
from jax.experimental import pallas as pl
from jax.experimental.pallas import tpu as pltpu

MASKED = -1e30
EPSILON = 1e-06
NT = (((1,), (1,)), ((), ()))
NN = (((1,), (0,)), ((), ()))


def dotf(a, b, dims=NN):
    return lax.dot_general(a, b, dims, preferred_element_type=jnp.float32)


def head_mask(width, head_dim, h):
    lane = lax.broadcasted_iota(jnp.int32, (1, width), 1)
    return (lane // head_dim == h).astype(jnp.float32).astype(jnp.bfloat16)


def fill_skew(bias_ref, skew_ref, heads, block, length):
    for h in range(heads):
        rows = jnp.broadcast_to(bias_ref[h : h + 1, :], (block, 2 * length))
        rolled = pltpu.roll(rows, 2 * length - (block - 1), 1, stride=1, stride_axis=0)
        skew_ref[h] = rolled[:, : 2 * length - block]


def attn_fwd_kernel(
    heads, head_dim, block, length, seqs, fs, lens_ref, q_ref, k_ref, v_ref, bias_ref, x_ref,
    out_ref, lse_ref, full_ref, skew_ref, kt_ref, *sems
):
    seq, blk = pl.program_id(0), pl.program_id(1)
    blocks = length // block
    grid_step = seq * blocks + blk
    steps = seqs * blocks
    width = heads * head_dim
    plane = Plane(fs)
    actions = gather_actions(plane, x_ref, full_ref, sems[:4], sems[4])

    @pl.when(grid_step == 0)
    def _():
        plane.barrier()
        actions[0]()

    @pl.when(grid_step == steps // 2)
    def _():
        actions[1]()

    @pl.when(grid_step == 0)
    def _():
        fill_skew(bias_ref, skew_ref, heads, block, length)

    @pl.when(blk == 0)
    def _():
        kt_ref[...] = k_ref[...].T

    valid_len = lens_ref[seq]
    key_pos = lax.broadcasted_iota(jnp.int32, (1, length), 1)
    key_mask = jnp.where(key_pos < valid_len, 0.0, MASKED)
    start = pl.multiple_of(length - block - blk * block, block)
    lane = lax.broadcasted_iota(jnp.int32, (block, 128), 1)
    out = jnp.zeros((block, width), jnp.float32)
    lse_all = jnp.zeros((block, 128), jnp.float32)
    for h in range(heads):
        mask = head_mask(width, head_dim, h)
        scores = dotf(q_ref[...] * mask, kt_ref[...])
        scores = scores + skew_ref[h, :, pl.ds(start, length)] + key_mask
        peak = jnp.max(scores, axis=1, keepdims=True)
        probs = jnp.exp(scores - peak)
        mass = jnp.sum(probs, axis=1, keepdims=True)
        probs = (probs * (1.0 / mass)).astype(jnp.bfloat16)
        out = out + dotf(probs, v_ref[...] * mask)
        lse_all = jnp.where(lane == h, peak + jnp.log(mass), lse_all)
    out_ref[...] = out.astype(jnp.bfloat16)
    lse_ref[...] = lse_all

    @pl.when(grid_step == steps - 1)
    def _():
        for action in actions[2:]:
            action()


def attn_fwd(qkv, offset_bias, lens, heads, head_dim, seqs, gathered, collective_id, block=256):
    rows, width3 = qkv.shape
    width = width3 // 3
    length = rows // seqs
    block = min(block, length)
    blocks = length // block
    fs = lax.axis_size("fsdp")
    wide = gathered.shape[1]
    gathered = gathered.reshape(seqs, -1, wide)
    b = gathered.shape[1]
    attended, lse, full = pl.pallas_call(
        functools.partial(attn_fwd_kernel, heads, head_dim, block, length, seqs, fs),
        grid=(seqs, blocks),
        in_specs=[
            pl.BlockSpec(memory_space=pltpu.SMEM),
            pl.BlockSpec((block, width), lambda s, i: (s * blocks + i, 0)),
            pl.BlockSpec((length, width), lambda s, i: (s, 1)),
            pl.BlockSpec((length, width), lambda s, i: (s, 2)),
            pl.BlockSpec((heads, 2 * length), lambda s, i: (0, 0)),
            vmem(),
        ],
        out_specs=[
            pl.BlockSpec((block, width), lambda s, i: (s * blocks + i, 0)),
            pl.BlockSpec((block, 128), lambda s, i: (s * blocks + i, 0)),
            anywhere(),
        ],
        scratch_shapes=[
            pltpu.VMEM((heads, block, 2 * length - block), jnp.float32),
            pltpu.VMEM((width, length), jnp.bfloat16),
        ]
        + gather_sems(fs)
        + [pltpu.SemaphoreType.DMA],
        out_shape=[
            jax.ShapeDtypeStruct((rows, width), jnp.bfloat16),
            jax.ShapeDtypeStruct((rows, 128), jnp.float32),
            jax.ShapeDtypeStruct((seqs, 2 * fs, b, wide), gathered.dtype),
        ],
        compiler_params=pltpu.CompilerParams(
            dimension_semantics=("arbitrary", "arbitrary"), vmem_limit_bytes=56 * 1024 * 1024,
            collective_id=collective_id, has_side_effects=True,
        ),
        cost_estimate=estimate(26),
        name="attn_fwd",
    )(lens, qkv, qkv, qkv, offset_bias, gathered)
    return attended, lse, full.reshape(-1, wide)


def attn_bwd_kernel(
    heads, head_dim, block, length, seqs, fs, lens_ref, q_ref, k_ref, v_ref, g_ref, lse_ref,
    bias_ref, *refs,
):
    seq, blk = pl.program_id(0), pl.program_id(1)
    blocks = length // block
    last_seq, last_blk = seqs - 1, blocks - 1
    grid_step = seq * blocks + blk
    steps = seqs * blocks
    if fs:
        x_ref, wg_ref, gu_ref, dq_ref, dk_ref, dv_ref, dbias_ref = refs[:7]
        out_ref, sum_ref, got_ref = refs[7:10]
        refs = refs[10:]
        column = Column(wg_ref, sum_ref, refs[6:9])
        back = Back((fs, 1, 2), gu_ref, got_ref, refs[9:12])
        swap = Swap(x_ref, out_ref, refs[12:])

        def begin():
            plane_and_column_greet()
            swap.start()
            column.start()
            back.start()

        todo = {0: begin, steps // 2: swap.hand_on}
        for step, action in todo.items():
            pl.when(grid_step == step)(action)
    else:
        dq_ref, dk_ref, dv_ref, dbias_ref = refs[:4]
        refs = refs[4:]
    skew_ref, kt_ref, vt_ref, acc_ref, dkt_ref, dvt_ref = refs[:6]
    width = heads * head_dim

    @pl.when((seq == 0) & (blk == 0))
    def _():
        fill_skew(bias_ref, skew_ref, heads, block, length)
        acc_ref[...] = jnp.zeros_like(acc_ref)

    @pl.when(blk == 0)
    def _():
        kt_ref[...] = k_ref[...].T
        vt_ref[...] = v_ref[...].T
        dkt_ref[...] = jnp.zeros_like(dkt_ref)
        dvt_ref[...] = jnp.zeros_like(dvt_ref)

    valid_len = lens_ref[seq]
    key_pos = lax.broadcasted_iota(jnp.int32, (1, length), 1)
    key_mask = jnp.where(key_pos < valid_len, 0.0, MASKED)
    start = pl.multiple_of(length - block - blk * block, block)
    q_t = q_ref[...].T
    g_t = g_ref[...].T
    dq = jnp.zeros((block, width), jnp.float32)
    row = lax.broadcasted_iota(jnp.int32, (width, 1), 0)
    for h in range(heads):
        mask = head_mask(width, head_dim, h)
        rmask = (row // head_dim == h).astype(jnp.float32).astype(jnp.bfloat16)
        scores = dotf(q_ref[...] * mask, kt_ref[...])
        scores = scores + skew_ref[h, :, pl.ds(start, length)] + key_mask
        probs = jnp.exp(scores - lse_ref[:, h : h + 1])
        grad_probs = dotf(g_ref[...] * mask, vt_ref[...])
        delta = jnp.sum(probs * grad_probs, axis=1, keepdims=True)
        ds = (probs * (grad_probs - delta)).astype(jnp.bfloat16)
        dq = dq + dotf(ds, k_ref[...] * mask)
        acc_ref[h, :, pl.ds(start, length)] += ds.astype(jnp.float32)
        dkt_ref[...] += dotf(q_t * rmask, ds)
        dvt_ref[...] += dotf(g_t * rmask, probs.astype(jnp.bfloat16))
    dq_ref[...] = dq.astype(jnp.bfloat16)

    @pl.when(blk == last_blk)
    def _():
        dk_ref[...] = dkt_ref[...].astype(jnp.bfloat16).T
        dv_ref[...] = dvt_ref[...].astype(jnp.bfloat16).T

    @pl.when((seq == last_seq) & (blk == last_blk))
    def _():
        for h in range(heads):
            part = jnp.concatenate(
                [acc_ref[h], jnp.zeros((block, block), jnp.float32)], axis=1
            )
            n = block
            while n > 8:
                n //= 2
                part = pltpu.roll(part[:n], n, 1) + part[n:]
            total = jnp.zeros((1, 2 * length), jnp.float32)
            for i in range(n):
                total = total + (pltpu.roll(part, n - 1 - i, 1) if i < n - 1 else part)[i : i + 1]
            dbias_ref[h : h + 1, :] = total

    if fs:

        @pl.when(grid_step == steps - 1)
        def _():
            column.close()
            back.arrived()
            back.close()
            swap.close()


def attn_bwd(
    qkv, grad, lse, offset_bias, lens, heads, head_dim, seqs, block=256, swapped=None,
    column=None, spread=None, collective_id=None,
):
    rows, width3 = qkv.shape
    width = width3 // 3
    length = rows // seqs
    block = min(block, length)
    blocks = length // block
    in_specs = [
        pl.BlockSpec(memory_space=pltpu.SMEM),
        pl.BlockSpec((block, width), lambda s, i: (s * blocks + i, 0)),
        pl.BlockSpec((length, width), lambda s, i: (s, 1)),
        pl.BlockSpec((length, width), lambda s, i: (s, 2)),
        pl.BlockSpec((block, width), lambda s, i: (s * blocks + i, 0)),
        pl.BlockSpec((block, 128), lambda s, i: (s * blocks + i, 0)),
        pl.BlockSpec((heads, 2 * length), lambda s, i: (0, 0)),
    ]
    out_specs = [
        pl.BlockSpec((block, width), lambda s, i: (s * blocks + i, 0)),
        pl.BlockSpec((length, width), lambda s, i: (s, 0)),
        pl.BlockSpec((length, width), lambda s, i: (s, 0)),
        pl.BlockSpec((heads, 2 * length), lambda s, i: (0, 0)),
    ]
    out_shape = [
        jax.ShapeDtypeStruct((rows, width), jnp.bfloat16),
        jax.ShapeDtypeStruct((rows, width), jnp.bfloat16),
        jax.ShapeDtypeStruct((rows, width), jnp.bfloat16),
        jax.ShapeDtypeStruct((heads, 2 * length), jnp.float32),
    ]
    scratch = [
        pltpu.VMEM((heads, block, 2 * length - block), jnp.float32),
        pltpu.VMEM((width, length), jnp.bfloat16),
        pltpu.VMEM((width, length), jnp.bfloat16),
        pltpu.VMEM((heads, block, 2 * length - block), jnp.float32),
        pltpu.VMEM((width, length), jnp.float32),
        pltpu.VMEM((width, length), jnp.float32),
    ]
    args = [lens, qkv, qkv, qkv, grad, lse, offset_bias]
    fs = 0
    if swapped is not None:
        fs, zs = lax.axis_size("fsdp"), lax.axis_size("z")
        column = column.reshape(zs, -1, column.shape[1])
        spread = spread.reshape(2 * fs, -1, spread.shape[2])
        args += [swapped, column, spread]
        in_specs += [vmem()] * 3
        out_specs += [anywhere(), vmem(), anywhere()]
        out_shape += [
            jax.ShapeDtypeStruct(swapped.shape, swapped.dtype),
            jax.ShapeDtypeStruct(column.shape[1:], jnp.float32),
            jax.ShapeDtypeStruct(spread.shape, spread.dtype),
        ]
        scratch += Column.scratch(column) + Back.scratch(2 * fs)
        scratch += Swap.scratch(fs, *swapped.shape)
    return pl.pallas_call(
        functools.partial(attn_bwd_kernel, heads, head_dim, block, length, seqs, fs),
        grid=(seqs, blocks),
        in_specs=in_specs,
        out_specs=out_specs,
        out_shape=out_shape,
        scratch_shapes=scratch,
        compiler_params=pltpu.CompilerParams(
            dimension_semantics=("arbitrary", "arbitrary"), vmem_limit_bytes=62 * 1024 * 1024,
            collective_id=collective_id, has_side_effects=fs > 0,
        ),
        cost_estimate=estimate(50),
        name="attn_bwd",
    )(*args)

MESH_ID = pl.DeviceIdType.MESH
MIB = 1024 * 1024


def remote_copy(src, dst, send_sem, recv_sem, device):
    return pltpu.make_async_remote_copy(
        src_ref=src, dst_ref=dst, send_sem=send_sem, recv_sem=recv_sem, device_id=device,
        device_id_type=MESH_ID,
    )


def landed(ref, sem):
    pltpu.make_async_copy(ref, ref, sem).wait()


def wide_tile(width):
    return math.gcd(width // 2, 1024)


def estimate(us):
    return pl.CostEstimate(flops=int(us * 0.02 * 1.1e9), bytes_accessed=int(us * 1e5), transcendentals=0)


def flip(f, bits):
    k = 1
    while k <= bits:
        if bits & k:
            f = f + (1 - 2 * (lax.rem(lax.div(f, k), 2))) * k
        k *= 2
    return f


class Plane:
    def __init__(self, fs):
        self.fs = fs
        self.f, self.z, self.c = (lax.axis_index(a) for a in ("fsdp", "z", "core"))
        self.bits = [1 << i for i in range(fs.bit_length() - 1)]
        self.orders = [self.bits, self.bits[::-1]]
        self.steps = len(self.bits)

    def peer(self, bit):
        return (flip(self.f, bit), self.z, self.c)

    def mate(self):
        return (self.f, self.z, 1 - self.c)

    def slot(self, rel, other=False):
        c = 1 - self.c if other else self.c
        return flip(self.f, rel) * 2 + c

    def barrier(self, more=0):
        bar = pltpu.get_barrier_semaphore()
        for dev in [self.mate()] + [self.peer(b) for b in self.bits]:
            pl.semaphore_signal(bar, inc=1, device_id=dev, device_id_type=MESH_ID)
        pl.semaphore_wait(bar, 1 + self.steps + more)


def gather_sems(fs):
    steps = fs.bit_length() - 1
    return [
        pltpu.SemaphoreType.DMA((2, steps, fs)),
        pltpu.SemaphoreType.DMA((2, fs)),
        pltpu.SemaphoreType.DMA((2, fs)),
        pltpu.SemaphoreType.DMA((2, fs)),
    ]


def run_gather(plane, x_ref, buf_ref, sems, consume):
    send, recv, mate_send, mate_recv = sems
    started = []

    def remote(*args):
        copy = remote_copy(*args)
        copy.start()
        started.append(copy)
        return copy

    def source(p, rel):
        return x_ref.at[p] if rel == 0 else buf_ref.at[p, plane.slot(rel)]

    def to_mate(p, rel):
        remote(
            source(p, rel), buf_ref.at[p, plane.slot(rel)], mate_send.at[p, rel],
            mate_recv.at[p, rel], plane.mate(),
        )

    def to_peer(p, step, rel):
        bit = plane.orders[p][step]
        return remote(
            source(p, rel), buf_ref.at[p, plane.slot(rel)], send.at[p, step, rel],
            recv.at[p, rel ^ bit], plane.peer(bit),
        )

    def finish(pairs):
        for p, rel in pairs:
            landed(buf_ref.at[p, plane.slot(rel, True)], mate_recv.at[p, rel])
            if consume is not None:
                consume(p, flip(plane.f, rel) * 2)

    first = [to_peer(p, 0, 0) for p in range(2)]
    for p in range(2):
        to_mate(p, 0)
    if consume is not None:
        for p in range(2):
            buf_ref[p, plane.slot(0)] = x_ref[p]
    have = [[0], [0]]
    pending = [(0, 0), (1, 0)]
    for step in range(plane.steps):
        for i in range(len(have[0])):
            finish(pending)
            if i == 0 and step + 1 < plane.steps:
                for copy in first:
                    copy.wait_send()
                    started[:] = [other for other in started if other is not copy]
                first = [to_peer(p, step + 1, 0) for p in range(2)]
            pending = [(p, have[p][i] ^ plane.orders[p][step]) for p in range(2)]
            for p, rel in pending:
                landed(buf_ref.at[p, plane.slot(rel)], recv.at[p, rel])
                to_mate(p, rel)
                for later in range(step + 1, plane.steps):
                    to_peer(p, later, rel)
        for p in range(2):
            have[p] = have[p] + [rel ^ plane.orders[p][step] for rel in have[p]]
    finish(pending)
    for copy in started:
        copy.wait_send()


def gather_actions(plane, x_ref, out_ref, sems, own_sem):
    send, recv, mate_send, mate_recv = sems

    def source(p, rel):
        return x_ref.at[p] if rel == 0 else out_ref.at[p, plane.slot(rel)]

    def to_mate(p, rel):
        return remote_copy(
            source(p, rel), out_ref.at[p, plane.slot(rel)], mate_send.at[p, rel],
            mate_recv.at[p, rel], plane.mate(),
        )

    def to_peer(p, step, rel):
        bit = plane.orders[p][step]
        return remote_copy(
            source(p, rel), out_ref.at[p, plane.slot(rel)], send.at[p, step, rel],
            recv.at[p, rel ^ bit], plane.peer(bit),
        )

    def own():
        return pltpu.make_async_copy(x_ref, out_ref.at[:, plane.slot(0)], own_sem)

    held = [[[0]], [[0]]]
    for step in range(plane.steps):
        for p in range(2):
            bit = plane.orders[p][step]
            held[p].append(held[p][-1] + [rel ^ bit for rel in held[p][-1]])

    def begin():
        for p in range(2):
            to_peer(p, 0, 0).start()
        for p in range(2):
            to_mate(p, 0).start()
        own().start()

    def group(step, i):
        if i == 0 and step + 1 < plane.steps:
            for p in range(2):
                to_peer(p, step, 0).wait_send()
                to_peer(p, step + 1, 0).start()
        for p in range(2):
            rel = held[p][step][i] ^ plane.orders[p][step]
            landed(out_ref.at[p, plane.slot(rel)], recv.at[p, rel])
            to_mate(p, rel).start()
            for later in range(step + 1, plane.steps):
                to_peer(p, later, rel).start()

    def close():
        for p in range(2):
            for rel in range(plane.fs):
                landed(out_ref.at[p, plane.slot(rel, True)], mate_recv.at[p, rel])
                to_mate(p, rel).wait_send()
            for step in range(plane.steps):
                for rel in held[p][step]:
                    if rel or step + 1 == plane.steps:
                        to_peer(p, step, rel).wait_send()
        own().wait()

    groups = [
        functools.partial(group, step, i)
        for step in range(plane.steps) for i in range(2**step)
    ]
    return [begin] + groups + [close]


class Line:
    def __init__(self, x_ref, out_ref, scratch):
        self.x_ref, self.out_ref = x_ref, out_ref
        self.send, self.recv, self.own_sem = scratch
        self.f, self.z, self.c = (lax.axis_index(a) for a in ("fsdp", "z", "core"))
        self.zs = out_ref.shape[0]

    @staticmethod
    def scratch(zs):
        dma = pltpu.SemaphoreType.DMA
        return [dma((2, zs)), dma((2, zs)), dma]

    def greet(self):
        bar = pltpu.get_barrier_semaphore()
        for way in (1, -1):
            to = lax.rem(self.z + way + self.zs, self.zs)
            pl.semaphore_signal(
                bar, inc=1, device_id=(self.f, to, self.c), device_id_type=MESH_ID
            )

    def copy(self, step, way):
        source = lax.rem(self.z - way * step + self.zs, self.zs)
        to = lax.rem(self.z + way + self.zs, self.zs)
        k = 0 if way > 0 else 1
        ref = self.out_ref.at[source]
        return remote_copy(
            ref if step else self.x_ref, ref, self.send.at[k, step], self.recv.at[k, step],
            (self.f, to, self.c),
        )

    def sends(self, step, way):
        if way > 0:
            return (self.z >= step) & (self.z < self.zs - 1)
        return (self.z < self.zs - step) & (self.z > 0)

    def arrived(self, step, way):
        k = 0 if way > 0 else 1
        source = lax.rem(self.z - way * (step + 1) + self.zs, self.zs)
        here = (self.z > step) if way > 0 else (self.z < self.zs - 1 - step)

        @pl.when(here)
        def _():
            landed(self.out_ref.at[source], self.recv.at[k, step])

    def own(self):
        return pltpu.make_async_copy(self.x_ref, self.out_ref.at[self.z], self.own_sem)

    def go(self, step):
        if step == 0:
            self.own().start()
        for way in (1, -1):
            if step:
                self.arrived(step - 1, way)
            if step < self.zs - 1:

                @pl.when(self.sends(step, way))
                def _(way=way):
                    self.copy(step, way).start()

    def close(self):
        self.own().wait()
        for step in range(self.zs - 1):
            for way in (1, -1):

                @pl.when(self.sends(step, way))
                def _(step=step, way=way):
                    self.copy(step, way).wait_send()


def scatter_scratch(fs, b, width):
    return [
        pltpu.VMEM((2, fs, b, width), jnp.bfloat16),
        pltpu.VMEM((2, fs, b, width), jnp.bfloat16),
        pltpu.VMEM((2, fs // 2, b, width), jnp.float32),
        pltpu.VMEM((2, fs, b, width), jnp.bfloat16),
        pltpu.VMEM((2, fs - 1, b, width), jnp.bfloat16),
        pltpu.SemaphoreType.DMA((fs, 2)),
        pltpu.SemaphoreType.DMA((fs, 2)),
        pltpu.SemaphoreType.DMA((2, fs)),
        pltpu.SemaphoreType.DMA((2, fs - 1)),
    ]


def scatter_actions(plane, partial, width, out_ref, scratch):
    give, got, total, outbox, inbox, give_sem, got_sem, send, recv = scratch
    b = out_ref.shape[1]
    rels = sorted(range(plane.fs), key=lambda r: (-bin(r).count("1"), r))
    whole = slice(0, width)

    def pieces(rel):
        if rel == rels[0]:
            return [slice(0, width // 2), slice(width // 2, width)]
        return [whole]

    def leaves(p, rel):
        for step, bit in enumerate(plane.orders[p]):
            if rel & bit:
                return step
        return plane.steps

    def place(p, step, rel):
        kept = [r for r in range(plane.fs) if leaves(p, r) > step]
        return plane.fs - 2 * len(kept) + kept.index(rel)

    def held(p, rel):
        return [r for r in range(plane.fs) if leaves(p, r) > 0].index(rel)

    def to_peer(p, rel):
        step = leaves(p, rel)
        bit = plane.orders[p][step]
        at = place(p, step, rel ^ bit)
        return remote_copy(
            outbox.at[p, rel], inbox.at[p, at], send.at[p, rel], recv.at[p, at], plane.peer(bit)
        )

    def to_mate(rel, i):
        cols = pieces(rel)[i]
        return remote_copy(
            give.at[:, rel, :, cols], got.at[:, rel, :, cols], give_sem.at[rel, i],
            got_sem.at[rel, i], plane.mate(),
        )

    def give_part(rel):
        theirs = plane.slot(rel, True)

        def body(cols):
            part = partial(theirs, cols).astype(jnp.bfloat16)
            give[0, rel, :, cols] = part[:b]
            give[1, rel, :, cols] = part[b:]

        for i, cols in enumerate(pieces(rel)):
            body(cols)
            to_mate(rel, i).start()

    def own_part(rel):
        mine = plane.slot(rel)

        def body(cols):
            part = partial(mine, cols)
            for p in range(2):
                here = part[p * b : (p + 1) * b] + got[p, rel, :, cols].astype(jnp.float32)
                if leaves(p, rel) == 0:
                    outbox[p, rel, :, cols] = here.astype(jnp.bfloat16)
                else:
                    total[p, held(p, rel), :, cols] = here

        for i, cols in enumerate(pieces(rel)):
            landed(got.at[:, rel, :, cols], got_sem.at[rel, i])
            body(cols)
        for p in range(2):
            if leaves(p, rel) == 0:
                to_peer(p, rel).start()

    def add_part(step, rel, p):
        at = place(p, step, rel)
        landed(inbox.at[p, at], recv.at[p, at])
        sends = leaves(p, rel) == step + 1

        def body(cols):
            here = total[p, held(p, rel), :, cols] + inbox[p, at, :, cols].astype(jnp.float32)
            if step + 1 == plane.steps:
                out_ref[p, :, cols] = here
            elif sends:
                outbox[p, rel, :, cols] = here.astype(jnp.bfloat16)
            else:
                total[p, held(p, rel), :, cols] = here

        body(whole)
        if sends and step + 1 < plane.steps:
            to_peer(p, rel).start()

    def close():
        for rel in rels:
            for i in range(len(pieces(rel))):
                to_mate(rel, i).wait_send()
            for p in range(2):
                if leaves(p, rel) < plane.steps:
                    to_peer(p, rel).wait_send()

    order = [(give_part, rels[0]), (own_part, rels[0]), (give_part, rels[1])]
    for i in range(2, len(rels)):
        order += [(give_part, rels[i]), (own_part, rels[i - 1])]
    order.append((own_part, rels[-1]))
    actions = [functools.partial(part, rel) for part, rel in order]
    for step in range(plane.steps):
        for rel in rels:
            for p in range(2):
                if leaves(p, rel) > step:
                    actions.append(functools.partial(add_part, step, rel, p))
    return actions + [close]


def vmem():
    return pl.BlockSpec(memory_space=pltpu.VMEM)


def anywhere():
    return pl.BlockSpec(memory_space=pl.ANY)


def plane_params(collective_id, limit=58):
    return pltpu.CompilerParams(
        collective_id=collective_id, has_side_effects=True, vmem_limit_bytes=limit * MIB
    )


class Staged:
    def __init__(self, refs, scratch):
        self.held = scratch[: len(refs)]
        self.loads = [
            pltpu.make_async_copy(ref, held, sem)
            for ref, held, sem in zip(refs, self.held, scratch[len(refs) :])
        ]
        for load in self.loads:
            load.start()

    @staticmethod
    def scratch(*arrays):
        dma = pltpu.SemaphoreType.DMA
        return [pltpu.VMEM(x.shape, x.dtype) for x in arrays] + [dma] * len(arrays)

    def wait(self):
        for load in self.loads:
            load.wait()


def gather_dot_kernel(fs, dims, tile, other, line, x_ref, *refs):
    count = 2 if other else 1
    hbm, refs = refs[:count], refs[count:]
    if line:
        l_ref, refs = refs[0], refs[1:]
    full_ref, y_ref, refs = refs[0], refs[1], refs[2:]
    if line:
        line, refs = Line(l_ref, refs[0], refs[1:4]), refs[4:]
    staged = Staged(hbm, refs[: 2 * count])
    buf_ref, sems = refs[2 * count], refs[2 * count + 1 :]
    plane = Plane(fs)
    if line:
        line.greet()
    plane.barrier(2 if line else 0)
    if line:
        line.go(0)
    w_ref = staged.held[0]
    a_ref = staged.held[1] if other else buf_ref
    keep_sem = sems[4]
    b, width = buf_ref.shape[2:]
    columns = y_ref.shape[3]
    kept = []

    def consume(p, slot):
        two = pl.ds(slot, 2)
        cp = pltpu.make_async_copy(
            buf_ref.at[p, two], full_ref.at[p, two], keep_sem.at[len(kept)]
        )
        cp.start()
        if not kept:
            staged.wait()
        kept.append(cp)

        def product(cols):
            w = w_ref[:, cols] if dims == NN else w_ref[cols, :]
            y = dotf(a_ref[p, two].reshape(2 * b, -1), w, dims)
            y_ref[p, two, :, cols] = y.astype(y_ref.dtype).reshape(2, b, tile)

        def one(j, carry):
            product(pl.ds(pl.multiple_of(j * tile, tile), tile))
            return carry

        if tile == columns:
            product(slice(None))
        else:
            lax.fori_loop(0, columns // tile, one, 0)
        if line and len(kept) % 2 == 0 and len(kept) // 2 < line.zs:
            line.go(len(kept) // 2)

    run_gather(plane, x_ref, buf_ref, sems[:4], consume)
    if line:
        for step in range(len(kept) // 2 + 1, line.zs):
            line.go(step)
        line.close()
    for cp in kept:
        cp.wait()


def plane_gather_dot(
    x, w, dims, seqs, collective_id, other=None, line=None, dtype=jnp.bfloat16
):
    fs, zs = lax.axis_size("fsdp"), lax.axis_size("z")
    x = x.reshape(seqs, -1, x.shape[1])
    _, b, width = x.shape
    columns = w.shape[1] if dims == NN else w.shape[0]
    tile = next((t for t in (1024, 768, 256, 128) if columns % t == 0), columns)
    lead = (seqs, 2 * fs, b)
    staged = [w] if other is None else [w, other.reshape(lead + (-1,))]
    out_shape = [
        jax.ShapeDtypeStruct(lead + (width,), x.dtype),
        jax.ShapeDtypeStruct(lead + (columns,), dtype),
    ]
    args, scratch = [x] + staged, []
    in_specs, out_specs = [vmem()] + [anywhere()] * len(staged), [anywhere(), vmem()]
    if line is not None:
        args.append(line)
        in_specs.append(vmem())
        out_shape.append(jax.ShapeDtypeStruct((zs,) + line.shape, line.dtype))
        out_specs.append(anywhere())
        scratch += Line.scratch(zs)
    out = pl.pallas_call(
        functools.partial(gather_dot_kernel, fs, dims, tile, other is not None, line is not None),
        out_shape=out_shape,
        in_specs=in_specs,
        out_specs=out_specs,
        scratch_shapes=scratch
        + Staged.scratch(*staged)
        + [pltpu.VMEM(lead + (width,), x.dtype)]
        + gather_sems(fs)
        + [pltpu.SemaphoreType.DMA((seqs * fs,))],
        compiler_params=plane_params(collective_id),
        cost_estimate=estimate(45),
        name="plane_gather_dot",
    )(*args)
    return (out[0].reshape(-1, width), out[1].reshape(-1, columns)) + tuple(out[2:])


class Swap:
    def __init__(self, x_ref, out_ref, scratch):
        self.x_ref, self.out_ref = x_ref, out_ref
        self.relay, self.own_sem, self.in_send, self.in_recv, self.on_send, self.on_recv = scratch
        self.f, self.z, self.c = (lax.axis_index(a) for a in ("fsdp", "z", "core"))
        self.fs, self.size = self.relay.shape[:2]

    @staticmethod
    def scratch(fs, rows, width):
        dma = pltpu.SemaphoreType.DMA
        return [
            pltpu.VMEM((fs, rows // fs, width), jnp.bfloat16), dma,
            dma((fs,)), dma((fs,)), dma((fs,)), dma((fs,)),
        ]

    def column(self, d):
        return lax.rem(self.f + d, self.fs)

    def part(self, ref, k):
        return ref.at[pl.ds(pl.multiple_of(k * self.size, self.size), self.size)]

    def straight(self):
        return remote_copy(
            self.part(self.x_ref, self.f), self.part(self.out_ref, self.f), self.in_send.at[0],
            self.on_recv.at[self.f], (self.z, self.f, self.c),
        )

    def inward(self, d):
        k = self.column(d)
        return remote_copy(
            self.part(self.x_ref, k), self.relay.at[d], self.in_send.at[d],
            self.in_recv.at[d], (k, self.z, self.c),
        )

    def onward(self, d):
        source = self.column(self.fs - d)
        return remote_copy(
            self.relay.at[d], self.part(self.out_ref, self.f), self.on_send.at[d],
            self.on_recv.at[self.f], (self.z, source, self.c),
        )

    def own(self):
        return pltpu.make_async_copy(self.x_ref, self.out_ref, self.own_sem)

    def start_inward(self):
        @pl.when(self.f != self.z)
        def _():
            for d in range(1, self.fs):
                self.inward(d).start()

    def start_straight(self):
        @pl.when(self.f != self.z)
        def _():
            self.straight().start()

        @pl.when(self.f == self.z)
        def _():
            self.own().start()

    def start(self):
        self.start_inward()
        self.start_straight()

    def relayed(self, body):
        for d in range(1, self.fs):

            @pl.when(self.column(self.fs - d) != self.z)
            def _(d=d):
                body(d)

    def hand_on(self):
        def one(d):
            landed(self.relay.at[d], self.in_recv.at[d])
            self.onward(d).start()

        self.relayed(one)

    def close(self):
        self.relayed(lambda d: self.onward(d).wait_send())

        @pl.when(self.f == self.z)
        def _():
            self.own().wait()

        @pl.when(self.f != self.z)
        def _():
            self.straight().wait_send()
            for d in range(1, self.fs):
                self.inward(d).wait_send()
            for k in range(self.fs):
                landed(self.part(self.out_ref, k), self.on_recv.at[k])


def plane_and_column_greet():
    fs, zs, cs = (lax.axis_size(a) for a in ("fsdp", "z", "core"))
    f, z, c = (lax.axis_index(a) for a in ("fsdp", "z", "core"))
    bar = pltpu.get_barrier_semaphore()
    places = [(lax.rem(f + df, fs), z, lax.rem(c + dc, cs)) for df in range(fs) for dc in range(cs)]
    places = places[1:] + [(f, lax.rem(z + dz, zs), c) for dz in range(1, zs)]
    places += [
        (lax.rem(f + df, fs), lax.rem(z + dz, zs), c) for df in range(1, fs) for dz in range(1, zs)
    ]
    for place in places:
        pl.semaphore_signal(bar, inc=1, device_id=place, device_id_type=MESH_ID)
    pl.semaphore_wait(bar, len(places))


class Column:
    def __init__(self, x_ref, sum_ref, scratch):
        self.x_ref, self.sum_ref = x_ref, sum_ref
        self.inbox, self.send, self.recv = scratch
        self.f, self.z, self.c = (lax.axis_index(a) for a in ("fsdp", "z", "core"))
        self.zs = x_ref.shape[0]

    @staticmethod
    def scratch(x):
        dma = pltpu.SemaphoreType.DMA
        return [pltpu.VMEM(x.shape, x.dtype), dma((x.shape[0],)), dma((x.shape[0],))]

    def copy(self, d):
        to = lax.rem(self.z + d, self.zs)
        return remote_copy(
            self.x_ref.at[to], self.inbox.at[d], self.send.at[d], self.recv.at[d],
            (self.f, to, self.c),
        )

    def start(self):
        for d in range(1, self.zs):
            self.copy(d).start()

    def close(self):
        for d in range(1, self.zs):
            self.copy(d).wait_send()
            landed(self.inbox.at[d], self.recv.at[d])
        total = self.x_ref[self.z].astype(jnp.float32)
        for d in range(1, self.zs):
            total = total + self.inbox[d].astype(jnp.float32)
        self.sum_ref[...] = total


class Back:
    def __init__(self, sizes, src_ref, got_ref, scratch):
        fs, zs, self.cs = sizes
        self.src_ref, self.got_ref = src_ref, got_ref
        self.send, self.recv, self.own_sem = scratch
        self.z = lax.axis_index("z")
        self.devices = fs * self.cs
        self.me = lax.axis_index("fsdp") * self.cs + lax.axis_index("core")

    @staticmethod
    def scratch(devices):
        dma = pltpu.SemaphoreType.DMA
        return [dma((devices,)), dma((devices,)), dma]

    def copy(self, d):
        to = lax.rem(self.me + d, self.devices)
        return remote_copy(
            self.src_ref.at[to], self.got_ref.at[self.me], self.send.at[d], self.recv.at[d],
            (lax.div(to, self.cs), self.z, lax.rem(to, self.cs)),
        )

    def own(self):
        return pltpu.make_async_copy(
            self.src_ref.at[self.me], self.got_ref.at[self.me], self.own_sem
        )

    def start(self):
        for d in range(1, self.devices):
            self.copy(d).start()
        self.own().start()

    def arrived(self):
        for d in range(1, self.devices):
            at = lax.rem(self.me + self.devices - d, self.devices)
            landed(self.got_ref.at[at], self.recv.at[d])
        self.own().wait()

    def close(self):
        for d in range(1, self.devices):
            self.copy(d).wait_send()


class Everyone:
    def __init__(self, sizes):
        self.fs, self.zs, self.cs = sizes
        self.n = math.prod(sizes)
        f, z, c = (lax.axis_index(a) for a in ("fsdp", "z", "core"))
        self.me = (f * self.zs + z) * self.cs + c

    def place(self, d):
        f, z, c = (lax.axis_index(a) for a in ("fsdp", "z", "core"))
        df, dz, dc = d // (self.zs * self.cs), d // self.cs % self.zs, d % self.cs
        return (lax.rem(f + df, self.fs), lax.rem(z + dz, self.zs), lax.rem(c + dc, self.cs))

    def index(self, place):
        return (place[0] * self.zs + place[1]) * self.cs + place[2]

    def back(self, d):
        f, z, c = (lax.axis_index(a) for a in ("fsdp", "z", "core"))
        df, dz, dc = d // (self.zs * self.cs), d // self.cs % self.zs, d % self.cs
        return self.index((
            lax.rem(f + self.fs - df, self.fs), lax.rem(z + self.zs - dz, self.zs),
            lax.rem(c + self.cs - dc, self.cs),
        ))

    def greet(self):
        bar = pltpu.get_barrier_semaphore()
        for d in range(1, self.n):
            pl.semaphore_signal(bar, inc=1, device_id=self.place(d), device_id_type=MESH_ID)

    def met(self):
        pl.semaphore_wait(pltpu.get_barrier_semaphore(), self.n - 1)

    def copy(self, d, x_ref, spread_out, slots, send, recv):
        to = self.place(d)
        src = x_ref.at[self.index(to)] if spread_out else x_ref.at[0]
        return remote_copy(src, slots.at[self.me], send.at[d], recv.at[d], to)

    def begin(self, x_ref, spread_out, slots, send, recv, own_sem):
        for d in range(1, self.n):
            self.copy(d, x_ref, spread_out, slots, send, recv).start()
        src = x_ref.at[self.me] if spread_out else x_ref.at[0]
        own = pltpu.make_async_copy(src, slots.at[self.me], own_sem)
        own.start()
        own.wait()

    def finish(self, x_ref, spread_out, slots, send, recv):
        for d in range(1, self.n):
            landed(slots.at[self.back(d)], recv.at[d])
        for d in range(1, self.n):
            self.copy(d, x_ref, spread_out, slots, send, recv).wait_send()


def slot_product(a_ref, w_ref, dims):
    def partial(slot, cols):
        a = a_ref[:, slot].reshape(-1, a_ref.shape[3])
        return dotf(a, w_ref[:, cols] if dims == NN else w_ref[cols, :], dims)

    return partial


def dot_scatter_kernel(fs, dims, beside, *refs):
    if beside:
        staged = Staged(refs[:2], refs[6:10])
        later = Staged(refs[2:4], refs[10:14])
        out_ref, g_ref, scratch = refs[4], refs[5], refs[14:]
        l_ref, r_ref = later.held
    else:
        staged = Staged(refs[:2], refs[3:7])
        out_ref, scratch = refs[2], refs[7:]
    plane = Plane(fs)
    plane.barrier()
    staged.wait()
    partial = slot_product(*staged.held, dims)
    actions = scatter_actions(plane, partial, out_ref.shape[2], out_ref, scratch)
    first = 2 * fs
    for action in actions[:first]:
        action()
    if beside:
        later.wait()
        block = 256

        def one(i, carry):
            here = pl.ds(pl.multiple_of(i * block, block), block)
            g_ref[here, :] = dotf(l_ref[:, here].T, r_ref[...]).astype(g_ref.dtype)
            return carry

        steps = l_ref.shape[1] // block
        lax.fori_loop(0, steps // 2, one, 0)
    middle = first + len(actions[first:-1]) - 2
    for action in actions[first:middle]:
        action()
    if beside:
        lax.fori_loop(steps // 2, steps, one, 0)
    for action in actions[middle:]:
        action()


def plane_dot_scatter(a, w, dims, seqs, collective_id, beside=None):
    fs = lax.axis_size("fsdp")
    a = a.reshape(seqs, 2 * fs, -1, a.shape[1])
    b = a.shape[2]
    width = w.shape[1] if dims == NN else w.shape[0]
    out_shape = [jax.ShapeDtypeStruct((seqs, b, width), jnp.float32)]
    args = [a, w]
    scratch = Staged.scratch(a, w)
    if beside is not None:
        l, r = beside
        args += [l, r]
        out_shape.append(jax.ShapeDtypeStruct((l.shape[1], r.shape[1]), jnp.bfloat16))
        scratch += Staged.scratch(l, r)
    out = pl.pallas_call(
        functools.partial(dot_scatter_kernel, fs, dims, beside is not None),
        out_shape=out_shape,
        in_specs=[anywhere()] * len(args),
        out_specs=[vmem()] * len(out_shape),
        scratch_shapes=scratch + scatter_scratch(fs, b, width),
        compiler_params=plane_params(collective_id, 62),
        cost_estimate=estimate(45),
        name="plane_dot_scatter",
    )(*args)
    rows = out[0].reshape(-1, width)
    return rows if beside is None else (rows, out[1])


def norm_turn_kernel(
    fs, a_hbm, w_hbm, hid_ref, cot_ref, gain_ref, wo_ref, o_ref, y_ref, wg_ref, grad_ref, gsum_ref,
    a_ref, w_ref, a_sem, w_sem, sum_ref, x_ref, buf_ref, acc_ref, *scratch
):
    staged = Staged((a_hbm, w_hbm), (a_ref, w_ref, a_sem, w_sem))
    plane = Plane(fs)
    plane.barrier()
    acc_ref[...] = jnp.zeros_like(acc_ref)
    staged.wait()
    b, width = x_ref.shape[1:]
    partial = slot_product(a_ref, w_ref, NT)
    for action in scatter_actions(plane, partial, width, sum_ref, scratch[4:]):
        action()
    block = 32
    tile = wide_tile(width)
    gain = gain_ref[...]

    def turn(i, total):
        p, at = lax.div(i, b // block), pl.multiple_of(lax.rem(i, b // block) * block, block)
        here = pl.ds(at, block)
        grad, hidden = sum_ref[p, here, :], hid_ref[p, here, :]
        scale = lax.rsqrt(jnp.mean(hidden * hidden, axis=1, keepdims=True) + EPSILON)
        weighted = grad * gain
        inner = jnp.mean(weighted * hidden, axis=1, keepdims=True)
        back = scale * (weighted - hidden * scale * scale * inner)
        back = cot_ref[p, here, :].astype(jnp.float32) + back
        grad_ref[p, here, :] = back
        x_ref[p, here, :] = back.astype(jnp.bfloat16)
        return total + grad * hidden * scale

    total = lax.fori_loop(
        0, 2 * (b // block), turn, jnp.zeros((block, width), jnp.float32)
    )
    gsum_ref[...] = jnp.sum(total, axis=0, keepdims=True)

    def consume(p, slot):
        two = pl.ds(slot, 2)
        rows = buf_ref[p, two].reshape(2 * b, width)
        y = dotf(rows, wo_ref[...], NT)
        y_ref[p, two] = y.astype(y_ref.dtype).reshape(2, b, -1)
        o_t = o_ref[p, two].reshape(2 * b, -1).T

        def grad(j, carry):
            cols = pl.ds(pl.multiple_of(j * tile, tile), tile)
            acc_ref[:, cols] += dotf(o_t, buf_ref[p, two, :, cols].reshape(2 * b, tile))
            return carry

        lax.fori_loop(0, width // tile, grad, 0)

    run_gather(plane, x_ref, buf_ref, scratch[:4], consume)
    wg_ref[...] = acc_ref[...].astype(wg_ref.dtype)


def norm_turn(a, w, hidden, cot, gain, w_o, attended, seqs, collective_id):
    fs = lax.axis_size("fsdp")
    lead = (seqs, 2 * fs, a.shape[0] // (2 * fs * seqs))
    b, width = lead[2], hidden.shape[1]
    own = (seqs, b, width)
    a = a.reshape(lead + (-1,))
    attended = attended.reshape(lead + (-1,))
    k = attended.shape[3]
    y, wg, grad, gsum = pl.pallas_call(
        functools.partial(norm_turn_kernel, fs),
        out_shape=[
            jax.ShapeDtypeStruct(lead + (k,), jnp.bfloat16),
            jax.ShapeDtypeStruct((k, width), jnp.bfloat16),
            jax.ShapeDtypeStruct(own, jnp.float32),
            jax.ShapeDtypeStruct((1, width), jnp.float32),
        ],
        in_specs=[anywhere()] * 2 + [vmem()] * 5,
        out_specs=[vmem()] * 4,
        scratch_shapes=Staged.scratch(a, w)
        + [
            pltpu.VMEM(own, jnp.float32),
            pltpu.VMEM(own, jnp.bfloat16),
            pltpu.VMEM(lead + (width,), jnp.bfloat16),
            pltpu.VMEM((k, width), jnp.float32),
        ]
        + gather_sems(fs)
        + scatter_scratch(fs, b, width),
        compiler_params=plane_params(collective_id, 62),
        cost_estimate=estimate(45),
        name="norm_turn",
    )(a, w, hidden.reshape(own), cot.reshape(own), gain, w_o, attended)
    return y.reshape(-1, k), wg, grad.reshape(-1, width), gsum[0]


GELU_C = math.sqrt(2.0 / math.pi)


def ffn_kernel(x_ref, gh_ref, g_ref, wgu_ref, h_ref, ggu_ref, wg_ref, acc_ref):
    step = pl.program_id(0)
    ff = h_ref.shape[1]

    @pl.when(step == 0)
    def _():
        acc_ref[...] = jnp.zeros_like(acc_ref)

    gate = dotf(x_ref[...], wgu_ref[:, :ff])
    up = dotf(x_ref[...], wgu_ref[:, ff:])
    grad_hidden = gh_ref[...]
    square = gate * gate
    tanh = jnp.tanh(GELU_C * gate * (1.0 + 0.044715 * square))
    half = 0.5 * (1.0 + tanh)
    act = gate * half
    slope = half + (0.5 * GELU_C) * gate * (1.0 - tanh * tanh) * (1.0 + 0.134145 * square)
    hidden = (act * up).astype(jnp.bfloat16)
    h_ref[...] = hidden
    ggu_ref[:, :ff] = (grad_hidden * up * slope).astype(jnp.bfloat16)
    ggu_ref[:, ff:] = (grad_hidden * act).astype(jnp.bfloat16)
    acc_ref[...] += dotf(hidden.T, g_ref[...])

    @pl.when(step == pl.num_programs(0) - 1)
    def _():
        wg_ref[...] = acc_ref[...].astype(jnp.bfloat16)


def ffn(x, grad_hidden, grad, w_gu):
    rows, width = x.shape
    ff = grad_hidden.shape[1]
    block = math.gcd(rows, 512)

    def blocks(columns):
        return pl.BlockSpec((block, columns), lambda i: (i, 0))

    def held(shape):
        return pl.BlockSpec(shape, lambda i: (0, 0), pipeline_mode=pl.Buffered(1))

    return pl.pallas_call(
        ffn_kernel,
        grid=(rows // block,),
        out_shape=[
            jax.ShapeDtypeStruct((rows, ff), jnp.bfloat16),
            jax.ShapeDtypeStruct((rows, 2 * ff), jnp.bfloat16),
            jax.ShapeDtypeStruct((ff, width), jnp.bfloat16),
        ],
        in_specs=[blocks(width), blocks(ff), blocks(width), held(w_gu.shape)],
        out_specs=[blocks(ff), blocks(2 * ff), pl.BlockSpec((ff, width), lambda i: (0, 0))],
        scratch_shapes=[pltpu.VMEM((ff, width), jnp.float32)],
        compiler_params=pltpu.CompilerParams(
            dimension_semantics=("arbitrary",), vmem_limit_bytes=60 * MIB
        ),
        cost_estimate=estimate(30),
        name="ffn",
    )(x, grad_hidden, grad, w_gu)

def column_runs(sizes, per_device, total, natural):
    fs, zs, cs = sizes
    if not natural:
        size = total // (fs * cs)
        return [(t * size, t, 0, size) for t in range(fs * cs)]
    return [
        (((f * zs + z) * cs + c) * per_device, f * cs + c, z * per_device, per_device)
        for f in range(fs) for z in range(zs) for c in range(cs)
    ]


def start_kernel(
    sizes, runs, small_ref, q_ref, k_ref, v_ref, gate_ref, up_ref, tok_ref, cot_ref, o_ref, d_ref,
    small_out, wqkv_ref, ggu_ref, x_ref, g_ref, o_out, d_out,
    slots, qkv_ref, gu_ref, s_send, s_recv, own_sem, q_send, q_recv, g_send, g_recv,
    line_send, line_recv, *swap_scratch,
):
    fs, zs, cs = sizes
    f, z, c = (lax.axis_index(a) for a in ("fsdp", "z", "core"))
    me = f * cs + c
    devices = fs * cs
    rows = qkv_ref.shape[1]
    everyone = Everyone(sizes)
    everyone.greet()

    def split(pieces_ref, parts, run):
        size = pieces_ref.shape[2] // len(parts)
        for i, part in enumerate(parts):
            for at, device, start, count in run:
                here = part[:, at : at + count].astype(jnp.bfloat16)
                pieces_ref[device, :, i * size + start : i * size + start + count] = here

    split(qkv_ref, (q_ref, k_ref, v_ref), runs[1])
    half = len(swap_scratch) // 2
    swaps = [
        Swap(tok_ref, x_ref, swap_scratch[:half]), Swap(cot_ref, g_ref, swap_scratch[half:])
    ]
    everyone.met()
    everyone.begin(small_ref, False, slots, s_send, s_recv, own_sem.at[0])

    def block(out_ref, index, lead):
        at = pl.ds(pl.multiple_of(lax.rem(index, cs) * rows, rows), rows)
        if lead is None:
            return out_ref.at[lax.div(index, cs), at]
        return out_ref.at[lax.div(index, cs), lead, at]

    def spread_copy(d, src_ref, out_ref, lead, send, recv):
        to = lax.rem(me + d, devices)
        return remote_copy(
            src_ref.at[to], block(out_ref, me, lead), send.at[d], recv.at[d],
            (lax.div(to, cs), z, lax.rem(to, cs)),
        )

    own_qkv = pltpu.make_async_copy(qkv_ref.at[me], block(wqkv_ref, me, z), own_sem.at[1])
    own_gu = pltpu.make_async_copy(gu_ref.at[me], block(ggu_ref, me, None), own_sem.at[2])
    own_qkv.start()
    for d in range(1, devices):
        spread_copy(d, qkv_ref, wqkv_ref, z, q_send, q_recv).start()
    swaps[0].start()
    split(gu_ref, (gate_ref, up_ref), runs[0])
    own_gu.start()
    o_out[...] = o_ref[...].astype(jnp.bfloat16)
    d_out[...] = d_ref[...].astype(jnp.bfloat16)
    def chip(p):
        return lax.rem(f + p, fs)

    def line(step, way, p):
        source = lax.rem(z - way * step + zs, zs)
        to = lax.rem(z + way + zs, zs)
        k = 0 if way > 0 else 1
        ref = wqkv_ref.at[chip(p), source]
        return remote_copy(
            ref, ref, line_send.at[k, step, p], line_recv.at[k, step, p], (f, to, c)
        )

    def sends(step, way):
        if way > 0:
            return (z >= step) & (z < zs - 1)
        return (z < zs - step) & (z > 0)

    def arrives(step, way):
        return (z > step) if way > 0 else (z < zs - 1 - step)

    def arrive(step, way, p):
        k = 0 if way > 0 else 1
        source = lax.rem(z - way * (step + 1) + zs, zs)
        landed(wqkv_ref.at[chip(p), source], line_recv.at[k, step, p])

    def spread_arrive(df, dc):
        index = chip(df) * cs + lax.rem(c + dc, cs)
        d = lax.rem(me - index + devices, devices)
        landed(block(wqkv_ref, index, z), q_recv.at[d])

    for step in range(zs - 1):
        for p in range(fs):
            if step == 0:
                if p == 0:
                    own_qkv.wait()
                for dc in range(cs):
                    if p or dc:
                        spread_arrive(p, dc)
            for way in (1, -1):
                if step:

                    @pl.when(arrives(step - 1, way))
                    def _(step=step, way=way, p=p):
                        arrive(step - 1, way, p)

                @pl.when(sends(step, way))
                def _(step=step, way=way, p=p):
                    line(step, way, p).start()

        if step == 0:
            swaps[0].hand_on()
            swaps[1].start()
            for d in range(1, devices):
                spread_copy(d, gu_ref, ggu_ref, None, g_send, g_recv).start()
        if step == 1:
            swaps[1].hand_on()
    for p in range(fs):
        for way in (1, -1):

            @pl.when(arrives(zs - 2, way))
            def _(way=way, p=p):
                arrive(zs - 2, way, p)

    everyone.finish(small_ref, False, slots, s_send, s_recv)
    small_out[...] = slots[...]
    own_gu.wait()
    for d in range(1, devices):
        landed(block(ggu_ref, lax.rem(me + devices - d, devices), None), g_recv.at[d])
    for d in range(1, devices):
        spread_copy(d, qkv_ref, wqkv_ref, z, q_send, q_recv).wait_send()
        spread_copy(d, gu_ref, ggu_ref, None, g_send, g_recv).wait_send()
    for step in range(zs - 1):
        for p in range(fs):
            for way in (1, -1):

                @pl.when(sends(step, way))
                def _(step=step, way=way, p=p):
                    line(step, way, p).wait_send()

    for swap in swaps:
        swap.close()


def start(small, qkv, gu, tokens, cotangent, own_o, own_d, runs, collective_id):
    sizes = tuple(lax.axis_size(a) for a in ("fsdp", "z", "core"))
    fs, zs, cs = sizes
    n = math.prod(sizes)
    devices = fs * cs
    rows = qkv[0].shape[0]
    qkv_cols = sum(w.shape[1] for w in qkv) // devices
    gu_cols = sum(w.shape[1] for w in gu) // devices
    dma = pltpu.SemaphoreType.DMA
    return pl.pallas_call(
        functools.partial(start_kernel, sizes, runs),
        out_shape=[
            jax.ShapeDtypeStruct((n, 8, 128), jnp.float32),
            jax.ShapeDtypeStruct((fs, zs, cs * rows, qkv_cols), jnp.bfloat16),
            jax.ShapeDtypeStruct((fs, cs * rows, gu_cols), jnp.bfloat16),
            jax.ShapeDtypeStruct(tokens.shape, tokens.dtype),
            jax.ShapeDtypeStruct(cotangent.shape, cotangent.dtype),
            jax.ShapeDtypeStruct(own_o.shape, jnp.bfloat16),
            jax.ShapeDtypeStruct(own_d.shape, jnp.bfloat16),
        ],
        in_specs=[vmem()] * 10,
        out_specs=[vmem()] + [anywhere()] * 4 + [vmem()] * 2,
        scratch_shapes=[
            pltpu.VMEM((n, 8, 128), jnp.float32),
            pltpu.VMEM((devices, rows, qkv_cols), jnp.bfloat16),
            pltpu.VMEM((devices, rows, gu_cols), jnp.bfloat16),
            dma((n,)), dma((n,)), dma((3,)),
            dma((devices,)), dma((devices,)), dma((devices,)), dma((devices,)),
            dma((2, zs, fs)), dma((2, zs, fs)),
        ]
        + Swap.scratch(fs, *tokens.shape) * 2,
        compiler_params=plane_params(collective_id),
        cost_estimate=estimate(120),
        name="start",
    )(small, *qkv, *gu, tokens, cotangent, own_o, own_d)


def finish_kernel(
    sizes, runs, small_ref, g_ref, qkv_ref, gu_ref, small_out, out_ref, gate_ref, up_ref,
    q_ref, k_ref, v_ref, slots, got_qkv, send, recv, own_sem, back_send, back_recv, back_sem,
    *swap_scratch
):
    everyone = Everyone(sizes)
    everyone.greet()
    back = Back(sizes, qkv_ref, got_qkv, (back_send, back_recv, back_sem))
    swap = Swap(g_ref, out_ref, swap_scratch)
    everyone.met()
    swap.start()
    everyone.begin(small_ref, True, slots, send, recv, own_sem)
    back.start()
    swap.hand_on()

    def join(got_ref, pieces, run):
        size = got_ref.shape[2] // len(pieces)
        for i, piece in enumerate(pieces):
            for to, device, start, count in run:
                part = got_ref[device, :, i * size + start : i * size + start + count]
                piece[:, to : to + count] = part.astype(jnp.float32)

    join(gu_ref, (gate_ref, up_ref), runs[0])
    back.arrived()
    join(got_qkv, (q_ref, k_ref, v_ref), runs[1])
    everyone.finish(small_ref, True, slots, send, recv)
    small_out[...] = jnp.sum(slots[...], axis=0)
    back.close()
    swap.close()


def finish(small, grad, sum_qkv, got_gu, runs, columns, collective_id):
    sizes = tuple(lax.axis_size(a) for a in ("fsdp", "z", "core"))
    fs, zs, cs = sizes
    n = math.prod(sizes)
    devices = fs * cs
    dma = pltpu.SemaphoreType.DMA
    sum_qkv = sum_qkv.reshape(devices, -1, sum_qkv.shape[2])
    wide = [jax.ShapeDtypeStruct((sum_qkv.shape[1], k), jnp.float32) for k in columns]
    return pl.pallas_call(
        functools.partial(finish_kernel, sizes, runs),
        out_shape=[
            jax.ShapeDtypeStruct((8, 128), small.dtype),
            jax.ShapeDtypeStruct(grad.shape, grad.dtype),
        ]
        + wide,
        in_specs=[vmem()] * 4,
        out_specs=[vmem(), anywhere()] + [vmem()] * len(wide),
        scratch_shapes=[
            pltpu.VMEM((n, 8, 128), small.dtype),
            pltpu.VMEM(sum_qkv.shape, jnp.bfloat16),
            dma((n,)), dma((n,)), dma,
        ]
        + Back.scratch(devices)
        + Swap.scratch(fs, *grad.shape),
        compiler_params=plane_params(collective_id),
        cost_estimate=estimate(45),
        name="finish",
    )(small, grad, sum_qkv, got_gu)


def to_tiles(x):
    return jnp.pad(x, ((0, 0), (0, 1024 - x.shape[1]))).reshape(-1, 8, 128)

from jax.sharding import Mesh
from jax.sharding import PartitionSpec as P

H = 32
HIGHEST = lax.Precision.HIGHEST
BF = jnp.bfloat16
F32 = jnp.float32
TP = ("fsdp", "core")
ALL = ("fsdp", "z", "core")


def rms_scale(values):
    return lax.rsqrt(jnp.mean(values * values, axis=1, keepdims=True) + EPSILON)


def norm_back(grad_normed, values, row_scale, gain_row):
    weighted = grad_normed * gain_row
    inner_mean = jnp.mean(weighted * values, axis=1, keepdims=True)
    return row_scale * (weighted - values * row_scale * row_scale * inner_mean)


class Layout:
    def __init__(self, per_device, head_dim):
        self.f, self.z, self.c = (lax.axis_size(a) for a in ALL)
        self.natural = per_device % head_dim == 0
        self.per_device = per_device

    def split(self, w):
        rows, cols = w.shape
        if self.natural:
            w = w.reshape(rows, self.f, self.z, self.c, self.per_device)
            w = w.transpose(1, 3, 0, 2, 4)
        else:
            w = w.reshape(rows, self.f, self.c, -1).transpose(1, 2, 0, 3)
        return w.reshape(self.f * self.c, rows, -1)

    def join(self, w):
        devices, rows, cols = w.shape
        if self.natural:
            w = w.reshape(self.f, self.c, rows, self.z, self.per_device)
            w = w.transpose(2, 0, 3, 1, 4)
        else:
            w = w.reshape(self.f, self.c, rows, cols).transpose(2, 0, 1, 3)
        return w.reshape(rows, -1)

    def gather(self, w):
        if self.natural:
            return lax.all_gather(w, "z", axis=0, tiled=True)
        both = lax.all_gather(w, ("z", "core"), axis=0, tiled=True)
        size = both.shape[0] // self.c
        return lax.dynamic_slice_in_dim(both, lax.axis_index("core") * size, size, 0)

    def whole(self, g):
        if self.natural:
            return g
        size = g.shape[0]
        both = jnp.zeros((size * self.c, g.shape[1]), g.dtype)
        both = lax.dynamic_update_slice_in_dim(both, g, lax.axis_index("core") * size, 0)
        both = lax.psum(both, "core").reshape(self.z, self.c, -1, g.shape[1])
        mine = lax.dynamic_index_in_dim(both, lax.axis_index("core"), 1, keepdims=False)
        return mine.reshape(-1, g.shape[1])

    def scatter(self, g):
        return lax.psum_scatter(g, "z", scatter_dimension=0, tiled=True)


def over_z(got):
    f, cr, cols = got.shape
    full = lax.all_gather(got, "z", axis=1, tiled=True)
    return full.reshape(-1, cols)


def reduce_z(grad):
    f, z = lax.axis_size("fsdp"), lax.axis_size("z")
    return lax.psum_scatter(
        grad.reshape(f, grad.shape[0] // f, -1), "z", scatter_dimension=1, tiled=True
    )


def shards(
    tokens, cotangent, lengths, buckets, norm1_gain, rel_bias,
    w_query, w_key, w_value, w_attn_out, norm2_gain, w_gate, w_up, w_down,
):
    fs, zs, cs = (lax.axis_size(a) for a in ALL)
    seqs, block_len, width = tokens.shape
    rows = seqs * block_len
    length = block_len * fs * cs
    head_dim = w_query.shape[1] // H
    heads = H // (fs * cs)
    buckets_n = rel_bias.shape[0] * fs * zs * cs // H
    head_cols = Layout(w_attn_out.shape[0], head_dim)
    ff_cols = Layout(w_down.shape[0], w_down.shape[0])

    own_small = jnp.concatenate([norm1_gain, norm2_gain, rel_bias]).astype(BF).astype(F32)
    own_small = jnp.concatenate([own_small, lengths.astype(F32)])
    sizes = (fs, zs, cs)
    runs = (
        column_runs(sizes, ff_cols.per_device, w_gate.shape[1], True),
        column_runs(sizes, head_cols.per_device, w_query.shape[1], head_cols.natural),
    )
    small, w_qkv, got_gu, x_in, cot, own_o, own_d = start(
        to_tiles(own_small[None]), (w_query, w_key, w_value), (w_gate, w_up),
        tokens.reshape(rows, width), cotangent.reshape(rows, width), w_attn_out, w_down, runs, 9,
    )
    w_qkv = w_qkv.reshape(width, -1)
    w_o = head_cols.gather(own_o)
    w_gu = over_z(got_gu)
    w_d = ff_cols.gather(own_d)
    small = small.reshape(-1, 1024)[:, : own_small.shape[0]]
    lens = lax.dynamic_index_in_dim(
        small[:, -seqs:], lax.axis_index("z") * zs * cs, 0, keepdims=False
    ).astype(jnp.int32)
    g = norm1_gain.shape[0]
    gain_one = small[:, :g].reshape(1, -1).astype(F32)
    gain_two = small[:, g : 2 * g].reshape(1, -1).astype(F32)
    table = small[:, 2 * g : -seqs].reshape(1, -1).astype(F32).reshape(H, buckets_n)
    plane_index = lax.axis_index("fsdp") * cs + lax.axis_index("core")
    table = head_cols.split(jnp.repeat(table.T, head_dim, axis=1))[:, :, ::head_dim]
    table = lax.dynamic_index_in_dim(table, plane_index, 0, keepdims=False).T
    one_hot = (buckets[:, None] == jnp.arange(buckets_n, dtype=jnp.int32)[None, :]).astype(F32)
    one_hot = jnp.pad(one_hot, ((0, 1), (0, 0)))
    offset_bias = jnp.dot(table, one_hot.T, precision=HIGHEST)

    ff = w_d.shape[0]

    positions = plane_index * block_len + jnp.arange(block_len, dtype=jnp.int32)
    valid = (positions[None, :] < lens[:, None]).astype(F32).reshape(rows, 1)

    x = x_in.reshape(rows, width).astype(F32)
    scale_one = rms_scale(x)
    grad_rows = cot.reshape(rows, width).astype(F32) * valid

    normed = (x * scale_one * gain_one).astype(BF)
    normed, qkv = plane_gather_dot(normed, w_qkv, NN, seqs, 2)
    branch = grad_rows.astype(BF)
    attended, lse, grad_branch = attn_fwd(
        qkv, offset_bias, lens, heads, head_dim, seqs, branch, 1
    )
    attn_sum = plane_dot_scatter(attended, w_o, NN, seqs, 3)
    hidden_one = x + attn_sum
    scale_two = rms_scale(hidden_one)
    normed_two, grad_hidden = plane_gather_dot(
        (hidden_one * scale_two * gain_two).astype(BF), w_d, NT, seqs, 4, other=grad_branch,
        dtype=F32,
    )
    hidden_ff, grad_gu, grad_w_down = ffn(normed_two, grad_hidden, grad_branch, w_gu)
    sum_down = ff_cols.scatter(grad_w_down)
    if fs <= 4:
        ff_sum, grad_w_gu = plane_dot_scatter(
            hidden_ff, w_d, NN, seqs, 7, beside=(normed_two, grad_gu)
        )
    else:
        ff_sum = plane_dot_scatter(hidden_ff, w_d, NN, seqs, 7)
        grad_w_gu = jnp.einsum("rd,rf->df", normed_two, grad_gu, preferred_element_type=F32)
        grad_w_gu = grad_w_gu.astype(BF)
    result = ((hidden_one + ff_sum) * valid).astype(BF)
    grad_w_gu, sum_down, grad_gu = lax.optimization_barrier((grad_w_gu, sum_down, grad_gu))
    sum_gu = reduce_z(grad_w_gu)
    if fs <= 4:
        grad_attended, grad_w_o, grad_hidden_one, gain_two_part = norm_turn(
            grad_gu, w_gu, hidden_one, branch, gain_two, w_o, attended, seqs, 5
        )
    else:
        grad_normed_two = plane_dot_scatter(grad_gu, w_gu, NT, seqs, 5)
        gain_two_part = jnp.sum(grad_normed_two * hidden_one * scale_two, axis=0)
        grad_hidden_one = grad_rows + norm_back(grad_normed_two, hidden_one, scale_two, gain_two)
        grad_attn, grad_attended = plane_gather_dot(
            grad_hidden_one.astype(BF), w_o, NT, seqs, 6
        )
        grad_w_o = jnp.einsum("rk,rd->kd", attended, grad_attn, preferred_element_type=F32)
        grad_w_o = grad_w_o.astype(BF)
    dq, dk, dv, grad_offset, output, sum_o, got_gu = attn_bwd(
        qkv, grad_attended, lse, offset_bias, lens, heads, head_dim, seqs,
        swapped=result, column=head_cols.whole(grad_w_o), spread=sum_gu, collective_id=11,
    )
    output = output.reshape(seqs, block_len, width)
    dqkv = jnp.concatenate([dq, dk, dv], axis=1)
    grad_w_qkv = jnp.einsum("rd,rk->dk", normed, dqkv, preferred_element_type=F32)
    grad_w_qkv, dqkv = lax.optimization_barrier((grad_w_qkv.astype(BF), dqkv))
    grad_w_qkv, sum_gu = lax.optimization_barrier((grad_w_qkv, sum_gu))
    sum_qkv = reduce_z(grad_w_qkv)
    grad_normed = plane_dot_scatter(dqkv, w_qkv, NT, seqs, 8)
    gain_one_part = jnp.sum(grad_normed * x * scale_one, axis=0)
    grad_x = grad_hidden_one + norm_back(grad_normed, x, scale_one, gain_one)

    grad_table = jnp.dot(grad_offset, one_hot, precision=HIGHEST)
    bias_all = jnp.zeros((fs * cs, heads, buckets_n), F32)
    bias_all = lax.dynamic_update_index_in_dim(bias_all, grad_table, plane_index, 0)
    bias_all = jnp.repeat(bias_all.transpose(0, 2, 1), head_dim, axis=2)
    bias_all = head_cols.join(bias_all)[:, ::head_dim].T.reshape(fs * zs * cs, -1)
    small_grad = jnp.concatenate(
        [
            gain_one_part.reshape(fs * zs * cs, -1),
            gain_two_part.reshape(fs * zs * cs, -1),
            bias_all,
        ],
        axis=1,
    )
    columns = (w_gate.shape[1],) * 2 + (w_query.shape[1],) * 3
    small_sum, grad_tokens, grad_gate_w, grad_up_w, grad_q_w, grad_k_w, grad_v_w = finish(
        to_tiles(small_grad), grad_x.astype(BF), sum_qkv, got_gu, runs, columns, 10
    )
    grad_tokens = grad_tokens.reshape(seqs, block_len, width)
    small_grad = small_sum.reshape(-1)[: small_grad.shape[1]]
    return (
        output,
        grad_tokens,
        small_grad[:g],
        small_grad[2 * g :],
        grad_q_w,
        grad_k_w,
        grad_v_w,
        sum_o,
        small_grad[g : 2 * g],
        grad_gate_w,
        grad_up_w,
        sum_down.astype(F32),
    )


def solution(mesh):
    fs, ctx = mesh.shape["fsdp"], mesh.shape["ctx"]
    mesh3 = Mesh(mesh.devices.reshape(fs, ctx // 2, 2), ALL)
    act = P("fsdp", ("z", "core"), None)
    vec, mat = P(ALL), P(ALL, None)
    in_specs = (act, act, P("fsdp"), P(), vec, vec, mat, mat, mat, mat, vec, mat, mat, mat)
    out_specs = (act, act, vec, vec, mat, mat, mat, mat, vec, mat, mat, mat)
    return jax.shard_map(shards, mesh=mesh3, in_specs=in_specs, out_specs=out_specs, check_vma=False)
```

```python
import functools, math
import jax, jax.numpy as jnp
from jax import lax
from jax.experimental import pallas as pl
from jax.experimental.pallas import tpu as pltpu

MASKED = -1e30
EPSILON = 1e-06
NT = (((1,), (1,)), ((), ()))
NN = (((1,), (0,)), ((), ()))


def dotf(a, b, dims=NN):
    return lax.dot_general(a, b, dims, preferred_element_type=jnp.float32)


def head_mask(width, head_dim, h):
    lane = lax.broadcasted_iota(jnp.int32, (1, width), 1)
    return (lane // head_dim == h).astype(jnp.float32).astype(jnp.bfloat16)


def fill_skew(bias_ref, skew_ref, heads, block, length):
    for h in range(heads):
        rows = jnp.broadcast_to(bias_ref[h : h + 1, :], (block, 2 * length))
        rolled = pltpu.roll(rows, 2 * length - (block - 1), 1, stride=1, stride_axis=0)
        skew_ref[h] = rolled[:, : 2 * length - block]


def attn_fwd_kernel(
    heads, head_dim, block, length, seqs, fs, lens_ref, q_ref, k_ref, v_ref, bias_ref, x_ref,
    out_ref, lse_ref, full_ref, skew_ref, kt_ref, *sems
):
    seq, blk = pl.program_id(0), pl.program_id(1)
    blocks = length // block
    grid_step = seq * blocks + blk
    steps = seqs * blocks
    width = heads * head_dim
    plane = Plane(fs)
    actions = gather_actions(plane, x_ref, full_ref, sems[:4], sems[4])

    @pl.when(grid_step == 0)
    def _():
        plane.barrier()
        actions[0]()

    @pl.when(grid_step == steps // 2)
    def _():
        actions[1]()

    @pl.when(grid_step == 0)
    def _():
        fill_skew(bias_ref, skew_ref, heads, block, length)

    @pl.when(blk == 0)
    def _():
        kt_ref[...] = k_ref[...].T

    valid_len = lens_ref[seq]
    key_pos = lax.broadcasted_iota(jnp.int32, (1, length), 1)
    key_mask = jnp.where(key_pos < valid_len, 0.0, MASKED)
    start = pl.multiple_of(length - block - blk * block, block)
    lane = lax.broadcasted_iota(jnp.int32, (block, 128), 1)
    out = jnp.zeros((block, width), jnp.float32)
    lse_all = jnp.zeros((block, 128), jnp.float32)
    for h in range(heads):
        mask = head_mask(width, head_dim, h)
        scores = dotf(q_ref[...] * mask, kt_ref[...])
        scores = scores + skew_ref[h, :, pl.ds(start, length)] + key_mask
        peak = jnp.max(scores, axis=1, keepdims=True)
        probs = jnp.exp(scores - peak)
        mass = jnp.sum(probs, axis=1, keepdims=True)
        probs = (probs * (1.0 / mass)).astype(jnp.bfloat16)
        out = out + dotf(probs, v_ref[...] * mask)
        lse_all = jnp.where(lane == h, peak + jnp.log(mass), lse_all)
    out_ref[...] = out.astype(jnp.bfloat16)
    lse_ref[...] = lse_all

    @pl.when(grid_step == steps - 1)
    def _():
        for action in actions[2:]:
            action()


def attn_fwd(qkv, offset_bias, lens, heads, head_dim, seqs, gathered, collective_id, block=256):
    rows, width3 = qkv.shape
    width = width3 // 3
    length = rows // seqs
    block = min(block, length)
    blocks = length // block
    fs = lax.axis_size("fsdp")
    wide = gathered.shape[1]
    gathered = gathered.reshape(seqs, -1, wide)
    b = gathered.shape[1]
    attended, lse, full = pl.pallas_call(
        functools.partial(attn_fwd_kernel, heads, head_dim, block, length, seqs, fs),
        grid=(seqs, blocks),
        in_specs=[
            pl.BlockSpec(memory_space=pltpu.SMEM),
            pl.BlockSpec((block, width), lambda s, i: (s * blocks + i, 0)),
            pl.BlockSpec((length, width), lambda s, i: (s, 1)),
            pl.BlockSpec((length, width), lambda s, i: (s, 2)),
            pl.BlockSpec((heads, 2 * length), lambda s, i: (0, 0)),
            vmem(),
        ],
        out_specs=[
            pl.BlockSpec((block, width), lambda s, i: (s * blocks + i, 0)),
            pl.BlockSpec((block, 128), lambda s, i: (s * blocks + i, 0)),
            anywhere(),
        ],
        scratch_shapes=[
            pltpu.VMEM((heads, block, 2 * length - block), jnp.float32),
            pltpu.VMEM((width, length), jnp.bfloat16),
        ]
        + gather_sems(fs)
        + [pltpu.SemaphoreType.DMA],
        out_shape=[
            jax.ShapeDtypeStruct((rows, width), jnp.bfloat16),
            jax.ShapeDtypeStruct((rows, 128), jnp.float32),
            jax.ShapeDtypeStruct((seqs, 2 * fs, b, wide), gathered.dtype),
        ],
        compiler_params=pltpu.CompilerParams(
            dimension_semantics=("arbitrary", "arbitrary"), vmem_limit_bytes=56 * 1024 * 1024,
            collective_id=collective_id, has_side_effects=True,
        ),
        cost_estimate=estimate(26),
        name="attn_fwd",
    )(lens, qkv, qkv, qkv, offset_bias, gathered)
    return attended, lse, full.reshape(-1, wide)


def attn_bwd_kernel(
    heads, head_dim, block, length, seqs, fs, lens_ref, q_ref, k_ref, v_ref, g_ref, lse_ref,
    bias_ref, *refs,
):
    seq, blk = pl.program_id(0), pl.program_id(1)
    blocks = length // block
    last_seq, last_blk = seqs - 1, blocks - 1
    grid_step = seq * blocks + blk
    steps = seqs * blocks
    if fs:
        x_ref, wg_ref, gu_ref, dq_ref, dk_ref, dv_ref, dbias_ref = refs[:7]
        out_ref, sum_ref, got_ref = refs[7:10]
        refs = refs[10:]
        column = Column(wg_ref, sum_ref, refs[6:9])
        back = Back((fs, 1, 2), gu_ref, got_ref, refs[9:12])
        swap = Swap(x_ref, out_ref, refs[12:])

        def begin():
            plane_and_column_greet()
            swap.start()
            column.start()
            back.start()

        todo = {0: begin, steps // 2: swap.hand_on}
        for step, action in todo.items():
            pl.when(grid_step == step)(action)
    else:
        dq_ref, dk_ref, dv_ref, dbias_ref = refs[:4]
        refs = refs[4:]
    skew_ref, kt_ref, vt_ref, acc_ref, dkt_ref, dvt_ref = refs[:6]
    width = heads * head_dim

    @pl.when((seq == 0) & (blk == 0))
    def _():
        fill_skew(bias_ref, skew_ref, heads, block, length)
        acc_ref[...] = jnp.zeros_like(acc_ref)

    @pl.when(blk == 0)
    def _():
        kt_ref[...] = k_ref[...].T
        vt_ref[...] = v_ref[...].T
        dkt_ref[...] = jnp.zeros_like(dkt_ref)
        dvt_ref[...] = jnp.zeros_like(dvt_ref)

    valid_len = lens_ref[seq]
    key_pos = lax.broadcasted_iota(jnp.int32, (1, length), 1)
    key_mask = jnp.where(key_pos < valid_len, 0.0, MASKED)
    start = pl.multiple_of(length - block - blk * block, block)
    q_t = q_ref[...].T
    g_t = g_ref[...].T
    dq = jnp.zeros((block, width), jnp.float32)
    row = lax.broadcasted_iota(jnp.int32, (width, 1), 0)
    for h in range(heads):
        mask = head_mask(width, head_dim, h)
        rmask = (row // head_dim == h).astype(jnp.float32).astype(jnp.bfloat16)
        scores = dotf(q_ref[...] * mask, kt_ref[...])
        scores = scores + skew_ref[h, :, pl.ds(start, length)] + key_mask
        probs = jnp.exp(scores - lse_ref[:, h : h + 1])
        grad_probs = dotf(g_ref[...] * mask, vt_ref[...])
        delta = jnp.sum(probs * grad_probs, axis=1, keepdims=True)
        ds = (probs * (grad_probs - delta)).astype(jnp.bfloat16)
        dq = dq + dotf(ds, k_ref[...] * mask)
        acc_ref[h, :, pl.ds(start, length)] += ds.astype(jnp.float32)
        dkt_ref[...] += dotf(q_t * rmask, ds)
        dvt_ref[...] += dotf(g_t * rmask, probs.astype(jnp.bfloat16))
    dq_ref[...] = dq.astype(jnp.bfloat16)

    @pl.when(blk == last_blk)
    def _():
        dk_ref[...] = dkt_ref[...].astype(jnp.bfloat16).T
        dv_ref[...] = dvt_ref[...].astype(jnp.bfloat16).T

    @pl.when((seq == last_seq) & (blk == last_blk))
    def _():
        for h in range(heads):
            part = jnp.concatenate(
                [acc_ref[h], jnp.zeros((block, block), jnp.float32)], axis=1
            )
            n = block
            while n > 8:
                n //= 2
                part = pltpu.roll(part[:n], n, 1) + part[n:]
            total = jnp.zeros((1, 2 * length), jnp.float32)
            for i in range(n):
                total = total + (pltpu.roll(part, n - 1 - i, 1) if i < n - 1 else part)[i : i + 1]
            dbias_ref[h : h + 1, :] = total

    if fs:

        @pl.when(grid_step == steps - 1)
        def _():
            column.close()
            back.arrived()
            back.close()
            swap.close()


def attn_bwd(
    qkv, grad, lse, offset_bias, lens, heads, head_dim, seqs, block=256, swapped=None,
    column=None, spread=None, collective_id=None,
):
    rows, width3 = qkv.shape
    width = width3 // 3
    length = rows // seqs
    block = min(block, length)
    blocks = length // block
    in_specs = [
        pl.BlockSpec(memory_space=pltpu.SMEM),
        pl.BlockSpec((block, width), lambda s, i: (s * blocks + i, 0)),
        pl.BlockSpec((length, width), lambda s, i: (s, 1)),
        pl.BlockSpec((length, width), lambda s, i: (s, 2)),
        pl.BlockSpec((block, width), lambda s, i: (s * blocks + i, 0)),
        pl.BlockSpec((block, 128), lambda s, i: (s * blocks + i, 0)),
        pl.BlockSpec((heads, 2 * length), lambda s, i: (0, 0)),
    ]
    out_specs = [
        pl.BlockSpec((block, width), lambda s, i: (s * blocks + i, 0)),
        pl.BlockSpec((length, width), lambda s, i: (s, 0)),
        pl.BlockSpec((length, width), lambda s, i: (s, 0)),
        pl.BlockSpec((heads, 2 * length), lambda s, i: (0, 0)),
    ]
    out_shape = [
        jax.ShapeDtypeStruct((rows, width), jnp.bfloat16),
        jax.ShapeDtypeStruct((rows, width), jnp.bfloat16),
        jax.ShapeDtypeStruct((rows, width), jnp.bfloat16),
        jax.ShapeDtypeStruct((heads, 2 * length), jnp.float32),
    ]
    scratch = [
        pltpu.VMEM((heads, block, 2 * length - block), jnp.float32),
        pltpu.VMEM((width, length), jnp.bfloat16),
        pltpu.VMEM((width, length), jnp.bfloat16),
        pltpu.VMEM((heads, block, 2 * length - block), jnp.float32),
        pltpu.VMEM((width, length), jnp.float32),
        pltpu.VMEM((width, length), jnp.float32),
    ]
    args = [lens, qkv, qkv, qkv, grad, lse, offset_bias]
    fs = 0
    if swapped is not None:
        fs, zs = lax.axis_size("fsdp"), lax.axis_size("z")
        column = column.reshape(zs, -1, column.shape[1])
        spread = spread.reshape(2 * fs, -1, spread.shape[2])
        args += [swapped, column, spread]
        in_specs += [vmem()] * 3
        out_specs += [anywhere(), vmem(), anywhere()]
        out_shape += [
            jax.ShapeDtypeStruct(swapped.shape, swapped.dtype),
            jax.ShapeDtypeStruct(column.shape[1:], jnp.float32),
            jax.ShapeDtypeStruct(spread.shape, spread.dtype),
        ]
        scratch += Column.scratch(column) + Back.scratch(2 * fs)
        scratch += Swap.scratch(fs, *swapped.shape)
    return pl.pallas_call(
        functools.partial(attn_bwd_kernel, heads, head_dim, block, length, seqs, fs),
        grid=(seqs, blocks),
        in_specs=in_specs,
        out_specs=out_specs,
        out_shape=out_shape,
        scratch_shapes=scratch,
        compiler_params=pltpu.CompilerParams(
            dimension_semantics=("arbitrary", "arbitrary"), vmem_limit_bytes=62 * 1024 * 1024,
            collective_id=collective_id, has_side_effects=fs > 0,
        ),
        cost_estimate=estimate(50),
        name="attn_bwd",
    )(*args)

MESH_ID = pl.DeviceIdType.MESH
MIB = 1024 * 1024


def remote_copy(src, dst, send_sem, recv_sem, device):
    return pltpu.make_async_remote_copy(
        src_ref=src, dst_ref=dst, send_sem=send_sem, recv_sem=recv_sem, device_id=device,
        device_id_type=MESH_ID,
    )


def landed(ref, sem):
    pltpu.make_async_copy(ref, ref, sem).wait()


def wide_tile(width):
    return math.gcd(width // 2, 1024)


def estimate(us):
    return pl.CostEstimate(flops=int(us * 0.02 * 1.1e9), bytes_accessed=int(us * 1e5), transcendentals=0)


def flip(f, bits):
    k = 1
    while k <= bits:
        if bits & k:
            f = f + (1 - 2 * (lax.rem(lax.div(f, k), 2))) * k
        k *= 2
    return f


class Plane:
    def __init__(self, fs):
        self.fs = fs
        self.f, self.z, self.c = (lax.axis_index(a) for a in ("fsdp", "z", "core"))
        self.bits = [1 << i for i in range(fs.bit_length() - 1)]
        self.orders = [self.bits, self.bits[::-1]]
        self.steps = len(self.bits)

    def peer(self, bit):
        return (flip(self.f, bit), self.z, self.c)

    def mate(self):
        return (self.f, self.z, 1 - self.c)

    def slot(self, rel, other=False):
        c = 1 - self.c if other else self.c
        return flip(self.f, rel) * 2 + c

    def barrier(self, more=0):
        bar = pltpu.get_barrier_semaphore()
        for dev in [self.mate()] + [self.peer(b) for b in self.bits]:
            pl.semaphore_signal(bar, inc=1, device_id=dev, device_id_type=MESH_ID)
        pl.semaphore_wait(bar, 1 + self.steps + more)


def gather_sems(fs):
    steps = fs.bit_length() - 1
    return [
        pltpu.SemaphoreType.DMA((2, steps, fs)),
        pltpu.SemaphoreType.DMA((2, fs)),
        pltpu.SemaphoreType.DMA((2, fs)),
        pltpu.SemaphoreType.DMA((2, fs)),
    ]


def run_gather(plane, x_ref, buf_ref, sems, consume):
    send, recv, mate_send, mate_recv = sems
    started = []

    def remote(*args):
        copy = remote_copy(*args)
        copy.start()
        started.append(copy)
        return copy

    def source(p, rel):
        return x_ref.at[p] if rel == 0 else buf_ref.at[p, plane.slot(rel)]

    def to_mate(p, rel):
        remote(
            source(p, rel), buf_ref.at[p, plane.slot(rel)], mate_send.at[p, rel],
            mate_recv.at[p, rel], plane.mate(),
        )

    def to_peer(p, step, rel):
        bit = plane.orders[p][step]
        return remote(
            source(p, rel), buf_ref.at[p, plane.slot(rel)], send.at[p, step, rel],
            recv.at[p, rel ^ bit], plane.peer(bit),
        )

    def finish(pairs):
        for p, rel in pairs:
            landed(buf_ref.at[p, plane.slot(rel, True)], mate_recv.at[p, rel])
            if consume is not None:
                consume(p, flip(plane.f, rel) * 2)

    first = [to_peer(p, 0, 0) for p in range(2)]
    for p in range(2):
        to_mate(p, 0)
    if consume is not None:
        for p in range(2):
            buf_ref[p, plane.slot(0)] = x_ref[p]
    have = [[0], [0]]
    pending = [(0, 0), (1, 0)]
    for step in range(plane.steps):
        for i in range(len(have[0])):
            finish(pending)
            if i == 0 and step + 1 < plane.steps:
                for copy in first:
                    copy.wait_send()
                    started[:] = [other for other in started if other is not copy]
                first = [to_peer(p, step + 1, 0) for p in range(2)]
            pending = [(p, have[p][i] ^ plane.orders[p][step]) for p in range(2)]
            for p, rel in pending:
                landed(buf_ref.at[p, plane.slot(rel)], recv.at[p, rel])
                to_mate(p, rel)
                for later in range(step + 1, plane.steps):
                    to_peer(p, later, rel)
        for p in range(2):
            have[p] = have[p] + [rel ^ plane.orders[p][step] for rel in have[p]]
    finish(pending)
    for copy in started:
        copy.wait_send()


def gather_actions(plane, x_ref, out_ref, sems, own_sem):
    send, recv, mate_send, mate_recv = sems

    def source(p, rel):
        return x_ref.at[p] if rel == 0 else out_ref.at[p, plane.slot(rel)]

    def to_mate(p, rel):
        return remote_copy(
            source(p, rel), out_ref.at[p, plane.slot(rel)], mate_send.at[p, rel],
            mate_recv.at[p, rel], plane.mate(),
        )

    def to_peer(p, step, rel):
        bit = plane.orders[p][step]
        return remote_copy(
            source(p, rel), out_ref.at[p, plane.slot(rel)], send.at[p, step, rel],
            recv.at[p, rel ^ bit], plane.peer(bit),
        )

    def own():
        return pltpu.make_async_copy(x_ref, out_ref.at[:, plane.slot(0)], own_sem)

    held = [[[0]], [[0]]]
    for step in range(plane.steps):
        for p in range(2):
            bit = plane.orders[p][step]
            held[p].append(held[p][-1] + [rel ^ bit for rel in held[p][-1]])

    def begin():
        for p in range(2):
            to_peer(p, 0, 0).start()
        for p in range(2):
            to_mate(p, 0).start()
        own().start()

    def group(step, i):
        if i == 0 and step + 1 < plane.steps:
            for p in range(2):
                to_peer(p, step, 0).wait_send()
                to_peer(p, step + 1, 0).start()
        for p in range(2):
            rel = held[p][step][i] ^ plane.orders[p][step]
            landed(out_ref.at[p, plane.slot(rel)], recv.at[p, rel])
            to_mate(p, rel).start()
            for later in range(step + 1, plane.steps):
                to_peer(p, later, rel).start()

    def close():
        for p in range(2):
            for rel in range(plane.fs):
                landed(out_ref.at[p, plane.slot(rel, True)], mate_recv.at[p, rel])
                to_mate(p, rel).wait_send()
            for step in range(plane.steps):
                for rel in held[p][step]:
                    if rel or step + 1 == plane.steps:
                        to_peer(p, step, rel).wait_send()
        own().wait()

    groups = [
        functools.partial(group, step, i)
        for step in range(plane.steps) for i in range(2**step)
    ]
    return [begin] + groups + [close]


class Line:
    def __init__(self, x_ref, out_ref, scratch):
        self.x_ref, self.out_ref = x_ref, out_ref
        self.send, self.recv, self.own_sem = scratch
        self.f, self.z, self.c = (lax.axis_index(a) for a in ("fsdp", "z", "core"))
        self.zs = out_ref.shape[0]

    @staticmethod
    def scratch(zs):
        dma = pltpu.SemaphoreType.DMA
        return [dma((2, zs)), dma((2, zs)), dma]

    def greet(self):
        bar = pltpu.get_barrier_semaphore()
        for way in (1, -1):
            to = lax.rem(self.z + way + self.zs, self.zs)
            pl.semaphore_signal(
                bar, inc=1, device_id=(self.f, to, self.c), device_id_type=MESH_ID
            )

    def copy(self, step, way):
        source = lax.rem(self.z - way * step + self.zs, self.zs)
        to = lax.rem(self.z + way + self.zs, self.zs)
        k = 0 if way > 0 else 1
        ref = self.out_ref.at[source]
        return remote_copy(
            ref if step else self.x_ref, ref, self.send.at[k, step], self.recv.at[k, step],
            (self.f, to, self.c),
        )

    def sends(self, step, way):
        if way > 0:
            return (self.z >= step) & (self.z < self.zs - 1)
        return (self.z < self.zs - step) & (self.z > 0)

    def arrived(self, step, way):
        k = 0 if way > 0 else 1
        source = lax.rem(self.z - way * (step + 1) + self.zs, self.zs)
        here = (self.z > step) if way > 0 else (self.z < self.zs - 1 - step)

        @pl.when(here)
        def _():
            landed(self.out_ref.at[source], self.recv.at[k, step])

    def own(self):
        return pltpu.make_async_copy(self.x_ref, self.out_ref.at[self.z], self.own_sem)

    def go(self, step):
        if step == 0:
            self.own().start()
        for way in (1, -1):
            if step:
                self.arrived(step - 1, way)
            if step < self.zs - 1:

                @pl.when(self.sends(step, way))
                def _(way=way):
                    self.copy(step, way).start()

    def close(self):
        self.own().wait()
        for step in range(self.zs - 1):
            for way in (1, -1):

                @pl.when(self.sends(step, way))
                def _(step=step, way=way):
                    self.copy(step, way).wait_send()


def scatter_scratch(fs, b, width):
    return [
        pltpu.VMEM((2, fs, b, width), jnp.bfloat16),
        pltpu.VMEM((2, fs, b, width), jnp.bfloat16),
        pltpu.VMEM((2, fs // 2, b, width), jnp.float32),
        pltpu.VMEM((2, fs, b, width), jnp.bfloat16),
        pltpu.VMEM((2, fs - 1, b, width), jnp.bfloat16),
        pltpu.SemaphoreType.DMA((fs, 2)),
        pltpu.SemaphoreType.DMA((fs, 2)),
        pltpu.SemaphoreType.DMA((2, fs)),
        pltpu.SemaphoreType.DMA((2, fs - 1)),
    ]


def scatter_actions(plane, partial, width, out_ref, scratch):
    give, got, total, outbox, inbox, give_sem, got_sem, send, recv = scratch
    b = out_ref.shape[1]
    rels = sorted(range(plane.fs), key=lambda r: (-bin(r).count("1"), r))
    whole = slice(0, width)

    def pieces(rel):
        if rel == rels[0]:
            return [slice(0, width // 2), slice(width // 2, width)]
        return [whole]

    def leaves(p, rel):
        for step, bit in enumerate(plane.orders[p]):
            if rel & bit:
                return step
        return plane.steps

    def place(p, step, rel):
        kept = [r for r in range(plane.fs) if leaves(p, r) > step]
        return plane.fs - 2 * len(kept) + kept.index(rel)

    def held(p, rel):
        return [r for r in range(plane.fs) if leaves(p, r) > 0].index(rel)

    def to_peer(p, rel):
        step = leaves(p, rel)
        bit = plane.orders[p][step]
        at = place(p, step, rel ^ bit)
        return remote_copy(
            outbox.at[p, rel], inbox.at[p, at], send.at[p, rel], recv.at[p, at], plane.peer(bit)
        )

    def to_mate(rel, i):
        cols = pieces(rel)[i]
        return remote_copy(
            give.at[:, rel, :, cols], got.at[:, rel, :, cols], give_sem.at[rel, i],
            got_sem.at[rel, i], plane.mate(),
        )

    def give_part(rel):
        theirs = plane.slot(rel, True)

        def body(cols):
            part = partial(theirs, cols).astype(jnp.bfloat16)
            give[0, rel, :, cols] = part[:b]
            give[1, rel, :, cols] = part[b:]

        for i, cols in enumerate(pieces(rel)):
            body(cols)
            to_mate(rel, i).start()

    def own_part(rel):
        mine = plane.slot(rel)

        def body(cols):
            part = partial(mine, cols)
            for p in range(2):
                here = part[p * b : (p + 1) * b] + got[p, rel, :, cols].astype(jnp.float32)
                if leaves(p, rel) == 0:
                    outbox[p, rel, :, cols] = here.astype(jnp.bfloat16)
                else:
                    total[p, held(p, rel), :, cols] = here

        for i, cols in enumerate(pieces(rel)):
            landed(got.at[:, rel, :, cols], got_sem.at[rel, i])
            body(cols)
        for p in range(2):
            if leaves(p, rel) == 0:
                to_peer(p, rel).start()

    def add_part(step, rel, p):
        at = place(p, step, rel)
        landed(inbox.at[p, at], recv.at[p, at])
        sends = leaves(p, rel) == step + 1

        def body(cols):
            here = total[p, held(p, rel), :, cols] + inbox[p, at, :, cols].astype(jnp.float32)
            if step + 1 == plane.steps:
                out_ref[p, :, cols] = here
            elif sends:
                outbox[p, rel, :, cols] = here.astype(jnp.bfloat16)
            else:
                total[p, held(p, rel), :, cols] = here

        body(whole)
        if sends and step + 1 < plane.steps:
            to_peer(p, rel).start()

    def close():
        for rel in rels:
            for i in range(len(pieces(rel))):
                to_mate(rel, i).wait_send()
            for p in range(2):
                if leaves(p, rel) < plane.steps:
                    to_peer(p, rel).wait_send()

    order = [(give_part, rels[0]), (own_part, rels[0]), (give_part, rels[1])]
    for i in range(2, len(rels)):
        order += [(give_part, rels[i]), (own_part, rels[i - 1])]
    order.append((own_part, rels[-1]))
    actions = [functools.partial(part, rel) for part, rel in order]
    for step in range(plane.steps):
        for rel in rels:
            for p in range(2):
                if leaves(p, rel) > step:
                    actions.append(functools.partial(add_part, step, rel, p))
    return actions + [close]


def vmem():
    return pl.BlockSpec(memory_space=pltpu.VMEM)


def anywhere():
    return pl.BlockSpec(memory_space=pl.ANY)


def plane_params(collective_id, limit=58):
    return pltpu.CompilerParams(
        collective_id=collective_id, has_side_effects=True, vmem_limit_bytes=limit * MIB
    )


class Staged:
    def __init__(self, refs, scratch):
        self.held = scratch[: len(refs)]
        self.loads = [
            pltpu.make_async_copy(ref, held, sem)
            for ref, held, sem in zip(refs, self.held, scratch[len(refs) :])
        ]
        for load in self.loads:
            load.start()

    @staticmethod
    def scratch(*arrays):
        dma = pltpu.SemaphoreType.DMA
        return [pltpu.VMEM(x.shape, x.dtype) for x in arrays] + [dma] * len(arrays)

    def wait(self):
        for load in self.loads:
            load.wait()


def gather_dot_kernel(fs, dims, tile, other, line, x_ref, *refs):
    count = 2 if other else 1
    hbm, refs = refs[:count], refs[count:]
    if line:
        l_ref, refs = refs[0], refs[1:]
    full_ref, y_ref, refs = refs[0], refs[1], refs[2:]
    if line:
        line, refs = Line(l_ref, refs[0], refs[1:4]), refs[4:]
    staged = Staged(hbm, refs[: 2 * count])
    buf_ref, sems = refs[2 * count], refs[2 * count + 1 :]
    plane = Plane(fs)
    if line:
        line.greet()
    plane.barrier(2 if line else 0)
    if line:
        line.go(0)
    w_ref = staged.held[0]
    a_ref = staged.held[1] if other else buf_ref
    keep_sem = sems[4]
    b, width = buf_ref.shape[2:]
    columns = y_ref.shape[3]
    kept = []

    def consume(p, slot):
        two = pl.ds(slot, 2)
        cp = pltpu.make_async_copy(
            buf_ref.at[p, two], full_ref.at[p, two], keep_sem.at[len(kept)]
        )
        cp.start()
        if not kept:
            staged.wait()
        kept.append(cp)

        def product(cols):
            w = w_ref[:, cols] if dims == NN else w_ref[cols, :]
            y = dotf(a_ref[p, two].reshape(2 * b, -1), w, dims)
            y_ref[p, two, :, cols] = y.astype(y_ref.dtype).reshape(2, b, tile)

        def one(j, carry):
            product(pl.ds(pl.multiple_of(j * tile, tile), tile))
            return carry

        if tile == columns:
            product(slice(None))
        else:
            lax.fori_loop(0, columns // tile, one, 0)
        if line and len(kept) % 2 == 0 and len(kept) // 2 < line.zs:
            line.go(len(kept) // 2)

    run_gather(plane, x_ref, buf_ref, sems[:4], consume)
    if line:
        for step in range(len(kept) // 2 + 1, line.zs):
            line.go(step)
        line.close()
    for cp in kept:
        cp.wait()


def plane_gather_dot(
    x, w, dims, seqs, collective_id, other=None, line=None, dtype=jnp.bfloat16
):
    fs, zs = lax.axis_size("fsdp"), lax.axis_size("z")
    x = x.reshape(seqs, -1, x.shape[1])
    _, b, width = x.shape
    columns = w.shape[1] if dims == NN else w.shape[0]
    tile = next((t for t in (1024, 768, 256, 128) if columns % t == 0), columns)
    lead = (seqs, 2 * fs, b)
    staged = [w] if other is None else [w, other.reshape(lead + (-1,))]
    out_shape = [
        jax.ShapeDtypeStruct(lead + (width,), x.dtype),
        jax.ShapeDtypeStruct(lead + (columns,), dtype),
    ]
    args, scratch = [x] + staged, []
    in_specs, out_specs = [vmem()] + [anywhere()] * len(staged), [anywhere(), vmem()]
    if line is not None:
        args.append(line)
        in_specs.append(vmem())
        out_shape.append(jax.ShapeDtypeStruct((zs,) + line.shape, line.dtype))
        out_specs.append(anywhere())
        scratch += Line.scratch(zs)
    out = pl.pallas_call(
        functools.partial(gather_dot_kernel, fs, dims, tile, other is not None, line is not None),
        out_shape=out_shape,
        in_specs=in_specs,
        out_specs=out_specs,
        scratch_shapes=scratch
        + Staged.scratch(*staged)
        + [pltpu.VMEM(lead + (width,), x.dtype)]
        + gather_sems(fs)
        + [pltpu.SemaphoreType.DMA((seqs * fs,))],
        compiler_params=plane_params(collective_id),
        cost_estimate=estimate(45),
        name="plane_gather_dot",
    )(*args)
    return (out[0].reshape(-1, width), out[1].reshape(-1, columns)) + tuple(out[2:])


class Swap:
    def __init__(self, x_ref, out_ref, scratch):
        self.x_ref, self.out_ref = x_ref, out_ref
        self.relay, self.own_sem, self.in_send, self.in_recv, self.on_send, self.on_recv = scratch
        self.f, self.z, self.c = (lax.axis_index(a) for a in ("fsdp", "z", "core"))
        self.fs, self.size = self.relay.shape[:2]

    @staticmethod
    def scratch(fs, rows, width):
        dma = pltpu.SemaphoreType.DMA
        return [
            pltpu.VMEM((fs, rows // fs, width), jnp.bfloat16), dma,
            dma((fs,)), dma((fs,)), dma((fs,)), dma((fs,)),
        ]

    def column(self, d):
        return lax.rem(self.f + d, self.fs)

    def part(self, ref, k):
        return ref.at[pl.ds(pl.multiple_of(k * self.size, self.size), self.size)]

    def straight(self):
        return remote_copy(
            self.part(self.x_ref, self.f), self.part(self.out_ref, self.f), self.in_send.at[0],
            self.on_recv.at[self.f], (self.z, self.f, self.c),
        )

    def inward(self, d):
        k = self.column(d)
        return remote_copy(
            self.part(self.x_ref, k), self.relay.at[d], self.in_send.at[d],
            self.in_recv.at[d], (k, self.z, self.c),
        )

    def onward(self, d):
        source = self.column(self.fs - d)
        return remote_copy(
            self.relay.at[d], self.part(self.out_ref, self.f), self.on_send.at[d],
            self.on_recv.at[self.f], (self.z, source, self.c),
        )

    def own(self):
        return pltpu.make_async_copy(self.x_ref, self.out_ref, self.own_sem)

    def start_inward(self):
        @pl.when(self.f != self.z)
        def _():
            for d in range(1, self.fs):
                self.inward(d).start()

    def start_straight(self):
        @pl.when(self.f != self.z)
        def _():
            self.straight().start()

        @pl.when(self.f == self.z)
        def _():
            self.own().start()

    def start(self):
        self.start_inward()
        self.start_straight()

    def relayed(self, body):
        for d in range(1, self.fs):

            @pl.when(self.column(self.fs - d) != self.z)
            def _(d=d):
                body(d)

    def hand_on(self):
        def one(d):
            landed(self.relay.at[d], self.in_recv.at[d])
            self.onward(d).start()

        self.relayed(one)

    def close(self):
        self.relayed(lambda d: self.onward(d).wait_send())

        @pl.when(self.f == self.z)
        def _():
            self.own().wait()

        @pl.when(self.f != self.z)
        def _():
            self.straight().wait_send()
            for d in range(1, self.fs):
                self.inward(d).wait_send()
            for k in range(self.fs):
                landed(self.part(self.out_ref, k), self.on_recv.at[k])


def plane_and_column_greet():
    fs, zs, cs = (lax.axis_size(a) for a in ("fsdp", "z", "core"))
    f, z, c = (lax.axis_index(a) for a in ("fsdp", "z", "core"))
    bar = pltpu.get_barrier_semaphore()
    places = [(lax.rem(f + df, fs), z, lax.rem(c + dc, cs)) for df in range(fs) for dc in range(cs)]
    places = places[1:] + [(f, lax.rem(z + dz, zs), c) for dz in range(1, zs)]
    places += [
        (lax.rem(f + df, fs), lax.rem(z + dz, zs), c) for df in range(1, fs) for dz in range(1, zs)
    ]
    for place in places:
        pl.semaphore_signal(bar, inc=1, device_id=place, device_id_type=MESH_ID)
    pl.semaphore_wait(bar, len(places))


class Column:
    def __init__(self, x_ref, sum_ref, scratch):
        self.x_ref, self.sum_ref = x_ref, sum_ref
        self.inbox, self.send, self.recv = scratch
        self.f, self.z, self.c = (lax.axis_index(a) for a in ("fsdp", "z", "core"))
        self.zs = x_ref.shape[0]

    @staticmethod
    def scratch(x):
        dma = pltpu.SemaphoreType.DMA
        return [pltpu.VMEM(x.shape, x.dtype), dma((x.shape[0],)), dma((x.shape[0],))]

    def copy(self, d):
        to = lax.rem(self.z + d, self.zs)
        return remote_copy(
            self.x_ref.at[to], self.inbox.at[d], self.send.at[d], self.recv.at[d],
            (self.f, to, self.c),
        )

    def start(self):
        for d in range(1, self.zs):
            self.copy(d).start()

    def close(self):
        for d in range(1, self.zs):
            self.copy(d).wait_send()
            landed(self.inbox.at[d], self.recv.at[d])
        total = self.x_ref[self.z].astype(jnp.float32)
        for d in range(1, self.zs):
            total = total + self.inbox[d].astype(jnp.float32)
        self.sum_ref[...] = total


class Back:
    def __init__(self, sizes, src_ref, got_ref, scratch):
        fs, zs, self.cs = sizes
        self.src_ref, self.got_ref = src_ref, got_ref
        self.send, self.recv, self.own_sem = scratch
        self.z = lax.axis_index("z")
        self.devices = fs * self.cs
        self.me = lax.axis_index("fsdp") * self.cs + lax.axis_index("core")

    @staticmethod
    def scratch(devices):
        dma = pltpu.SemaphoreType.DMA
        return [dma((devices,)), dma((devices,)), dma]

    def copy(self, d):
        to = lax.rem(self.me + d, self.devices)
        return remote_copy(
            self.src_ref.at[to], self.got_ref.at[self.me], self.send.at[d], self.recv.at[d],
            (lax.div(to, self.cs), self.z, lax.rem(to, self.cs)),
        )

    def own(self):
        return pltpu.make_async_copy(
            self.src_ref.at[self.me], self.got_ref.at[self.me], self.own_sem
        )

    def start(self):
        for d in range(1, self.devices):
            self.copy(d).start()
        self.own().start()

    def arrived(self):
        for d in range(1, self.devices):
            at = lax.rem(self.me + self.devices - d, self.devices)
            landed(self.got_ref.at[at], self.recv.at[d])
        self.own().wait()

    def close(self):
        for d in range(1, self.devices):
            self.copy(d).wait_send()


class Everyone:
    def __init__(self, sizes):
        self.fs, self.zs, self.cs = sizes
        self.n = math.prod(sizes)
        f, z, c = (lax.axis_index(a) for a in ("fsdp", "z", "core"))
        self.me = (f * self.zs + z) * self.cs + c

    def place(self, d):
        f, z, c = (lax.axis_index(a) for a in ("fsdp", "z", "core"))
        df, dz, dc = d // (self.zs * self.cs), d // self.cs % self.zs, d % self.cs
        return (lax.rem(f + df, self.fs), lax.rem(z + dz, self.zs), lax.rem(c + dc, self.cs))

    def index(self, place):
        return (place[0] * self.zs + place[1]) * self.cs + place[2]

    def back(self, d):
        f, z, c = (lax.axis_index(a) for a in ("fsdp", "z", "core"))
        df, dz, dc = d // (self.zs * self.cs), d // self.cs % self.zs, d % self.cs
        return self.index((
            lax.rem(f + self.fs - df, self.fs), lax.rem(z + self.zs - dz, self.zs),
            lax.rem(c + self.cs - dc, self.cs),
        ))

    def greet(self):
        bar = pltpu.get_barrier_semaphore()
        for d in range(1, self.n):
            pl.semaphore_signal(bar, inc=1, device_id=self.place(d), device_id_type=MESH_ID)

    def met(self):
        pl.semaphore_wait(pltpu.get_barrier_semaphore(), self.n - 1)

    def copy(self, d, x_ref, spread_out, slots, send, recv):
        to = self.place(d)
        src = x_ref.at[self.index(to)] if spread_out else x_ref.at[0]
        return remote_copy(src, slots.at[self.me], send.at[d], recv.at[d], to)

    def begin(self, x_ref, spread_out, slots, send, recv, own_sem):
        for d in range(1, self.n):
            self.copy(d, x_ref, spread_out, slots, send, recv).start()
        src = x_ref.at[self.me] if spread_out else x_ref.at[0]
        own = pltpu.make_async_copy(src, slots.at[self.me], own_sem)
        own.start()
        own.wait()

    def finish(self, x_ref, spread_out, slots, send, recv):
        for d in range(1, self.n):
            landed(slots.at[self.back(d)], recv.at[d])
        for d in range(1, self.n):
            self.copy(d, x_ref, spread_out, slots, send, recv).wait_send()


def slot_product(a_ref, w_ref, dims):
    def partial(slot, cols):
        a = a_ref[:, slot].reshape(-1, a_ref.shape[3])
        return dotf(a, w_ref[:, cols] if dims == NN else w_ref[cols, :], dims)

    return partial


def row_blocks(ref, block, body):
    per = ref.shape[1] // block

    def one(i, carry):
        here = pl.ds(pl.multiple_of(lax.rem(i, per) * block, block), block)
        body(lax.div(i, per), here)
        return carry

    lax.fori_loop(0, 2 * per, one, 0)


def dot_scatter_kernel(fs, dims, beside, then, *refs):
    hbm, refs = refs[:2], refs[2:]
    if beside:
        later, refs = refs[:2], refs[2:]
    if then:
        (base_ref, factor_ref), refs = refs[:2], refs[2:]
    outs, refs = refs[: 2 if then == "norm" else 1], refs[2 if then == "norm" else 1 :]
    if beside:
        g_ref, refs = refs[0], refs[1:]
    staged, refs = Staged(hbm, refs[:4]), refs[4:]
    if beside:
        later, refs = Staged(later, refs[:4]), refs[4:]
        l_ref, r_ref = later.held
    sum_ref = outs[0]
    if then:
        sum_ref, refs = refs[0], refs[1:]
    plane = Plane(fs)
    plane.barrier()
    staged.wait()
    partial = slot_product(*staged.held, dims)
    actions = scatter_actions(plane, partial, sum_ref.shape[2], sum_ref, refs)
    first = 2 * fs
    for action in actions[:first]:
        action()
    if beside:
        later.wait()
        block = 256

        def one(i, carry):
            here = pl.ds(pl.multiple_of(i * block, block), block)
            g_ref[here, :] = dotf(l_ref[:, here].T, r_ref[...]).astype(g_ref.dtype)
            return carry

        steps = l_ref.shape[1] // block
        lax.fori_loop(0, steps // 2, one, 0)
    middle = first + len(actions[first:-1]) - 2
    for action in actions[first:middle]:
        action()
    if beside:
        lax.fori_loop(steps // 2, steps, one, 0)
    for action in actions[middle:]:
        action()

    def normed(p, here):
        hidden = base_ref[p, here, :].astype(jnp.float32) + sum_ref[p, here, :]
        outs[0][p, here, :] = hidden
        scale = lax.rsqrt(jnp.mean(hidden * hidden, axis=1, keepdims=True) + EPSILON)
        outs[1][p, here, :] = (hidden * scale * factor_ref[...]).astype(jnp.bfloat16)

    def result(p, here):
        hidden = base_ref[p, here, :] + sum_ref[p, here, :]
        outs[0][p, here, :] = (hidden * factor_ref[p, here, :]).astype(jnp.bfloat16)

    if then:
        row_blocks(sum_ref, 32, normed if then == "norm" else result)


def plane_dot_scatter(
    a, w, dims, seqs, collective_id, beside=None, norm=None, result=None
):
    fs = lax.axis_size("fsdp")
    a = a.reshape(seqs, 2 * fs, -1, a.shape[1])
    b = a.shape[2]
    width = w.shape[1] if dims == NN else w.shape[0]
    own = (seqs, b, width)
    args = [a, w]
    in_specs = [anywhere()] * 2
    scratch = Staged.scratch(a, w)
    out_shape = [jax.ShapeDtypeStruct(own, jnp.bfloat16 if result else jnp.float32)]
    if beside is not None:
        args += beside
        in_specs += [anywhere()] * 2
        scratch += Staged.scratch(*beside)
    if norm is not None:
        args += [norm[0].reshape(own), norm[1]]
        out_shape.append(jax.ShapeDtypeStruct(own, jnp.bfloat16))
    if result is not None:
        args += [result[0].reshape(own), result[1].reshape(seqs, b, 1)]
    if norm is not None or result is not None:
        in_specs += [vmem()] * 2
        scratch.append(pltpu.VMEM(own, jnp.float32))
    if beside is not None:
        out_shape.append(
            jax.ShapeDtypeStruct((beside[0].shape[1], beside[1].shape[1]), jnp.bfloat16)
        )
    then = "norm" if norm is not None else "result" if result is not None else ""
    out = pl.pallas_call(
        functools.partial(dot_scatter_kernel, fs, dims, beside is not None, then),
        out_shape=out_shape,
        in_specs=in_specs,
        out_specs=[vmem()] * len(out_shape),
        scratch_shapes=scratch + scatter_scratch(fs, b, width),
        compiler_params=plane_params(collective_id, 62),
        cost_estimate=estimate(45),
        name="plane_dot_scatter",
    )(*args)
    out = [out[0].reshape(-1, width)] + list(out[1:])
    if norm is not None:
        out[1] = out[1].reshape(-1, width)
    return out if len(out) > 1 else out[0]


def norm_turn_kernel(
    fs, a_hbm, w_hbm, hid_ref, cot_ref, gain_ref, wo_ref, o_ref, y_ref, wg_ref, grad_ref, gsum_ref,
    a_ref, w_ref, a_sem, w_sem, sum_ref, x_ref, buf_ref, acc_ref, *scratch
):
    staged = Staged((a_hbm, w_hbm), (a_ref, w_ref, a_sem, w_sem))
    plane = Plane(fs)
    plane.barrier()
    acc_ref[...] = jnp.zeros_like(acc_ref)
    staged.wait()
    b, width = x_ref.shape[1:]
    partial = slot_product(a_ref, w_ref, NT)
    for action in scatter_actions(plane, partial, width, sum_ref, scratch[4:]):
        action()
    block = 32
    tile = wide_tile(width)
    gain = gain_ref[...]

    def turn(i, total):
        p, at = lax.div(i, b // block), pl.multiple_of(lax.rem(i, b // block) * block, block)
        here = pl.ds(at, block)
        grad, hidden = sum_ref[p, here, :], hid_ref[p, here, :]
        scale = lax.rsqrt(jnp.mean(hidden * hidden, axis=1, keepdims=True) + EPSILON)
        weighted = grad * gain
        inner = jnp.mean(weighted * hidden, axis=1, keepdims=True)
        back = scale * (weighted - hidden * scale * scale * inner)
        back = cot_ref[p, here, :].astype(jnp.float32) + back
        grad_ref[p, here, :] = back
        x_ref[p, here, :] = back.astype(jnp.bfloat16)
        return total + grad * hidden * scale

    total = lax.fori_loop(
        0, 2 * (b // block), turn, jnp.zeros((block, width), jnp.float32)
    )
    gsum_ref[...] = jnp.sum(total, axis=0, keepdims=True)

    def consume(p, slot):
        two = pl.ds(slot, 2)
        rows = buf_ref[p, two].reshape(2 * b, width)
        y = dotf(rows, wo_ref[...], NT)
        y_ref[p, two] = y.astype(y_ref.dtype).reshape(2, b, -1)
        o_t = o_ref[p, two].reshape(2 * b, -1).T

        def grad(j, carry):
            cols = pl.ds(pl.multiple_of(j * tile, tile), tile)
            acc_ref[:, cols] += dotf(o_t, buf_ref[p, two, :, cols].reshape(2 * b, tile))
            return carry

        lax.fori_loop(0, width // tile, grad, 0)

    run_gather(plane, x_ref, buf_ref, scratch[:4], consume)
    wg_ref[...] = acc_ref[...].astype(wg_ref.dtype)


def norm_turn(a, w, hidden, cot, gain, w_o, attended, seqs, collective_id):
    fs = lax.axis_size("fsdp")
    lead = (seqs, 2 * fs, a.shape[0] // (2 * fs * seqs))
    b, width = lead[2], hidden.shape[1]
    own = (seqs, b, width)
    a = a.reshape(lead + (-1,))
    attended = attended.reshape(lead + (-1,))
    k = attended.shape[3]
    y, wg, grad, gsum = pl.pallas_call(
        functools.partial(norm_turn_kernel, fs),
        out_shape=[
            jax.ShapeDtypeStruct(lead + (k,), jnp.bfloat16),
            jax.ShapeDtypeStruct((k, width), jnp.bfloat16),
            jax.ShapeDtypeStruct(own, jnp.float32),
            jax.ShapeDtypeStruct((1, width), jnp.float32),
        ],
        in_specs=[anywhere()] * 2 + [vmem()] * 5,
        out_specs=[vmem()] * 4,
        scratch_shapes=Staged.scratch(a, w)
        + [
            pltpu.VMEM(own, jnp.float32),
            pltpu.VMEM(own, jnp.bfloat16),
            pltpu.VMEM(lead + (width,), jnp.bfloat16),
            pltpu.VMEM((k, width), jnp.float32),
        ]
        + gather_sems(fs)
        + scatter_scratch(fs, b, width),
        compiler_params=plane_params(collective_id, 62),
        cost_estimate=estimate(45),
        name="norm_turn",
    )(a, w, hidden.reshape(own), cot.reshape(own), gain, w_o, attended)
    return y.reshape(-1, k), wg, grad.reshape(-1, width), gsum[0]


GELU_C = math.sqrt(2.0 / math.pi)


def ffn_kernel(x_ref, gh_ref, g_ref, wgu_ref, h_ref, ggu_ref, wg_ref, acc_ref):
    step = pl.program_id(0)
    ff = h_ref.shape[1]

    @pl.when(step == 0)
    def _():
        acc_ref[...] = jnp.zeros_like(acc_ref)

    gate = dotf(x_ref[...], wgu_ref[:, :ff])
    up = dotf(x_ref[...], wgu_ref[:, ff:])
    grad_hidden = gh_ref[...]
    square = gate * gate
    tanh = jnp.tanh(GELU_C * gate * (1.0 + 0.044715 * square))
    half = 0.5 * (1.0 + tanh)
    act = gate * half
    slope = half + (0.5 * GELU_C) * gate * (1.0 - tanh * tanh) * (1.0 + 0.134145 * square)
    hidden = (act * up).astype(jnp.bfloat16)
    h_ref[...] = hidden
    ggu_ref[:, :ff] = (grad_hidden * up * slope).astype(jnp.bfloat16)
    ggu_ref[:, ff:] = (grad_hidden * act).astype(jnp.bfloat16)
    acc_ref[...] += dotf(hidden.T, g_ref[...])

    @pl.when(step == pl.num_programs(0) - 1)
    def _():
        wg_ref[...] = acc_ref[...].astype(jnp.bfloat16)


def ffn(x, grad_hidden, grad, w_gu):
    rows, width = x.shape
    ff = grad_hidden.shape[1]
    block = math.gcd(rows, 512)

    def blocks(columns):
        return pl.BlockSpec((block, columns), lambda i: (i, 0))

    def held(shape):
        return pl.BlockSpec(shape, lambda i: (0, 0), pipeline_mode=pl.Buffered(1))

    return pl.pallas_call(
        ffn_kernel,
        grid=(rows // block,),
        out_shape=[
            jax.ShapeDtypeStruct((rows, ff), jnp.bfloat16),
            jax.ShapeDtypeStruct((rows, 2 * ff), jnp.bfloat16),
            jax.ShapeDtypeStruct((ff, width), jnp.bfloat16),
        ],
        in_specs=[blocks(width), blocks(ff), blocks(width), held(w_gu.shape)],
        out_specs=[blocks(ff), blocks(2 * ff), pl.BlockSpec((ff, width), lambda i: (0, 0))],
        scratch_shapes=[pltpu.VMEM((ff, width), jnp.float32)],
        compiler_params=pltpu.CompilerParams(
            dimension_semantics=("arbitrary",), vmem_limit_bytes=60 * MIB
        ),
        cost_estimate=estimate(30),
        name="ffn",
    )(x, grad_hidden, grad, w_gu)

def column_runs(sizes, per_device, total, natural):
    fs, zs, cs = sizes
    if not natural:
        size = total // (fs * cs)
        return [(t * size, t, 0, size) for t in range(fs * cs)]
    return [
        (((f * zs + z) * cs + c) * per_device, f * cs + c, z * per_device, per_device)
        for f in range(fs) for z in range(zs) for c in range(cs)
    ]


def start_kernel(
    sizes, runs, small_ref, q_ref, k_ref, v_ref, gate_ref, up_ref, tok_ref, cot_ref, o_ref, d_ref,
    small_out, wqkv_ref, ggu_ref, x_ref, g_ref, o_out, d_out,
    slots, qkv_ref, gu_ref, s_send, s_recv, own_sem, q_send, q_recv, g_send, g_recv,
    line_send, line_recv, *swap_scratch,
):
    fs, zs, cs = sizes
    f, z, c = (lax.axis_index(a) for a in ("fsdp", "z", "core"))
    me = f * cs + c
    devices = fs * cs
    rows = qkv_ref.shape[1]
    everyone = Everyone(sizes)
    everyone.greet()

    def split(pieces_ref, parts, run):
        size = pieces_ref.shape[2] // len(parts)
        for i, part in enumerate(parts):
            for at, device, start, count in run:
                here = part[:, at : at + count].astype(jnp.bfloat16)
                pieces_ref[device, :, i * size + start : i * size + start + count] = here

    split(qkv_ref, (q_ref, k_ref, v_ref), runs[1])
    half = len(swap_scratch) // 2
    swaps = [
        Swap(tok_ref, x_ref, swap_scratch[:half]), Swap(cot_ref, g_ref, swap_scratch[half:])
    ]
    everyone.met()
    everyone.begin(small_ref, False, slots, s_send, s_recv, own_sem.at[0])

    def block(out_ref, index, lead):
        at = pl.ds(pl.multiple_of(lax.rem(index, cs) * rows, rows), rows)
        if lead is None:
            return out_ref.at[lax.div(index, cs), at]
        return out_ref.at[lax.div(index, cs), lead, at]

    def spread_copy(d, src_ref, out_ref, lead, send, recv):
        to = lax.rem(me + d, devices)
        return remote_copy(
            src_ref.at[to], block(out_ref, me, lead), send.at[d], recv.at[d],
            (lax.div(to, cs), z, lax.rem(to, cs)),
        )

    own_qkv = pltpu.make_async_copy(qkv_ref.at[me], block(wqkv_ref, me, z), own_sem.at[1])
    own_gu = pltpu.make_async_copy(gu_ref.at[me], block(ggu_ref, me, None), own_sem.at[2])
    own_qkv.start()
    for d in range(1, devices):
        spread_copy(d, qkv_ref, wqkv_ref, z, q_send, q_recv).start()
    swaps[0].start()
    split(gu_ref, (gate_ref, up_ref), runs[0])
    own_gu.start()
    o_out[...] = o_ref[...].astype(jnp.bfloat16)
    d_out[...] = d_ref[...].astype(jnp.bfloat16)
    def chip(p):
        return lax.rem(f + p, fs)

    def line(step, way, p):
        source = lax.rem(z - way * step + zs, zs)
        to = lax.rem(z + way + zs, zs)
        k = 0 if way > 0 else 1
        ref = wqkv_ref.at[chip(p), source]
        return remote_copy(
            ref, ref, line_send.at[k, step, p], line_recv.at[k, step, p], (f, to, c)
        )

    def sends(step, way):
        if way > 0:
            return (z >= step) & (z < zs - 1)
        return (z < zs - step) & (z > 0)

    def arrives(step, way):
        return (z > step) if way > 0 else (z < zs - 1 - step)

    def arrive(step, way, p):
        k = 0 if way > 0 else 1
        source = lax.rem(z - way * (step + 1) + zs, zs)
        landed(wqkv_ref.at[chip(p), source], line_recv.at[k, step, p])

    def spread_arrive(df, dc):
        index = chip(df) * cs + lax.rem(c + dc, cs)
        d = lax.rem(me - index + devices, devices)
        landed(block(wqkv_ref, index, z), q_recv.at[d])

    for step in range(zs - 1):
        for p in range(fs):
            if step == 0:
                if p == 0:
                    own_qkv.wait()
                for dc in range(cs):
                    if p or dc:
                        spread_arrive(p, dc)
            for way in (1, -1):
                if step:

                    @pl.when(arrives(step - 1, way))
                    def _(step=step, way=way, p=p):
                        arrive(step - 1, way, p)

                @pl.when(sends(step, way))
                def _(step=step, way=way, p=p):
                    line(step, way, p).start()

        if step == 0:
            swaps[0].hand_on()
            swaps[1].start()
            for d in range(1, devices):
                spread_copy(d, gu_ref, ggu_ref, None, g_send, g_recv).start()
        if step == 1:
            swaps[1].hand_on()
    for p in range(fs):
        for way in (1, -1):

            @pl.when(arrives(zs - 2, way))
            def _(way=way, p=p):
                arrive(zs - 2, way, p)

    everyone.finish(small_ref, False, slots, s_send, s_recv)
    small_out[...] = slots[...]
    own_gu.wait()
    for d in range(1, devices):
        landed(block(ggu_ref, lax.rem(me + devices - d, devices), None), g_recv.at[d])
    for d in range(1, devices):
        spread_copy(d, qkv_ref, wqkv_ref, z, q_send, q_recv).wait_send()
        spread_copy(d, gu_ref, ggu_ref, None, g_send, g_recv).wait_send()
    for step in range(zs - 1):
        for p in range(fs):
            for way in (1, -1):

                @pl.when(sends(step, way))
                def _(step=step, way=way, p=p):
                    line(step, way, p).wait_send()

    for swap in swaps:
        swap.close()


def start(small, qkv, gu, tokens, cotangent, own_o, own_d, runs, collective_id):
    sizes = tuple(lax.axis_size(a) for a in ("fsdp", "z", "core"))
    fs, zs, cs = sizes
    n = math.prod(sizes)
    devices = fs * cs
    rows = qkv[0].shape[0]
    qkv_cols = sum(w.shape[1] for w in qkv) // devices
    gu_cols = sum(w.shape[1] for w in gu) // devices
    dma = pltpu.SemaphoreType.DMA
    return pl.pallas_call(
        functools.partial(start_kernel, sizes, runs),
        out_shape=[
            jax.ShapeDtypeStruct((n, 8, 128), jnp.float32),
            jax.ShapeDtypeStruct((fs, zs, cs * rows, qkv_cols), jnp.bfloat16),
            jax.ShapeDtypeStruct((fs, cs * rows, gu_cols), jnp.bfloat16),
            jax.ShapeDtypeStruct(tokens.shape, tokens.dtype),
            jax.ShapeDtypeStruct(cotangent.shape, cotangent.dtype),
            jax.ShapeDtypeStruct(own_o.shape, jnp.bfloat16),
            jax.ShapeDtypeStruct(own_d.shape, jnp.bfloat16),
        ],
        in_specs=[vmem()] * 10,
        out_specs=[vmem()] + [anywhere()] * 4 + [vmem()] * 2,
        scratch_shapes=[
            pltpu.VMEM((n, 8, 128), jnp.float32),
            pltpu.VMEM((devices, rows, qkv_cols), jnp.bfloat16),
            pltpu.VMEM((devices, rows, gu_cols), jnp.bfloat16),
            dma((n,)), dma((n,)), dma((3,)),
            dma((devices,)), dma((devices,)), dma((devices,)), dma((devices,)),
            dma((2, zs, fs)), dma((2, zs, fs)),
        ]
        + Swap.scratch(fs, *tokens.shape) * 2,
        compiler_params=plane_params(collective_id),
        cost_estimate=estimate(120),
        name="start",
    )(small, *qkv, *gu, tokens, cotangent, own_o, own_d)


def finish_kernel(
    sizes, runs, small_ref, g_ref, qkv_ref, gu_ref, small_out, out_ref, gate_ref, up_ref,
    q_ref, k_ref, v_ref, slots, got_qkv, send, recv, own_sem, back_send, back_recv, back_sem,
    *swap_scratch
):
    everyone = Everyone(sizes)
    everyone.greet()
    back = Back(sizes, qkv_ref, got_qkv, (back_send, back_recv, back_sem))
    swap = Swap(g_ref, out_ref, swap_scratch)
    everyone.met()
    swap.start()
    everyone.begin(small_ref, True, slots, send, recv, own_sem)
    back.start()
    swap.hand_on()

    def join(got_ref, pieces, run):
        size = got_ref.shape[2] // len(pieces)
        for i, piece in enumerate(pieces):
            for to, device, start, count in run:
                part = got_ref[device, :, i * size + start : i * size + start + count]
                piece[:, to : to + count] = part.astype(jnp.float32)

    join(gu_ref, (gate_ref, up_ref), runs[0])
    back.arrived()
    join(got_qkv, (q_ref, k_ref, v_ref), runs[1])
    everyone.finish(small_ref, True, slots, send, recv)
    small_out[...] = jnp.sum(slots[...], axis=0)
    back.close()
    swap.close()


def finish(small, grad, sum_qkv, got_gu, runs, columns, collective_id):
    sizes = tuple(lax.axis_size(a) for a in ("fsdp", "z", "core"))
    fs, zs, cs = sizes
    n = math.prod(sizes)
    devices = fs * cs
    dma = pltpu.SemaphoreType.DMA
    sum_qkv = sum_qkv.reshape(devices, -1, sum_qkv.shape[2])
    wide = [jax.ShapeDtypeStruct((sum_qkv.shape[1], k), jnp.float32) for k in columns]
    return pl.pallas_call(
        functools.partial(finish_kernel, sizes, runs),
        out_shape=[
            jax.ShapeDtypeStruct((8, 128), small.dtype),
            jax.ShapeDtypeStruct(grad.shape, grad.dtype),
        ]
        + wide,
        in_specs=[vmem()] * 4,
        out_specs=[vmem(), anywhere()] + [vmem()] * len(wide),
        scratch_shapes=[
            pltpu.VMEM((n, 8, 128), small.dtype),
            pltpu.VMEM(sum_qkv.shape, jnp.bfloat16),
            dma((n,)), dma((n,)), dma,
        ]
        + Back.scratch(devices)
        + Swap.scratch(fs, *grad.shape),
        compiler_params=plane_params(collective_id),
        cost_estimate=estimate(45),
        name="finish",
    )(small, grad, sum_qkv, got_gu)


def to_tiles(x):
    return jnp.pad(x, ((0, 0), (0, 1024 - x.shape[1]))).reshape(-1, 8, 128)

from jax.sharding import Mesh
from jax.sharding import PartitionSpec as P

H = 32
HIGHEST = lax.Precision.HIGHEST
BF = jnp.bfloat16
F32 = jnp.float32
TP = ("fsdp", "core")
ALL = ("fsdp", "z", "core")


def rms_scale(values):
    return lax.rsqrt(jnp.mean(values * values, axis=1, keepdims=True) + EPSILON)


def norm_back(grad_normed, values, row_scale, gain_row):
    weighted = grad_normed * gain_row
    inner_mean = jnp.mean(weighted * values, axis=1, keepdims=True)
    return row_scale * (weighted - values * row_scale * row_scale * inner_mean)


class Layout:
    def __init__(self, per_device, head_dim):
        self.f, self.z, self.c = (lax.axis_size(a) for a in ALL)
        self.natural = per_device % head_dim == 0
        self.per_device = per_device

    def split(self, w):
        rows, cols = w.shape
        if self.natural:
            w = w.reshape(rows, self.f, self.z, self.c, self.per_device)
            w = w.transpose(1, 3, 0, 2, 4)
        else:
            w = w.reshape(rows, self.f, self.c, -1).transpose(1, 2, 0, 3)
        return w.reshape(self.f * self.c, rows, -1)

    def join(self, w):
        devices, rows, cols = w.shape
        if self.natural:
            w = w.reshape(self.f, self.c, rows, self.z, self.per_device)
            w = w.transpose(2, 0, 3, 1, 4)
        else:
            w = w.reshape(self.f, self.c, rows, cols).transpose(2, 0, 1, 3)
        return w.reshape(rows, -1)

    def gather(self, w):
        if self.natural:
            return lax.all_gather(w, "z", axis=0, tiled=True)
        both = lax.all_gather(w, ("z", "core"), axis=0, tiled=True)
        size = both.shape[0] // self.c
        return lax.dynamic_slice_in_dim(both, lax.axis_index("core") * size, size, 0)

    def whole(self, g):
        if self.natural:
            return g
        size = g.shape[0]
        both = jnp.zeros((size * self.c, g.shape[1]), g.dtype)
        both = lax.dynamic_update_slice_in_dim(both, g, lax.axis_index("core") * size, 0)
        both = lax.psum(both, "core").reshape(self.z, self.c, -1, g.shape[1])
        mine = lax.dynamic_index_in_dim(both, lax.axis_index("core"), 1, keepdims=False)
        return mine.reshape(-1, g.shape[1])

    def scatter(self, g):
        return lax.psum_scatter(g, "z", scatter_dimension=0, tiled=True)


def over_z(got):
    f, cr, cols = got.shape
    full = lax.all_gather(got, "z", axis=1, tiled=True)
    return full.reshape(-1, cols)


def reduce_z(grad):
    f, z = lax.axis_size("fsdp"), lax.axis_size("z")
    return lax.psum_scatter(
        grad.reshape(f, grad.shape[0] // f, -1), "z", scatter_dimension=1, tiled=True
    )


def shards(
    tokens, cotangent, lengths, buckets, norm1_gain, rel_bias,
    w_query, w_key, w_value, w_attn_out, norm2_gain, w_gate, w_up, w_down,
):
    fs, zs, cs = (lax.axis_size(a) for a in ALL)
    seqs, block_len, width = tokens.shape
    rows = seqs * block_len
    length = block_len * fs * cs
    head_dim = w_query.shape[1] // H
    heads = H // (fs * cs)
    buckets_n = rel_bias.shape[0] * fs * zs * cs // H
    head_cols = Layout(w_attn_out.shape[0], head_dim)
    ff_cols = Layout(w_down.shape[0], w_down.shape[0])

    own_small = jnp.concatenate([norm1_gain, norm2_gain, rel_bias]).astype(BF).astype(F32)
    own_small = jnp.concatenate([own_small, lengths.astype(F32)])
    sizes = (fs, zs, cs)
    runs = (
        column_runs(sizes, ff_cols.per_device, w_gate.shape[1], True),
        column_runs(sizes, head_cols.per_device, w_query.shape[1], head_cols.natural),
    )
    small, w_qkv, got_gu, x_in, cot, own_o, own_d = start(
        to_tiles(own_small[None]), (w_query, w_key, w_value), (w_gate, w_up),
        tokens.reshape(rows, width), cotangent.reshape(rows, width), w_attn_out, w_down, runs, 9,
    )
    w_qkv = w_qkv.reshape(width, -1)
    w_o = head_cols.gather(own_o)
    w_gu = over_z(got_gu)
    w_d = ff_cols.gather(own_d)
    small = small.reshape(-1, 1024)[:, : own_small.shape[0]]
    lens = lax.dynamic_index_in_dim(
        small[:, -seqs:], lax.axis_index("z") * zs * cs, 0, keepdims=False
    ).astype(jnp.int32)
    g = norm1_gain.shape[0]
    gain_one = small[:, :g].reshape(1, -1).astype(F32)
    gain_two = small[:, g : 2 * g].reshape(1, -1).astype(F32)
    table = small[:, 2 * g : -seqs].reshape(1, -1).astype(F32).reshape(H, buckets_n)
    plane_index = lax.axis_index("fsdp") * cs + lax.axis_index("core")
    table = head_cols.split(jnp.repeat(table.T, head_dim, axis=1))[:, :, ::head_dim]
    table = lax.dynamic_index_in_dim(table, plane_index, 0, keepdims=False).T
    one_hot = (buckets[:, None] == jnp.arange(buckets_n, dtype=jnp.int32)[None, :]).astype(F32)
    one_hot = jnp.pad(one_hot, ((0, 1), (0, 0)))
    offset_bias = jnp.dot(table, one_hot.T, precision=HIGHEST)

    ff = w_d.shape[0]

    positions = plane_index * block_len + jnp.arange(block_len, dtype=jnp.int32)
    valid = (positions[None, :] < lens[:, None]).astype(F32).reshape(rows, 1)

    x = x_in.reshape(rows, width).astype(F32)
    scale_one = rms_scale(x)
    grad_rows = cot.reshape(rows, width).astype(F32) * valid

    normed = (x * scale_one * gain_one).astype(BF)
    normed, qkv = plane_gather_dot(normed, w_qkv, NN, seqs, 2)
    branch = grad_rows.astype(BF)
    attended, lse, grad_branch = attn_fwd(
        qkv, offset_bias, lens, heads, head_dim, seqs, branch, 1
    )
    hidden_one, normed_two = plane_dot_scatter(
        attended, w_o, NN, seqs, 3, norm=(x_in, gain_two)
    )
    normed_two, grad_hidden = plane_gather_dot(
        normed_two, w_d, NT, seqs, 4, other=grad_branch, dtype=F32
    )
    hidden_ff, grad_gu, grad_w_down = ffn(normed_two, grad_hidden, grad_branch, w_gu)
    sum_down = ff_cols.scatter(grad_w_down)
    last = (hidden_one, valid)
    if fs <= 4:
        result, grad_w_gu = plane_dot_scatter(
            hidden_ff, w_d, NN, seqs, 7, beside=(normed_two, grad_gu), result=last
        )
    else:
        result = plane_dot_scatter(hidden_ff, w_d, NN, seqs, 7, result=last)
        grad_w_gu = jnp.einsum("rd,rf->df", normed_two, grad_gu, preferred_element_type=F32)
        grad_w_gu = grad_w_gu.astype(BF)
    grad_w_gu, sum_down, grad_gu = lax.optimization_barrier((grad_w_gu, sum_down, grad_gu))
    sum_gu = reduce_z(grad_w_gu)
    if fs <= 4:
        grad_attended, grad_w_o, grad_hidden_one, gain_two_part = norm_turn(
            grad_gu, w_gu, hidden_one, branch, gain_two, w_o, attended, seqs, 5
        )
    else:
        grad_normed_two = plane_dot_scatter(grad_gu, w_gu, NT, seqs, 5)
        scale_two = rms_scale(hidden_one)
        gain_two_part = jnp.sum(grad_normed_two * hidden_one * scale_two, axis=0)
        grad_hidden_one = grad_rows + norm_back(grad_normed_two, hidden_one, scale_two, gain_two)
        grad_attn, grad_attended = plane_gather_dot(
            grad_hidden_one.astype(BF), w_o, NT, seqs, 6
        )
        grad_w_o = jnp.einsum("rk,rd->kd", attended, grad_attn, preferred_element_type=F32)
        grad_w_o = grad_w_o.astype(BF)
    dq, dk, dv, grad_offset, output, sum_o, got_gu = attn_bwd(
        qkv, grad_attended, lse, offset_bias, lens, heads, head_dim, seqs,
        swapped=result, column=head_cols.whole(grad_w_o), spread=sum_gu, collective_id=11,
    )
    output = output.reshape(seqs, block_len, width)
    dqkv = jnp.concatenate([dq, dk, dv], axis=1)
    grad_w_qkv = jnp.einsum("rd,rk->dk", normed, dqkv, preferred_element_type=F32)
    grad_w_qkv, dqkv = lax.optimization_barrier((grad_w_qkv.astype(BF), dqkv))
    grad_w_qkv, sum_gu = lax.optimization_barrier((grad_w_qkv, sum_gu))
    sum_qkv = reduce_z(grad_w_qkv)
    grad_normed = plane_dot_scatter(dqkv, w_qkv, NT, seqs, 8)
    gain_one_part = jnp.sum(grad_normed * x * scale_one, axis=0)
    grad_x = grad_hidden_one + norm_back(grad_normed, x, scale_one, gain_one)

    grad_table = jnp.dot(grad_offset, one_hot, precision=HIGHEST)
    bias_all = jnp.zeros((fs * cs, heads, buckets_n), F32)
    bias_all = lax.dynamic_update_index_in_dim(bias_all, grad_table, plane_index, 0)
    bias_all = jnp.repeat(bias_all.transpose(0, 2, 1), head_dim, axis=2)
    bias_all = head_cols.join(bias_all)[:, ::head_dim].T.reshape(fs * zs * cs, -1)
    small_grad = jnp.concatenate(
        [
            gain_one_part.reshape(fs * zs * cs, -1),
            gain_two_part.reshape(fs * zs * cs, -1),
            bias_all,
        ],
        axis=1,
    )
    columns = (w_gate.shape[1],) * 2 + (w_query.shape[1],) * 3
    small_sum, grad_tokens, grad_gate_w, grad_up_w, grad_q_w, grad_k_w, grad_v_w = finish(
        to_tiles(small_grad), grad_x.astype(BF), sum_qkv, got_gu, runs, columns, 10
    )
    grad_tokens = grad_tokens.reshape(seqs, block_len, width)
    small_grad = small_sum.reshape(-1)[: small_grad.shape[1]]
    return (
        output,
        grad_tokens,
        small_grad[:g],
        small_grad[2 * g :],
        grad_q_w,
        grad_k_w,
        grad_v_w,
        sum_o,
        small_grad[g : 2 * g],
        grad_gate_w,
        grad_up_w,
        sum_down.astype(F32),
    )


def solution(mesh):
    fs, ctx = mesh.shape["fsdp"], mesh.shape["ctx"]
    mesh3 = Mesh(mesh.devices.reshape(fs, ctx // 2, 2), ALL)
    act = P("fsdp", ("z", "core"), None)
    vec, mat = P(ALL), P(ALL, None)
    in_specs = (act, act, P("fsdp"), P(), vec, vec, mat, mat, mat, mat, vec, mat, mat, mat)
    out_specs = (act, act, vec, vec, mat, mat, mat, mat, vec, mat, mat, mat)
    return jax.shard_map(shards, mesh=mesh3, in_specs=in_specs, out_specs=out_specs, check_vma=False)
```

```python
import functools, math
import jax, jax.numpy as jnp
from jax import lax
from jax.experimental import pallas as pl
from jax.experimental.pallas import tpu as pltpu

MASKED = -1e30
EPSILON = 1e-06
NT = (((1,), (1,)), ((), ()))
NN = (((1,), (0,)), ((), ()))


def dotf(a, b, dims=NN):
    return lax.dot_general(a, b, dims, preferred_element_type=jnp.float32)


def head_mask(width, head_dim, h):
    lane = lax.broadcasted_iota(jnp.int32, (1, width), 1)
    return (lane // head_dim == h).astype(jnp.float32).astype(jnp.bfloat16)


def fill_skew(bias_ref, skew_ref, heads, block, length):
    for h in range(heads):
        rows = jnp.broadcast_to(bias_ref[h : h + 1, :], (block, 2 * length))
        rolled = pltpu.roll(rows, 2 * length - (block - 1), 1, stride=1, stride_axis=0)
        skew_ref[h] = rolled[:, : 2 * length - block]


def attn_fwd_kernel(
    heads, head_dim, block, length, seqs, fs, lens_ref, q_ref, k_ref, v_ref, bias_ref, x_ref,
    out_ref, lse_ref, full_ref, skew_ref, kt_ref, *sems
):
    seq, blk = pl.program_id(0), pl.program_id(1)
    blocks = length // block
    grid_step = seq * blocks + blk
    steps = seqs * blocks
    width = heads * head_dim
    plane = Plane(fs)
    actions = gather_actions(plane, x_ref, full_ref, sems[:4], sems[4])

    @pl.when(grid_step == 0)
    def _():
        plane.barrier()
        actions[0]()

    @pl.when(grid_step == steps // 2)
    def _():
        actions[1]()

    @pl.when(grid_step == 0)
    def _():
        fill_skew(bias_ref, skew_ref, heads, block, length)

    @pl.when(blk == 0)
    def _():
        kt_ref[...] = k_ref[...].T

    valid_len = lens_ref[seq]
    key_pos = lax.broadcasted_iota(jnp.int32, (1, length), 1)
    key_mask = jnp.where(key_pos < valid_len, 0.0, MASKED)
    start = pl.multiple_of(length - block - blk * block, block)
    lane = lax.broadcasted_iota(jnp.int32, (block, 128), 1)
    out = jnp.zeros((block, width), jnp.float32)
    lse_all = jnp.zeros((block, 128), jnp.float32)
    for h in range(heads):
        mask = head_mask(width, head_dim, h)
        scores = dotf(q_ref[...] * mask, kt_ref[...])
        scores = scores + skew_ref[h, :, pl.ds(start, length)] + key_mask
        peak = jnp.max(scores, axis=1, keepdims=True)
        probs = jnp.exp(scores - peak)
        mass = jnp.sum(probs, axis=1, keepdims=True)
        probs = (probs * (1.0 / mass)).astype(jnp.bfloat16)
        out = out + dotf(probs, v_ref[...] * mask)
        lse_all = jnp.where(lane == h, peak + jnp.log(mass), lse_all)
    out_ref[...] = out.astype(jnp.bfloat16)
    lse_ref[...] = lse_all

    @pl.when(grid_step == steps - 1)
    def _():
        for action in actions[2:]:
            action()


def attn_fwd(qkv, offset_bias, lens, heads, head_dim, seqs, gathered, collective_id, block=256):
    rows, width3 = qkv.shape
    width = width3 // 3
    length = rows // seqs
    block = min(block, length)
    blocks = length // block
    fs = lax.axis_size("fsdp")
    wide = gathered.shape[1]
    gathered = gathered.reshape(seqs, -1, wide)
    b = gathered.shape[1]
    attended, lse, full = pl.pallas_call(
        functools.partial(attn_fwd_kernel, heads, head_dim, block, length, seqs, fs),
        grid=(seqs, blocks),
        in_specs=[
            pl.BlockSpec(memory_space=pltpu.SMEM),
            pl.BlockSpec((block, width), lambda s, i: (s * blocks + i, 0)),
            pl.BlockSpec((length, width), lambda s, i: (s, 1)),
            pl.BlockSpec((length, width), lambda s, i: (s, 2)),
            pl.BlockSpec((heads, 2 * length), lambda s, i: (0, 0)),
            vmem(),
        ],
        out_specs=[
            pl.BlockSpec((block, width), lambda s, i: (s * blocks + i, 0)),
            pl.BlockSpec((block, 128), lambda s, i: (s * blocks + i, 0)),
            anywhere(),
        ],
        scratch_shapes=[
            pltpu.VMEM((heads, block, 2 * length - block), jnp.float32),
            pltpu.VMEM((width, length), jnp.bfloat16),
        ]
        + gather_sems(fs)
        + [pltpu.SemaphoreType.DMA],
        out_shape=[
            jax.ShapeDtypeStruct((rows, width), jnp.bfloat16),
            jax.ShapeDtypeStruct((rows, 128), jnp.float32),
            jax.ShapeDtypeStruct((seqs, 2 * fs, b, wide), gathered.dtype),
        ],
        compiler_params=pltpu.CompilerParams(
            dimension_semantics=("arbitrary", "arbitrary"), vmem_limit_bytes=56 * 1024 * 1024,
            collective_id=collective_id, has_side_effects=True,
        ),
        cost_estimate=estimate(26),
        name="attn_fwd",
    )(lens, qkv, qkv, qkv, offset_bias, gathered)
    return attended, lse, full.reshape(-1, wide)


def attn_bwd_kernel(
    heads, head_dim, block, length, seqs, fs, lens_ref, q_ref, k_ref, v_ref, g_ref, lse_ref,
    bias_ref, *refs,
):
    seq, blk = pl.program_id(0), pl.program_id(1)
    blocks = length // block
    last_seq, last_blk = seqs - 1, blocks - 1
    grid_step = seq * blocks + blk
    steps = seqs * blocks
    x_ref, wg_ref, gu_ref, n_hbm, dqkv_ref, dbias_ref, dw_ref = refs[:7]
    out_ref, sum_ref, got_ref = refs[7:10]
    refs = refs[10:]
    n_ref, n_sem, dw_acc = refs[6:9]
    refs = refs[:6] + refs[9:]
    column = Column(wg_ref, sum_ref, refs[6:9])
    back = Back((fs, 1, 2), gu_ref, got_ref, refs[9:12])
    swap = Swap(x_ref, out_ref, refs[12:])

    def begin():
        plane_and_column_greet()
        swap.start()
        column.start()
        back.start()

    todo = {0: begin, steps // 2: swap.hand_on}
    for step, action in todo.items():
        pl.when(grid_step == step)(action)
    skew_ref, kt_ref, vt_ref, acc_ref, dkt_ref, dvt_ref = refs[:6]
    width = heads * head_dim

    @pl.when((seq == 0) & (blk == 0))
    def _():
        fill_skew(bias_ref, skew_ref, heads, block, length)
        acc_ref[...] = jnp.zeros_like(acc_ref)
        dw_acc[...] = jnp.zeros_like(dw_acc)

    rows = pl.ds(pl.multiple_of(seq * length, length), length)
    load = pltpu.make_async_copy(n_hbm.at[rows], n_ref, n_sem)

    @pl.when(blk == 0)
    def _():
        load.start()
        kt_ref[...] = k_ref[...].T
        vt_ref[...] = v_ref[...].T
        dkt_ref[...] = jnp.zeros_like(dkt_ref)
        dvt_ref[...] = jnp.zeros_like(dvt_ref)

    valid_len = lens_ref[seq]
    key_pos = lax.broadcasted_iota(jnp.int32, (1, length), 1)
    key_mask = jnp.where(key_pos < valid_len, 0.0, MASKED)
    start = pl.multiple_of(length - block - blk * block, block)
    q_t = q_ref[...].T
    g_t = g_ref[...].T
    dq = jnp.zeros((block, width), jnp.float32)
    row = lax.broadcasted_iota(jnp.int32, (width, 1), 0)
    for h in range(heads):
        mask = head_mask(width, head_dim, h)
        rmask = (row // head_dim == h).astype(jnp.float32).astype(jnp.bfloat16)
        scores = dotf(q_ref[...] * mask, kt_ref[...])
        scores = scores + skew_ref[h, :, pl.ds(start, length)] + key_mask
        probs = jnp.exp(scores - lse_ref[:, h : h + 1])
        grad_probs = dotf(g_ref[...] * mask, vt_ref[...])
        delta = jnp.sum(probs * grad_probs, axis=1, keepdims=True)
        ds = (probs * (grad_probs - delta)).astype(jnp.bfloat16)
        dq = dq + dotf(ds, k_ref[...] * mask)
        acc_ref[h, :, pl.ds(start, length)] += ds.astype(jnp.float32)
        dkt_ref[...] += dotf(q_t * rmask, ds)
        dvt_ref[...] += dotf(g_t * rmask, probs.astype(jnp.bfloat16))
    here = pl.ds(pl.multiple_of(blk * block, block), block)
    dqkv_ref[here, :width] = dq.astype(jnp.bfloat16)

    @pl.when(blk == last_blk)
    def _():
        dqkv_ref[:, width : 2 * width] = dkt_ref[...].astype(jnp.bfloat16).T
        dqkv_ref[:, 2 * width :] = dvt_ref[...].astype(jnp.bfloat16).T
        load.wait()

        def weight(i, carry):
            cols = pl.ds(pl.multiple_of(i * 256, 256), 256)
            part = dw_acc[cols, :] + dotf(n_ref[:, cols].T, dqkv_ref[...])
            dw_acc[cols, :] = part
            dw_ref[cols, :] = part.astype(jnp.bfloat16)
            return carry

        lax.fori_loop(0, n_ref.shape[1] // 256, weight, 0)

    @pl.when((seq == last_seq) & (blk == last_blk))
    def _():
        for h in range(heads):
            part = jnp.concatenate(
                [acc_ref[h], jnp.zeros((block, block), jnp.float32)], axis=1
            )
            n = block
            while n > 8:
                n //= 2
                part = pltpu.roll(part[:n], n, 1) + part[n:]
            total = jnp.zeros((1, 2 * length), jnp.float32)
            for i in range(n):
                total = total + (pltpu.roll(part, n - 1 - i, 1) if i < n - 1 else part)[i : i + 1]
            dbias_ref[h : h + 1, :] = total

    @pl.when(grid_step == steps - 1)
    def _():
        column.close()
        back.arrived()
        back.close()
        swap.close()


def attn_bwd(
    qkv, grad, lse, offset_bias, lens, heads, head_dim, seqs, normed, swapped, column, spread,
    collective_id, block=256,
):
    rows, width3 = qkv.shape
    width = width3 // 3
    length = rows // seqs
    block = min(block, length)
    blocks = length // block
    fs, zs = lax.axis_size("fsdp"), lax.axis_size("z")
    column = column.reshape(zs, -1, column.shape[1])
    spread = spread.reshape(2 * fs, -1, spread.shape[2])
    wide = normed.shape[1]
    return pl.pallas_call(
        functools.partial(attn_bwd_kernel, heads, head_dim, block, length, seqs, fs),
        grid=(seqs, blocks),
        in_specs=[
            pl.BlockSpec(memory_space=pltpu.SMEM),
            pl.BlockSpec((block, width), lambda s, i: (s * blocks + i, 0)),
            pl.BlockSpec((length, width), lambda s, i: (s, 1)),
            pl.BlockSpec((length, width), lambda s, i: (s, 2)),
            pl.BlockSpec((block, width), lambda s, i: (s * blocks + i, 0)),
            pl.BlockSpec((block, 128), lambda s, i: (s * blocks + i, 0)),
            pl.BlockSpec((heads, 2 * length), lambda s, i: (0, 0)),
        ]
        + [vmem()] * 3
        + [anywhere()],
        out_specs=[
            pl.BlockSpec((length, width3), lambda s, i: (s, 0)),
            pl.BlockSpec((heads, 2 * length), lambda s, i: (0, 0)),
            vmem(), anywhere(), vmem(), anywhere(),
        ],
        out_shape=[
            jax.ShapeDtypeStruct((rows, width3), jnp.bfloat16),
            jax.ShapeDtypeStruct((heads, 2 * length), jnp.float32),
            jax.ShapeDtypeStruct((wide, width3), jnp.bfloat16),
            jax.ShapeDtypeStruct(swapped.shape, swapped.dtype),
            jax.ShapeDtypeStruct(column.shape[1:], jnp.float32),
            jax.ShapeDtypeStruct(spread.shape, spread.dtype),
        ],
        scratch_shapes=[
            pltpu.VMEM((heads, block, 2 * length - block), jnp.float32),
            pltpu.VMEM((width, length), jnp.bfloat16),
            pltpu.VMEM((width, length), jnp.bfloat16),
            pltpu.VMEM((heads, block, 2 * length - block), jnp.float32),
            pltpu.VMEM((width, length), jnp.float32),
            pltpu.VMEM((width, length), jnp.float32),
            pltpu.VMEM((length, wide), jnp.bfloat16),
            pltpu.SemaphoreType.DMA,
            pltpu.VMEM((wide, width3), jnp.float32),
        ]
        + Column.scratch(column)
        + Back.scratch(2 * fs)
        + Swap.scratch(fs, *swapped.shape),
        compiler_params=pltpu.CompilerParams(
            dimension_semantics=("arbitrary", "arbitrary"), vmem_limit_bytes=62 * 1024 * 1024,
            collective_id=collective_id, has_side_effects=True,
        ),
        cost_estimate=estimate(50),
        name="attn_bwd",
    )(lens, qkv, qkv, qkv, grad, lse, offset_bias, swapped, column, spread, normed)

MESH_ID = pl.DeviceIdType.MESH
MIB = 1024 * 1024


def remote_copy(src, dst, send_sem, recv_sem, device):
    return pltpu.make_async_remote_copy(
        src_ref=src, dst_ref=dst, send_sem=send_sem, recv_sem=recv_sem, device_id=device,
        device_id_type=MESH_ID,
    )


def landed(ref, sem):
    pltpu.make_async_copy(ref, ref, sem).wait()


def wide_tile(width):
    return math.gcd(width // 2, 1024)


def estimate(us):
    return pl.CostEstimate(flops=int(us * 0.02 * 1.1e9), bytes_accessed=int(us * 1e5), transcendentals=0)


def flip(f, bits):
    k = 1
    while k <= bits:
        if bits & k:
            f = f + (1 - 2 * (lax.rem(lax.div(f, k), 2))) * k
        k *= 2
    return f


class Plane:
    def __init__(self, fs):
        self.fs = fs
        self.f, self.z, self.c = (lax.axis_index(a) for a in ("fsdp", "z", "core"))
        self.bits = [1 << i for i in range(fs.bit_length() - 1)]
        self.orders = [self.bits, self.bits[::-1]]
        self.steps = len(self.bits)

    def peer(self, bit):
        return (flip(self.f, bit), self.z, self.c)

    def mate(self):
        return (self.f, self.z, 1 - self.c)

    def slot(self, rel, other=False):
        c = 1 - self.c if other else self.c
        return flip(self.f, rel) * 2 + c

    def barrier(self, more=0):
        bar = pltpu.get_barrier_semaphore()
        for dev in [self.mate()] + [self.peer(b) for b in self.bits]:
            pl.semaphore_signal(bar, inc=1, device_id=dev, device_id_type=MESH_ID)
        pl.semaphore_wait(bar, 1 + self.steps + more)


def gather_sems(fs):
    steps = fs.bit_length() - 1
    return [
        pltpu.SemaphoreType.DMA((2, steps, fs)),
        pltpu.SemaphoreType.DMA((2, fs)),
        pltpu.SemaphoreType.DMA((2, fs)),
        pltpu.SemaphoreType.DMA((2, fs)),
    ]


def run_gather(plane, x_ref, buf_ref, sems, consume):
    send, recv, mate_send, mate_recv = sems
    started = []

    def remote(*args):
        copy = remote_copy(*args)
        copy.start()
        started.append(copy)
        return copy

    def source(p, rel):
        return x_ref.at[p] if rel == 0 else buf_ref.at[p, plane.slot(rel)]

    def to_mate(p, rel):
        remote(
            source(p, rel), buf_ref.at[p, plane.slot(rel)], mate_send.at[p, rel],
            mate_recv.at[p, rel], plane.mate(),
        )

    def to_peer(p, step, rel):
        bit = plane.orders[p][step]
        return remote(
            source(p, rel), buf_ref.at[p, plane.slot(rel)], send.at[p, step, rel],
            recv.at[p, rel ^ bit], plane.peer(bit),
        )

    def finish(pairs):
        for p, rel in pairs:
            landed(buf_ref.at[p, plane.slot(rel, True)], mate_recv.at[p, rel])
            if consume is not None:
                consume(p, flip(plane.f, rel) * 2)

    first = [to_peer(p, 0, 0) for p in range(2)]
    for p in range(2):
        to_mate(p, 0)
    if consume is not None:
        for p in range(2):
            buf_ref[p, plane.slot(0)] = x_ref[p]
    have = [[0], [0]]
    pending = [(0, 0), (1, 0)]
    for step in range(plane.steps):
        for i in range(len(have[0])):
            finish(pending)
            if i == 0 and step + 1 < plane.steps:
                for copy in first:
                    copy.wait_send()
                    started[:] = [other for other in started if other is not copy]
                first = [to_peer(p, step + 1, 0) for p in range(2)]
            pending = [(p, have[p][i] ^ plane.orders[p][step]) for p in range(2)]
            for p, rel in pending:
                landed(buf_ref.at[p, plane.slot(rel)], recv.at[p, rel])
                to_mate(p, rel)
                for later in range(step + 1, plane.steps):
                    to_peer(p, later, rel)
        for p in range(2):
            have[p] = have[p] + [rel ^ plane.orders[p][step] for rel in have[p]]
    finish(pending)
    for copy in started:
        copy.wait_send()


def gather_actions(plane, x_ref, out_ref, sems, own_sem):
    send, recv, mate_send, mate_recv = sems

    def source(p, rel):
        return x_ref.at[p] if rel == 0 else out_ref.at[p, plane.slot(rel)]

    def to_mate(p, rel):
        return remote_copy(
            source(p, rel), out_ref.at[p, plane.slot(rel)], mate_send.at[p, rel],
            mate_recv.at[p, rel], plane.mate(),
        )

    def to_peer(p, step, rel):
        bit = plane.orders[p][step]
        return remote_copy(
            source(p, rel), out_ref.at[p, plane.slot(rel)], send.at[p, step, rel],
            recv.at[p, rel ^ bit], plane.peer(bit),
        )

    def own():
        return pltpu.make_async_copy(x_ref, out_ref.at[:, plane.slot(0)], own_sem)

    held = [[[0]], [[0]]]
    for step in range(plane.steps):
        for p in range(2):
            bit = plane.orders[p][step]
            held[p].append(held[p][-1] + [rel ^ bit for rel in held[p][-1]])

    def begin():
        for p in range(2):
            to_peer(p, 0, 0).start()
        for p in range(2):
            to_mate(p, 0).start()
        own().start()

    def group(step, i):
        if i == 0 and step + 1 < plane.steps:
            for p in range(2):
                to_peer(p, step, 0).wait_send()
                to_peer(p, step + 1, 0).start()
        for p in range(2):
            rel = held[p][step][i] ^ plane.orders[p][step]
            landed(out_ref.at[p, plane.slot(rel)], recv.at[p, rel])
            to_mate(p, rel).start()
            for later in range(step + 1, plane.steps):
                to_peer(p, later, rel).start()

    def close():
        for p in range(2):
            for rel in range(plane.fs):
                landed(out_ref.at[p, plane.slot(rel, True)], mate_recv.at[p, rel])
                to_mate(p, rel).wait_send()
            for step in range(plane.steps):
                for rel in held[p][step]:
                    if rel or step + 1 == plane.steps:
                        to_peer(p, step, rel).wait_send()
        own().wait()

    groups = [
        functools.partial(group, step, i)
        for step in range(plane.steps) for i in range(2**step)
    ]
    return [begin] + groups + [close]


class Line:
    def __init__(self, x_ref, out_ref, scratch):
        self.x_ref, self.out_ref = x_ref, out_ref
        self.send, self.recv, self.own_sem = scratch
        self.f, self.z, self.c = (lax.axis_index(a) for a in ("fsdp", "z", "core"))
        self.zs = out_ref.shape[0]

    @staticmethod
    def scratch(zs):
        dma = pltpu.SemaphoreType.DMA
        return [dma((2, zs)), dma((2, zs)), dma]

    def greet(self):
        bar = pltpu.get_barrier_semaphore()
        for way in (1, -1):
            to = lax.rem(self.z + way + self.zs, self.zs)
            pl.semaphore_signal(
                bar, inc=1, device_id=(self.f, to, self.c), device_id_type=MESH_ID
            )

    def copy(self, step, way):
        source = lax.rem(self.z - way * step + self.zs, self.zs)
        to = lax.rem(self.z + way + self.zs, self.zs)
        k = 0 if way > 0 else 1
        ref = self.out_ref.at[source]
        return remote_copy(
            ref if step else self.x_ref, ref, self.send.at[k, step], self.recv.at[k, step],
            (self.f, to, self.c),
        )

    def sends(self, step, way):
        if way > 0:
            return (self.z >= step) & (self.z < self.zs - 1)
        return (self.z < self.zs - step) & (self.z > 0)

    def arrived(self, step, way):
        k = 0 if way > 0 else 1
        source = lax.rem(self.z - way * (step + 1) + self.zs, self.zs)
        here = (self.z > step) if way > 0 else (self.z < self.zs - 1 - step)

        @pl.when(here)
        def _():
            landed(self.out_ref.at[source], self.recv.at[k, step])

    def own(self):
        return pltpu.make_async_copy(self.x_ref, self.out_ref.at[self.z], self.own_sem)

    def go(self, step):
        if step == 0:
            self.own().start()
        for way in (1, -1):
            if step:
                self.arrived(step - 1, way)
            if step < self.zs - 1:

                @pl.when(self.sends(step, way))
                def _(way=way):
                    self.copy(step, way).start()

    def close(self):
        self.own().wait()
        for step in range(self.zs - 1):
            for way in (1, -1):

                @pl.when(self.sends(step, way))
                def _(step=step, way=way):
                    self.copy(step, way).wait_send()


def scatter_scratch(fs, b, width):
    return [
        pltpu.VMEM((2, fs, b, width), jnp.bfloat16),
        pltpu.VMEM((2, fs, b, width), jnp.bfloat16),
        pltpu.VMEM((2, fs // 2, b, width), jnp.float32),
        pltpu.VMEM((2, fs, b, width), jnp.bfloat16),
        pltpu.VMEM((2, fs - 1, b, width), jnp.bfloat16),
        pltpu.SemaphoreType.DMA((fs, 2)),
        pltpu.SemaphoreType.DMA((fs, 2)),
        pltpu.SemaphoreType.DMA((2, fs)),
        pltpu.SemaphoreType.DMA((2, fs - 1)),
    ]


def scatter_actions(plane, partial, width, out_ref, scratch):
    give, got, total, outbox, inbox, give_sem, got_sem, send, recv = scratch
    b = out_ref.shape[1]
    rels = sorted(range(plane.fs), key=lambda r: (-bin(r).count("1"), r))
    whole = slice(0, width)

    def pieces(rel):
        if rel == rels[0]:
            return [slice(0, width // 2), slice(width // 2, width)]
        return [whole]

    def leaves(p, rel):
        for step, bit in enumerate(plane.orders[p]):
            if rel & bit:
                return step
        return plane.steps

    def place(p, step, rel):
        kept = [r for r in range(plane.fs) if leaves(p, r) > step]
        return plane.fs - 2 * len(kept) + kept.index(rel)

    def held(p, rel):
        return [r for r in range(plane.fs) if leaves(p, r) > 0].index(rel)

    def to_peer(p, rel):
        step = leaves(p, rel)
        bit = plane.orders[p][step]
        at = place(p, step, rel ^ bit)
        return remote_copy(
            outbox.at[p, rel], inbox.at[p, at], send.at[p, rel], recv.at[p, at], plane.peer(bit)
        )

    def to_mate(rel, i):
        cols = pieces(rel)[i]
        return remote_copy(
            give.at[:, rel, :, cols], got.at[:, rel, :, cols], give_sem.at[rel, i],
            got_sem.at[rel, i], plane.mate(),
        )

    def give_part(rel):
        theirs = plane.slot(rel, True)

        def body(cols):
            part = partial(theirs, cols).astype(jnp.bfloat16)
            give[0, rel, :, cols] = part[:b]
            give[1, rel, :, cols] = part[b:]

        for i, cols in enumerate(pieces(rel)):
            body(cols)
            to_mate(rel, i).start()

    def own_part(rel):
        mine = plane.slot(rel)

        def body(cols):
            part = partial(mine, cols)
            for p in range(2):
                here = part[p * b : (p + 1) * b] + got[p, rel, :, cols].astype(jnp.float32)
                if leaves(p, rel) == 0:
                    outbox[p, rel, :, cols] = here.astype(jnp.bfloat16)
                else:
                    total[p, held(p, rel), :, cols] = here

        for i, cols in enumerate(pieces(rel)):
            landed(got.at[:, rel, :, cols], got_sem.at[rel, i])
            body(cols)
        for p in range(2):
            if leaves(p, rel) == 0:
                to_peer(p, rel).start()

    def add_part(step, rel, p):
        at = place(p, step, rel)
        landed(inbox.at[p, at], recv.at[p, at])
        sends = leaves(p, rel) == step + 1

        def body(cols):
            here = total[p, held(p, rel), :, cols] + inbox[p, at, :, cols].astype(jnp.float32)
            if step + 1 == plane.steps:
                out_ref[p, :, cols] = here
            elif sends:
                outbox[p, rel, :, cols] = here.astype(jnp.bfloat16)
            else:
                total[p, held(p, rel), :, cols] = here

        body(whole)
        if sends and step + 1 < plane.steps:
            to_peer(p, rel).start()

    def close():
        for rel in rels:
            for i in range(len(pieces(rel))):
                to_mate(rel, i).wait_send()
            for p in range(2):
                if leaves(p, rel) < plane.steps:
                    to_peer(p, rel).wait_send()

    order = [(give_part, rels[0]), (own_part, rels[0]), (give_part, rels[1])]
    for i in range(2, len(rels)):
        order += [(give_part, rels[i]), (own_part, rels[i - 1])]
    order.append((own_part, rels[-1]))
    actions = [functools.partial(part, rel) for part, rel in order]
    for step in range(plane.steps):
        for rel in rels:
            for p in range(2):
                if leaves(p, rel) > step:
                    actions.append(functools.partial(add_part, step, rel, p))
    return actions + [close]


def vmem():
    return pl.BlockSpec(memory_space=pltpu.VMEM)


def anywhere():
    return pl.BlockSpec(memory_space=pl.ANY)


def plane_params(collective_id, limit=58):
    return pltpu.CompilerParams(
        collective_id=collective_id, has_side_effects=True, vmem_limit_bytes=limit * MIB
    )


class Staged:
    def __init__(self, refs, scratch):
        self.held = scratch[: len(refs)]
        self.loads = [
            pltpu.make_async_copy(ref, held, sem)
            for ref, held, sem in zip(refs, self.held, scratch[len(refs) :])
        ]
        for load in self.loads:
            load.start()

    @staticmethod
    def scratch(*arrays):
        dma = pltpu.SemaphoreType.DMA
        return [pltpu.VMEM(x.shape, x.dtype) for x in arrays] + [dma] * len(arrays)

    def wait(self):
        for load in self.loads:
            load.wait()


def gather_dot_kernel(fs, dims, tile, other, line, x_ref, *refs):
    count = 2 if other else 1
    hbm, refs = refs[:count], refs[count:]
    if line:
        l_ref, refs = refs[0], refs[1:]
    full_ref, y_ref, refs = refs[0], refs[1], refs[2:]
    if line:
        line, refs = Line(l_ref, refs[0], refs[1:4]), refs[4:]
    staged = Staged(hbm, refs[: 2 * count])
    buf_ref, sems = refs[2 * count], refs[2 * count + 1 :]
    plane = Plane(fs)
    if line:
        line.greet()
    plane.barrier(2 if line else 0)
    if line:
        line.go(0)
    w_ref = staged.held[0]
    a_ref = staged.held[1] if other else buf_ref
    keep_sem = sems[4]
    b, width = buf_ref.shape[2:]
    columns = y_ref.shape[3]
    kept = []

    def consume(p, slot):
        two = pl.ds(slot, 2)
        cp = pltpu.make_async_copy(
            buf_ref.at[p, two], full_ref.at[p, two], keep_sem.at[len(kept)]
        )
        cp.start()
        if not kept:
            staged.wait()
        kept.append(cp)

        def product(cols):
            w = w_ref[:, cols] if dims == NN else w_ref[cols, :]
            y = dotf(a_ref[p, two].reshape(2 * b, -1), w, dims)
            y_ref[p, two, :, cols] = y.astype(y_ref.dtype).reshape(2, b, tile)

        def one(j, carry):
            product(pl.ds(pl.multiple_of(j * tile, tile), tile))
            return carry

        if tile == columns:
            product(slice(None))
        else:
            lax.fori_loop(0, columns // tile, one, 0)
        if line and len(kept) % 2 == 0 and len(kept) // 2 < line.zs:
            line.go(len(kept) // 2)

    run_gather(plane, x_ref, buf_ref, sems[:4], consume)
    if line:
        for step in range(len(kept) // 2 + 1, line.zs):
            line.go(step)
        line.close()
    for cp in kept:
        cp.wait()


def plane_gather_dot(
    x, w, dims, seqs, collective_id, other=None, line=None, dtype=jnp.bfloat16
):
    fs, zs = lax.axis_size("fsdp"), lax.axis_size("z")
    x = x.reshape(seqs, -1, x.shape[1])
    _, b, width = x.shape
    columns = w.shape[1] if dims == NN else w.shape[0]
    tile = next((t for t in (1024, 768, 256, 128) if columns % t == 0), columns)
    lead = (seqs, 2 * fs, b)
    staged = [w] if other is None else [w, other.reshape(lead + (-1,))]
    out_shape = [
        jax.ShapeDtypeStruct(lead + (width,), x.dtype),
        jax.ShapeDtypeStruct(lead + (columns,), dtype),
    ]
    args, scratch = [x] + staged, []
    in_specs, out_specs = [vmem()] + [anywhere()] * len(staged), [anywhere(), vmem()]
    if line is not None:
        args.append(line)
        in_specs.append(vmem())
        out_shape.append(jax.ShapeDtypeStruct((zs,) + line.shape, line.dtype))
        out_specs.append(anywhere())
        scratch += Line.scratch(zs)
    out = pl.pallas_call(
        functools.partial(gather_dot_kernel, fs, dims, tile, other is not None, line is not None),
        out_shape=out_shape,
        in_specs=in_specs,
        out_specs=out_specs,
        scratch_shapes=scratch
        + Staged.scratch(*staged)
        + [pltpu.VMEM(lead + (width,), x.dtype)]
        + gather_sems(fs)
        + [pltpu.SemaphoreType.DMA((seqs * fs,))],
        compiler_params=plane_params(collective_id),
        cost_estimate=estimate(45),
        name="plane_gather_dot",
    )(*args)
    return (out[0].reshape(-1, width), out[1].reshape(-1, columns)) + tuple(out[2:])


class Swap:
    def __init__(self, x_ref, out_ref, scratch):
        self.x_ref, self.out_ref = x_ref, out_ref
        self.relay, self.own_sem, self.in_send, self.in_recv, self.on_send, self.on_recv = scratch
        self.f, self.z, self.c = (lax.axis_index(a) for a in ("fsdp", "z", "core"))
        self.fs, self.size = self.relay.shape[:2]

    @staticmethod
    def scratch(fs, rows, width):
        dma = pltpu.SemaphoreType.DMA
        return [
            pltpu.VMEM((fs, rows // fs, width), jnp.bfloat16), dma,
            dma((fs,)), dma((fs,)), dma((fs,)), dma((fs,)),
        ]

    def column(self, d):
        return lax.rem(self.f + d, self.fs)

    def part(self, ref, k):
        return ref.at[pl.ds(pl.multiple_of(k * self.size, self.size), self.size)]

    def straight(self):
        return remote_copy(
            self.part(self.x_ref, self.f), self.part(self.out_ref, self.f), self.in_send.at[0],
            self.on_recv.at[self.f], (self.z, self.f, self.c),
        )

    def inward(self, d):
        k = self.column(d)
        return remote_copy(
            self.part(self.x_ref, k), self.relay.at[d], self.in_send.at[d],
            self.in_recv.at[d], (k, self.z, self.c),
        )

    def onward(self, d):
        source = self.column(self.fs - d)
        return remote_copy(
            self.relay.at[d], self.part(self.out_ref, self.f), self.on_send.at[d],
            self.on_recv.at[self.f], (self.z, source, self.c),
        )

    def own(self):
        return pltpu.make_async_copy(self.x_ref, self.out_ref, self.own_sem)

    def start_inward(self):
        @pl.when(self.f != self.z)
        def _():
            for d in range(1, self.fs):
                self.inward(d).start()

    def start_straight(self):
        @pl.when(self.f != self.z)
        def _():
            self.straight().start()

        @pl.when(self.f == self.z)
        def _():
            self.own().start()

    def start(self):
        self.start_inward()
        self.start_straight()

    def relayed(self, body):
        for d in range(1, self.fs):

            @pl.when(self.column(self.fs - d) != self.z)
            def _(d=d):
                body(d)

    def hand_on(self):
        def one(d):
            landed(self.relay.at[d], self.in_recv.at[d])
            self.onward(d).start()

        self.relayed(one)

    def close(self):
        self.relayed(lambda d: self.onward(d).wait_send())

        @pl.when(self.f == self.z)
        def _():
            self.own().wait()

        @pl.when(self.f != self.z)
        def _():
            self.straight().wait_send()
            for d in range(1, self.fs):
                self.inward(d).wait_send()
            for k in range(self.fs):
                landed(self.part(self.out_ref, k), self.on_recv.at[k])


def plane_and_column_greet():
    fs, zs, cs = (lax.axis_size(a) for a in ("fsdp", "z", "core"))
    f, z, c = (lax.axis_index(a) for a in ("fsdp", "z", "core"))
    bar = pltpu.get_barrier_semaphore()
    places = [(lax.rem(f + df, fs), z, lax.rem(c + dc, cs)) for df in range(fs) for dc in range(cs)]
    places = places[1:] + [(f, lax.rem(z + dz, zs), c) for dz in range(1, zs)]
    places += [
        (lax.rem(f + df, fs), lax.rem(z + dz, zs), c) for df in range(1, fs) for dz in range(1, zs)
    ]
    for place in places:
        pl.semaphore_signal(bar, inc=1, device_id=place, device_id_type=MESH_ID)
    pl.semaphore_wait(bar, len(places))


class Column:
    def __init__(self, x_ref, sum_ref, scratch):
        self.x_ref, self.sum_ref = x_ref, sum_ref
        self.inbox, self.send, self.recv = scratch
        self.f, self.z, self.c = (lax.axis_index(a) for a in ("fsdp", "z", "core"))
        self.zs = x_ref.shape[0]

    @staticmethod
    def scratch(x):
        dma = pltpu.SemaphoreType.DMA
        return [pltpu.VMEM(x.shape, x.dtype), dma((x.shape[0],)), dma((x.shape[0],))]

    def copy(self, d):
        to = lax.rem(self.z + d, self.zs)
        return remote_copy(
            self.x_ref.at[to], self.inbox.at[d], self.send.at[d], self.recv.at[d],
            (self.f, to, self.c),
        )

    def start(self):
        for d in range(1, self.zs):
            self.copy(d).start()

    def close(self):
        for d in range(1, self.zs):
            self.copy(d).wait_send()
            landed(self.inbox.at[d], self.recv.at[d])
        total = self.x_ref[self.z].astype(jnp.float32)
        for d in range(1, self.zs):
            total = total + self.inbox[d].astype(jnp.float32)
        self.sum_ref[...] = total


class Back:
    def __init__(self, sizes, src_ref, got_ref, scratch):
        fs, zs, self.cs = sizes
        self.src_ref, self.got_ref = src_ref, got_ref
        self.send, self.recv, self.own_sem = scratch
        self.z = lax.axis_index("z")
        self.devices = fs * self.cs
        self.me = lax.axis_index("fsdp") * self.cs + lax.axis_index("core")

    @staticmethod
    def scratch(devices):
        dma = pltpu.SemaphoreType.DMA
        return [dma((devices,)), dma((devices,)), dma]

    def copy(self, d):
        to = lax.rem(self.me + d, self.devices)
        return remote_copy(
            self.src_ref.at[to], self.got_ref.at[self.me], self.send.at[d], self.recv.at[d],
            (lax.div(to, self.cs), self.z, lax.rem(to, self.cs)),
        )

    def own(self):
        return pltpu.make_async_copy(
            self.src_ref.at[self.me], self.got_ref.at[self.me], self.own_sem
        )

    def start(self):
        for d in range(1, self.devices):
            self.copy(d).start()
        self.own().start()

    def arrived(self):
        for d in range(1, self.devices):
            at = lax.rem(self.me + self.devices - d, self.devices)
            landed(self.got_ref.at[at], self.recv.at[d])
        self.own().wait()

    def close(self):
        for d in range(1, self.devices):
            self.copy(d).wait_send()


class Everyone:
    def __init__(self, sizes):
        self.fs, self.zs, self.cs = sizes
        self.n = math.prod(sizes)
        f, z, c = (lax.axis_index(a) for a in ("fsdp", "z", "core"))
        self.me = (f * self.zs + z) * self.cs + c

    def place(self, d):
        f, z, c = (lax.axis_index(a) for a in ("fsdp", "z", "core"))
        df, dz, dc = d // (self.zs * self.cs), d // self.cs % self.zs, d % self.cs
        return (lax.rem(f + df, self.fs), lax.rem(z + dz, self.zs), lax.rem(c + dc, self.cs))

    def index(self, place):
        return (place[0] * self.zs + place[1]) * self.cs + place[2]

    def back(self, d):
        f, z, c = (lax.axis_index(a) for a in ("fsdp", "z", "core"))
        df, dz, dc = d // (self.zs * self.cs), d // self.cs % self.zs, d % self.cs
        return self.index((
            lax.rem(f + self.fs - df, self.fs), lax.rem(z + self.zs - dz, self.zs),
            lax.rem(c + self.cs - dc, self.cs),
        ))

    def greet(self):
        bar = pltpu.get_barrier_semaphore()
        for d in range(1, self.n):
            pl.semaphore_signal(bar, inc=1, device_id=self.place(d), device_id_type=MESH_ID)

    def met(self):
        pl.semaphore_wait(pltpu.get_barrier_semaphore(), self.n - 1)

    def copy(self, d, x_ref, spread_out, slots, send, recv):
        to = self.place(d)
        src = x_ref.at[self.index(to)] if spread_out else x_ref.at[0]
        return remote_copy(src, slots.at[self.me], send.at[d], recv.at[d], to)

    def begin(self, x_ref, spread_out, slots, send, recv, own_sem):
        for d in range(1, self.n):
            self.copy(d, x_ref, spread_out, slots, send, recv).start()
        src = x_ref.at[self.me] if spread_out else x_ref.at[0]
        own = pltpu.make_async_copy(src, slots.at[self.me], own_sem)
        own.start()
        own.wait()

    def finish(self, x_ref, spread_out, slots, send, recv):
        for d in range(1, self.n):
            landed(slots.at[self.back(d)], recv.at[d])
        for d in range(1, self.n):
            self.copy(d, x_ref, spread_out, slots, send, recv).wait_send()


def slot_product(a_ref, w_ref, dims):
    def partial(slot, cols):
        a = a_ref[:, slot].reshape(-1, a_ref.shape[3])
        return dotf(a, w_ref[:, cols] if dims == NN else w_ref[cols, :], dims)

    return partial


def row_blocks(ref, block, body):
    per = ref.shape[1] // block

    def one(i, carry):
        here = pl.ds(pl.multiple_of(lax.rem(i, per) * block, block), block)
        body(lax.div(i, per), here)
        return carry

    lax.fori_loop(0, 2 * per, one, 0)


def dot_scatter_kernel(fs, dims, beside, then, *refs):
    hbm, refs = refs[:2], refs[2:]
    if beside:
        later, refs = refs[:2], refs[2:]
    if then:
        (base_ref, factor_ref), refs = refs[:2], refs[2:]
    outs, refs = refs[: 2 if then == "norm" else 1], refs[2 if then == "norm" else 1 :]
    if beside:
        g_ref, refs = refs[0], refs[1:]
    staged, refs = Staged(hbm, refs[:4]), refs[4:]
    if beside:
        later, refs = Staged(later, refs[:4]), refs[4:]
        l_ref, r_ref = later.held
    sum_ref = outs[0]
    if then:
        sum_ref, refs = refs[0], refs[1:]
    plane = Plane(fs)
    plane.barrier()
    staged.wait()
    partial = slot_product(*staged.held, dims)
    actions = scatter_actions(plane, partial, sum_ref.shape[2], sum_ref, refs)
    first = 2 * fs
    for action in actions[:first]:
        action()
    if beside:
        later.wait()
        block = 256

        def one(i, carry):
            here = pl.ds(pl.multiple_of(i * block, block), block)
            g_ref[here, :] = dotf(l_ref[:, here].T, r_ref[...]).astype(g_ref.dtype)
            return carry

        steps = l_ref.shape[1] // block
        lax.fori_loop(0, steps // 2, one, 0)
    middle = first + len(actions[first:-1]) - 2
    for action in actions[first:middle]:
        action()
    if beside:
        lax.fori_loop(steps // 2, steps, one, 0)
    for action in actions[middle:]:
        action()

    def normed(p, here):
        hidden = base_ref[p, here, :].astype(jnp.float32) + sum_ref[p, here, :]
        outs[0][p, here, :] = hidden
        scale = lax.rsqrt(jnp.mean(hidden * hidden, axis=1, keepdims=True) + EPSILON)
        outs[1][p, here, :] = (hidden * scale * factor_ref[...]).astype(jnp.bfloat16)

    def result(p, here):
        hidden = base_ref[p, here, :] + sum_ref[p, here, :]
        outs[0][p, here, :] = (hidden * factor_ref[p, here, :]).astype(jnp.bfloat16)

    if then:
        row_blocks(sum_ref, 32, normed if then == "norm" else result)


def plane_dot_scatter(
    a, w, dims, seqs, collective_id, beside=None, norm=None, result=None
):
    fs = lax.axis_size("fsdp")
    a = a.reshape(seqs, 2 * fs, -1, a.shape[1])
    b = a.shape[2]
    width = w.shape[1] if dims == NN else w.shape[0]
    own = (seqs, b, width)
    args = [a, w]
    in_specs = [anywhere()] * 2
    scratch = Staged.scratch(a, w)
    out_shape = [jax.ShapeDtypeStruct(own, jnp.bfloat16 if result else jnp.float32)]
    if beside is not None:
        args += beside
        in_specs += [anywhere()] * 2
        scratch += Staged.scratch(*beside)
    if norm is not None:
        args += [norm[0].reshape(own), norm[1]]
        out_shape.append(jax.ShapeDtypeStruct(own, jnp.bfloat16))
    if result is not None:
        args += [result[0].reshape(own), result[1].reshape(seqs, b, 1)]
    if norm is not None or result is not None:
        in_specs += [vmem()] * 2
        scratch.append(pltpu.VMEM(own, jnp.float32))
    if beside is not None:
        out_shape.append(
            jax.ShapeDtypeStruct((beside[0].shape[1], beside[1].shape[1]), jnp.bfloat16)
        )
    then = "norm" if norm is not None else "result" if result is not None else ""
    out = pl.pallas_call(
        functools.partial(dot_scatter_kernel, fs, dims, beside is not None, then),
        out_shape=out_shape,
        in_specs=in_specs,
        out_specs=[vmem()] * len(out_shape),
        scratch_shapes=scratch + scatter_scratch(fs, b, width),
        compiler_params=plane_params(collective_id, 62),
        cost_estimate=estimate(45),
        name="plane_dot_scatter",
    )(*args)
    out = [out[0].reshape(-1, width)] + list(out[1:])
    if norm is not None:
        out[1] = out[1].reshape(-1, width)
    return out if len(out) > 1 else out[0]


def norm_turn_kernel(
    fs, a_hbm, w_hbm, hid_ref, cot_ref, gain_ref, wo_ref, o_ref, y_ref, wg_ref, grad_ref, gsum_ref,
    a_ref, w_ref, a_sem, w_sem, sum_ref, x_ref, buf_ref, acc_ref, *scratch
):
    staged = Staged((a_hbm, w_hbm), (a_ref, w_ref, a_sem, w_sem))
    plane = Plane(fs)
    plane.barrier()
    acc_ref[...] = jnp.zeros_like(acc_ref)
    staged.wait()
    b, width = x_ref.shape[1:]
    partial = slot_product(a_ref, w_ref, NT)
    for action in scatter_actions(plane, partial, width, sum_ref, scratch[4:]):
        action()
    block = 32
    tile = wide_tile(width)
    gain = gain_ref[...]

    def turn(i, total):
        p, at = lax.div(i, b // block), pl.multiple_of(lax.rem(i, b // block) * block, block)
        here = pl.ds(at, block)
        grad, hidden = sum_ref[p, here, :], hid_ref[p, here, :]
        scale = lax.rsqrt(jnp.mean(hidden * hidden, axis=1, keepdims=True) + EPSILON)
        weighted = grad * gain
        inner = jnp.mean(weighted * hidden, axis=1, keepdims=True)
        back = scale * (weighted - hidden * scale * scale * inner)
        back = cot_ref[p, here, :].astype(jnp.float32) + back
        grad_ref[p, here, :] = back
        x_ref[p, here, :] = back.astype(jnp.bfloat16)
        return total + grad * hidden * scale

    total = lax.fori_loop(
        0, 2 * (b // block), turn, jnp.zeros((block, width), jnp.float32)
    )
    gsum_ref[...] = jnp.sum(total, axis=0, keepdims=True)

    def consume(p, slot):
        two = pl.ds(slot, 2)
        rows = buf_ref[p, two].reshape(2 * b, width)
        y = dotf(rows, wo_ref[...], NT)
        y_ref[p, two] = y.astype(y_ref.dtype).reshape(2, b, -1)
        o_t = o_ref[p, two].reshape(2 * b, -1).T

        def grad(j, carry):
            cols = pl.ds(pl.multiple_of(j * tile, tile), tile)
            acc_ref[:, cols] += dotf(o_t, buf_ref[p, two, :, cols].reshape(2 * b, tile))
            return carry

        lax.fori_loop(0, width // tile, grad, 0)

    run_gather(plane, x_ref, buf_ref, scratch[:4], consume)
    wg_ref[...] = acc_ref[...].astype(wg_ref.dtype)


def norm_turn(a, w, hidden, cot, gain, w_o, attended, seqs, collective_id):
    fs = lax.axis_size("fsdp")
    lead = (seqs, 2 * fs, a.shape[0] // (2 * fs * seqs))
    b, width = lead[2], hidden.shape[1]
    own = (seqs, b, width)
    a = a.reshape(lead + (-1,))
    attended = attended.reshape(lead + (-1,))
    k = attended.shape[3]
    y, wg, grad, gsum = pl.pallas_call(
        functools.partial(norm_turn_kernel, fs),
        out_shape=[
            jax.ShapeDtypeStruct(lead + (k,), jnp.bfloat16),
            jax.ShapeDtypeStruct((k, width), jnp.bfloat16),
            jax.ShapeDtypeStruct(own, jnp.float32),
            jax.ShapeDtypeStruct((1, width), jnp.float32),
        ],
        in_specs=[anywhere()] * 2 + [vmem()] * 5,
        out_specs=[vmem()] * 4,
        scratch_shapes=Staged.scratch(a, w)
        + [
            pltpu.VMEM(own, jnp.float32),
            pltpu.VMEM(own, jnp.bfloat16),
            pltpu.VMEM(lead + (width,), jnp.bfloat16),
            pltpu.VMEM((k, width), jnp.float32),
        ]
        + gather_sems(fs)
        + scatter_scratch(fs, b, width),
        compiler_params=plane_params(collective_id, 62),
        cost_estimate=estimate(45),
        name="norm_turn",
    )(a, w, hidden.reshape(own), cot.reshape(own), gain, w_o, attended)
    return y.reshape(-1, k), wg, grad.reshape(-1, width), gsum[0]


GELU_C = math.sqrt(2.0 / math.pi)


def ffn_kernel(x_ref, gh_ref, g_ref, wgu_ref, h_ref, ggu_ref, wg_ref, acc_ref):
    step = pl.program_id(0)
    ff = h_ref.shape[1]

    @pl.when(step == 0)
    def _():
        acc_ref[...] = jnp.zeros_like(acc_ref)

    gate = dotf(x_ref[...], wgu_ref[:, :ff])
    up = dotf(x_ref[...], wgu_ref[:, ff:])
    grad_hidden = gh_ref[...]
    square = gate * gate
    tanh = jnp.tanh(GELU_C * gate * (1.0 + 0.044715 * square))
    half = 0.5 * (1.0 + tanh)
    act = gate * half
    slope = half + (0.5 * GELU_C) * gate * (1.0 - tanh * tanh) * (1.0 + 0.134145 * square)
    hidden = (act * up).astype(jnp.bfloat16)
    h_ref[...] = hidden
    ggu_ref[:, :ff] = (grad_hidden * up * slope).astype(jnp.bfloat16)
    ggu_ref[:, ff:] = (grad_hidden * act).astype(jnp.bfloat16)
    acc_ref[...] += dotf(hidden.T, g_ref[...])

    @pl.when(step == pl.num_programs(0) - 1)
    def _():
        wg_ref[...] = acc_ref[...].astype(jnp.bfloat16)


def ffn(x, grad_hidden, grad, w_gu):
    rows, width = x.shape
    ff = grad_hidden.shape[1]
    block = math.gcd(rows, 512)

    def blocks(columns):
        return pl.BlockSpec((block, columns), lambda i: (i, 0))

    def held(shape):
        return pl.BlockSpec(shape, lambda i: (0, 0), pipeline_mode=pl.Buffered(1))

    return pl.pallas_call(
        ffn_kernel,
        grid=(rows // block,),
        out_shape=[
            jax.ShapeDtypeStruct((rows, ff), jnp.bfloat16),
            jax.ShapeDtypeStruct((rows, 2 * ff), jnp.bfloat16),
            jax.ShapeDtypeStruct((ff, width), jnp.bfloat16),
        ],
        in_specs=[blocks(width), blocks(ff), blocks(width), held(w_gu.shape)],
        out_specs=[blocks(ff), blocks(2 * ff), pl.BlockSpec((ff, width), lambda i: (0, 0))],
        scratch_shapes=[pltpu.VMEM((ff, width), jnp.float32)],
        compiler_params=pltpu.CompilerParams(
            dimension_semantics=("arbitrary",), vmem_limit_bytes=60 * MIB
        ),
        cost_estimate=estimate(30),
        name="ffn",
    )(x, grad_hidden, grad, w_gu)

def column_runs(sizes, per_device, total, natural):
    fs, zs, cs = sizes
    if not natural:
        size = total // (fs * cs)
        return [(t * size, t, 0, size) for t in range(fs * cs)]
    return [
        (((f * zs + z) * cs + c) * per_device, f * cs + c, z * per_device, per_device)
        for f in range(fs) for z in range(zs) for c in range(cs)
    ]


def start_kernel(
    sizes, runs, small_ref, q_ref, k_ref, v_ref, gate_ref, up_ref, tok_ref, cot_ref, o_ref, d_ref,
    small_out, wqkv_ref, ggu_ref, x_ref, g_ref, o_out, d_out,
    slots, qkv_ref, gu_ref, s_send, s_recv, own_sem, q_send, q_recv, g_send, g_recv,
    line_send, line_recv, *swap_scratch,
):
    fs, zs, cs = sizes
    f, z, c = (lax.axis_index(a) for a in ("fsdp", "z", "core"))
    me = f * cs + c
    devices = fs * cs
    rows = qkv_ref.shape[1]
    everyone = Everyone(sizes)
    everyone.greet()

    def split(pieces_ref, parts, run):
        size = pieces_ref.shape[2] // len(parts)
        for i, part in enumerate(parts):
            for at, device, start, count in run:
                here = part[:, at : at + count].astype(jnp.bfloat16)
                pieces_ref[device, :, i * size + start : i * size + start + count] = here

    split(qkv_ref, (q_ref, k_ref, v_ref), runs[1])
    half = len(swap_scratch) // 2
    swaps = [
        Swap(tok_ref, x_ref, swap_scratch[:half]), Swap(cot_ref, g_ref, swap_scratch[half:])
    ]
    everyone.met()
    everyone.begin(small_ref, False, slots, s_send, s_recv, own_sem.at[0])

    def block(out_ref, index, lead):
        at = pl.ds(pl.multiple_of(lax.rem(index, cs) * rows, rows), rows)
        if lead is None:
            return out_ref.at[lax.div(index, cs), at]
        return out_ref.at[lax.div(index, cs), lead, at]

    def spread_copy(d, src_ref, out_ref, lead, send, recv):
        to = lax.rem(me + d, devices)
        return remote_copy(
            src_ref.at[to], block(out_ref, me, lead), send.at[d], recv.at[d],
            (lax.div(to, cs), z, lax.rem(to, cs)),
        )

    own_qkv = pltpu.make_async_copy(qkv_ref.at[me], block(wqkv_ref, me, z), own_sem.at[1])
    own_gu = pltpu.make_async_copy(gu_ref.at[me], block(ggu_ref, me, None), own_sem.at[2])
    own_qkv.start()
    for d in range(1, devices):
        spread_copy(d, qkv_ref, wqkv_ref, z, q_send, q_recv).start()
    swaps[0].start()
    split(gu_ref, (gate_ref, up_ref), runs[0])
    own_gu.start()
    o_out[...] = o_ref[...].astype(jnp.bfloat16)
    d_out[...] = d_ref[...].astype(jnp.bfloat16)
    def chip(p):
        return lax.rem(f + p, fs)

    def line(step, way, p):
        source = lax.rem(z - way * step + zs, zs)
        to = lax.rem(z + way + zs, zs)
        k = 0 if way > 0 else 1
        ref = wqkv_ref.at[chip(p), source]
        return remote_copy(
            ref, ref, line_send.at[k, step, p], line_recv.at[k, step, p], (f, to, c)
        )

    def sends(step, way):
        if way > 0:
            return (z >= step) & (z < zs - 1)
        return (z < zs - step) & (z > 0)

    def arrives(step, way):
        return (z > step) if way > 0 else (z < zs - 1 - step)

    def arrive(step, way, p):
        k = 0 if way > 0 else 1
        source = lax.rem(z - way * (step + 1) + zs, zs)
        landed(wqkv_ref.at[chip(p), source], line_recv.at[k, step, p])

    def spread_arrive(df, dc):
        index = chip(df) * cs + lax.rem(c + dc, cs)
        d = lax.rem(me - index + devices, devices)
        landed(block(wqkv_ref, index, z), q_recv.at[d])

    for step in range(zs - 1):
        for p in range(fs):
            if step == 0:
                if p == 0:
                    own_qkv.wait()
                for dc in range(cs):
                    if p or dc:
                        spread_arrive(p, dc)
            for way in (1, -1):
                if step:

                    @pl.when(arrives(step - 1, way))
                    def _(step=step, way=way, p=p):
                        arrive(step - 1, way, p)

                @pl.when(sends(step, way))
                def _(step=step, way=way, p=p):
                    line(step, way, p).start()

        if step == 0:
            swaps[0].hand_on()
            swaps[1].start()
            for d in range(1, devices):
                spread_copy(d, gu_ref, ggu_ref, None, g_send, g_recv).start()
        if step == 1:
            swaps[1].hand_on()
    for p in range(fs):
        for way in (1, -1):

            @pl.when(arrives(zs - 2, way))
            def _(way=way, p=p):
                arrive(zs - 2, way, p)

    everyone.finish(small_ref, False, slots, s_send, s_recv)
    small_out[...] = slots[...]
    own_gu.wait()
    for d in range(1, devices):
        landed(block(ggu_ref, lax.rem(me + devices - d, devices), None), g_recv.at[d])
    for d in range(1, devices):
        spread_copy(d, qkv_ref, wqkv_ref, z, q_send, q_recv).wait_send()
        spread_copy(d, gu_ref, ggu_ref, None, g_send, g_recv).wait_send()
    for step in range(zs - 1):
        for p in range(fs):
            for way in (1, -1):

                @pl.when(sends(step, way))
                def _(step=step, way=way, p=p):
                    line(step, way, p).wait_send()

    for swap in swaps:
        swap.close()


def start(small, qkv, gu, tokens, cotangent, own_o, own_d, runs, collective_id):
    sizes = tuple(lax.axis_size(a) for a in ("fsdp", "z", "core"))
    fs, zs, cs = sizes
    n = math.prod(sizes)
    devices = fs * cs
    rows = qkv[0].shape[0]
    qkv_cols = sum(w.shape[1] for w in qkv) // devices
    gu_cols = sum(w.shape[1] for w in gu) // devices
    dma = pltpu.SemaphoreType.DMA
    return pl.pallas_call(
        functools.partial(start_kernel, sizes, runs),
        out_shape=[
            jax.ShapeDtypeStruct((n, 8, 128), jnp.float32),
            jax.ShapeDtypeStruct((fs, zs, cs * rows, qkv_cols), jnp.bfloat16),
            jax.ShapeDtypeStruct((fs, cs * rows, gu_cols), jnp.bfloat16),
            jax.ShapeDtypeStruct(tokens.shape, tokens.dtype),
            jax.ShapeDtypeStruct(cotangent.shape, cotangent.dtype),
            jax.ShapeDtypeStruct(own_o.shape, jnp.bfloat16),
            jax.ShapeDtypeStruct(own_d.shape, jnp.bfloat16),
        ],
        in_specs=[vmem()] * 10,
        out_specs=[vmem()] + [anywhere()] * 4 + [vmem()] * 2,
        scratch_shapes=[
            pltpu.VMEM((n, 8, 128), jnp.float32),
            pltpu.VMEM((devices, rows, qkv_cols), jnp.bfloat16),
            pltpu.VMEM((devices, rows, gu_cols), jnp.bfloat16),
            dma((n,)), dma((n,)), dma((3,)),
            dma((devices,)), dma((devices,)), dma((devices,)), dma((devices,)),
            dma((2, zs, fs)), dma((2, zs, fs)),
        ]
        + Swap.scratch(fs, *tokens.shape) * 2,
        compiler_params=plane_params(collective_id),
        cost_estimate=estimate(120),
        name="start",
    )(small, *qkv, *gu, tokens, cotangent, own_o, own_d)


def finish_kernel(
    sizes, runs, small_ref, g_ref, qkv_ref, gu_ref, small_out, out_ref, gate_ref, up_ref,
    q_ref, k_ref, v_ref, slots, got_qkv, send, recv, own_sem, back_send, back_recv, back_sem,
    *swap_scratch
):
    everyone = Everyone(sizes)
    everyone.greet()
    back = Back(sizes, qkv_ref, got_qkv, (back_send, back_recv, back_sem))
    swap = Swap(g_ref, out_ref, swap_scratch)
    everyone.met()
    swap.start()
    everyone.begin(small_ref, True, slots, send, recv, own_sem)
    back.start()
    swap.hand_on()

    def join(got_ref, pieces, run):
        size = got_ref.shape[2] // len(pieces)
        for i, piece in enumerate(pieces):
            for to, device, start, count in run:
                part = got_ref[device, :, i * size + start : i * size + start + count]
                piece[:, to : to + count] = part.astype(jnp.float32)

    join(gu_ref, (gate_ref, up_ref), runs[0])
    back.arrived()
    join(got_qkv, (q_ref, k_ref, v_ref), runs[1])
    everyone.finish(small_ref, True, slots, send, recv)
    small_out[...] = jnp.sum(slots[...], axis=0)
    back.close()
    swap.close()


def finish(small, grad, sum_qkv, got_gu, runs, columns, collective_id):
    sizes = tuple(lax.axis_size(a) for a in ("fsdp", "z", "core"))
    fs, zs, cs = sizes
    n = math.prod(sizes)
    devices = fs * cs
    dma = pltpu.SemaphoreType.DMA
    sum_qkv = sum_qkv.reshape(devices, -1, sum_qkv.shape[2])
    wide = [jax.ShapeDtypeStruct((sum_qkv.shape[1], k), jnp.float32) for k in columns]
    return pl.pallas_call(
        functools.partial(finish_kernel, sizes, runs),
        out_shape=[
            jax.ShapeDtypeStruct((8, 128), small.dtype),
            jax.ShapeDtypeStruct(grad.shape, grad.dtype),
        ]
        + wide,
        in_specs=[vmem()] * 4,
        out_specs=[vmem(), anywhere()] + [vmem()] * len(wide),
        scratch_shapes=[
            pltpu.VMEM((n, 8, 128), small.dtype),
            pltpu.VMEM(sum_qkv.shape, jnp.bfloat16),
            dma((n,)), dma((n,)), dma,
        ]
        + Back.scratch(devices)
        + Swap.scratch(fs, *grad.shape),
        compiler_params=plane_params(collective_id),
        cost_estimate=estimate(45),
        name="finish",
    )(small, grad, sum_qkv, got_gu)


def to_tiles(x):
    return jnp.pad(x, ((0, 0), (0, 1024 - x.shape[1]))).reshape(-1, 8, 128)

from jax.sharding import Mesh
from jax.sharding import PartitionSpec as P

H = 32
HIGHEST = lax.Precision.HIGHEST
BF = jnp.bfloat16
F32 = jnp.float32
TP = ("fsdp", "core")
ALL = ("fsdp", "z", "core")


def rms_scale(values):
    return lax.rsqrt(jnp.mean(values * values, axis=1, keepdims=True) + EPSILON)


def norm_back(grad_normed, values, row_scale, gain_row):
    weighted = grad_normed * gain_row
    inner_mean = jnp.mean(weighted * values, axis=1, keepdims=True)
    return row_scale * (weighted - values * row_scale * row_scale * inner_mean)


class Layout:
    def __init__(self, per_device, head_dim):
        self.f, self.z, self.c = (lax.axis_size(a) for a in ALL)
        self.natural = per_device % head_dim == 0
        self.per_device = per_device

    def split(self, w):
        rows, cols = w.shape
        if self.natural:
            w = w.reshape(rows, self.f, self.z, self.c, self.per_device)
            w = w.transpose(1, 3, 0, 2, 4)
        else:
            w = w.reshape(rows, self.f, self.c, -1).transpose(1, 2, 0, 3)
        return w.reshape(self.f * self.c, rows, -1)

    def join(self, w):
        devices, rows, cols = w.shape
        if self.natural:
            w = w.reshape(self.f, self.c, rows, self.z, self.per_device)
            w = w.transpose(2, 0, 3, 1, 4)
        else:
            w = w.reshape(self.f, self.c, rows, cols).transpose(2, 0, 1, 3)
        return w.reshape(rows, -1)

    def gather(self, w):
        if self.natural:
            return lax.all_gather(w, "z", axis=0, tiled=True)
        both = lax.all_gather(w, ("z", "core"), axis=0, tiled=True)
        size = both.shape[0] // self.c
        return lax.dynamic_slice_in_dim(both, lax.axis_index("core") * size, size, 0)

    def whole(self, g):
        if self.natural:
            return g
        size = g.shape[0]
        both = jnp.zeros((size * self.c, g.shape[1]), g.dtype)
        both = lax.dynamic_update_slice_in_dim(both, g, lax.axis_index("core") * size, 0)
        both = lax.psum(both, "core").reshape(self.z, self.c, -1, g.shape[1])
        mine = lax.dynamic_index_in_dim(both, lax.axis_index("core"), 1, keepdims=False)
        return mine.reshape(-1, g.shape[1])

    def scatter(self, g):
        return lax.psum_scatter(g, "z", scatter_dimension=0, tiled=True)


def over_z(got):
    f, cr, cols = got.shape
    full = lax.all_gather(got, "z", axis=1, tiled=True)
    return full.reshape(-1, cols)


def reduce_z(grad):
    f, z = lax.axis_size("fsdp"), lax.axis_size("z")
    return lax.psum_scatter(
        grad.reshape(f, grad.shape[0] // f, -1), "z", scatter_dimension=1, tiled=True
    )


def shards(
    tokens, cotangent, lengths, buckets, norm1_gain, rel_bias,
    w_query, w_key, w_value, w_attn_out, norm2_gain, w_gate, w_up, w_down,
):
    fs, zs, cs = (lax.axis_size(a) for a in ALL)
    seqs, block_len, width = tokens.shape
    rows = seqs * block_len
    length = block_len * fs * cs
    head_dim = w_query.shape[1] // H
    heads = H // (fs * cs)
    buckets_n = rel_bias.shape[0] * fs * zs * cs // H
    head_cols = Layout(w_attn_out.shape[0], head_dim)
    ff_cols = Layout(w_down.shape[0], w_down.shape[0])

    own_small = jnp.concatenate([norm1_gain, norm2_gain, rel_bias]).astype(BF).astype(F32)
    own_small = jnp.concatenate([own_small, lengths.astype(F32)])
    sizes = (fs, zs, cs)
    runs = (
        column_runs(sizes, ff_cols.per_device, w_gate.shape[1], True),
        column_runs(sizes, head_cols.per_device, w_query.shape[1], head_cols.natural),
    )
    small, w_qkv, got_gu, x_in, cot, own_o, own_d = start(
        to_tiles(own_small[None]), (w_query, w_key, w_value), (w_gate, w_up),
        tokens.reshape(rows, width), cotangent.reshape(rows, width), w_attn_out, w_down, runs, 9,
    )
    w_qkv = w_qkv.reshape(width, -1)
    w_o = head_cols.gather(own_o)
    w_gu = over_z(got_gu)
    w_d = ff_cols.gather(own_d)
    small = small.reshape(-1, 1024)[:, : own_small.shape[0]]
    lens = lax.dynamic_index_in_dim(
        small[:, -seqs:], lax.axis_index("z") * zs * cs, 0, keepdims=False
    ).astype(jnp.int32)
    g = norm1_gain.shape[0]
    gain_one = small[:, :g].reshape(1, -1).astype(F32)
    gain_two = small[:, g : 2 * g].reshape(1, -1).astype(F32)
    table = small[:, 2 * g : -seqs].reshape(1, -1).astype(F32).reshape(H, buckets_n)
    plane_index = lax.axis_index("fsdp") * cs + lax.axis_index("core")
    table = head_cols.split(jnp.repeat(table.T, head_dim, axis=1))[:, :, ::head_dim]
    table = lax.dynamic_index_in_dim(table, plane_index, 0, keepdims=False).T
    one_hot = (buckets[:, None] == jnp.arange(buckets_n, dtype=jnp.int32)[None, :]).astype(F32)
    one_hot = jnp.pad(one_hot, ((0, 1), (0, 0)))
    offset_bias = jnp.dot(table, one_hot.T, precision=HIGHEST)

    ff = w_d.shape[0]

    positions = plane_index * block_len + jnp.arange(block_len, dtype=jnp.int32)
    valid = (positions[None, :] < lens[:, None]).astype(F32).reshape(rows, 1)

    x = x_in.reshape(rows, width).astype(F32)
    scale_one = rms_scale(x)
    grad_rows = cot.reshape(rows, width).astype(F32) * valid

    normed = (x * scale_one * gain_one).astype(BF)
    normed, qkv = plane_gather_dot(normed, w_qkv, NN, seqs, 2)
    branch = grad_rows.astype(BF)
    attended, lse, grad_branch = attn_fwd(
        qkv, offset_bias, lens, heads, head_dim, seqs, branch, 1
    )
    hidden_one, normed_two = plane_dot_scatter(
        attended, w_o, NN, seqs, 3, norm=(x_in, gain_two)
    )
    normed_two, grad_hidden = plane_gather_dot(
        normed_two, w_d, NT, seqs, 4, other=grad_branch, dtype=F32
    )
    hidden_ff, grad_gu, grad_w_down = ffn(normed_two, grad_hidden, grad_branch, w_gu)
    sum_down = ff_cols.scatter(grad_w_down)
    last = (hidden_one, valid)
    if fs <= 4:
        result, grad_w_gu = plane_dot_scatter(
            hidden_ff, w_d, NN, seqs, 7, beside=(normed_two, grad_gu), result=last
        )
    else:
        result = plane_dot_scatter(hidden_ff, w_d, NN, seqs, 7, result=last)
        grad_w_gu = jnp.einsum("rd,rf->df", normed_two, grad_gu, preferred_element_type=F32)
        grad_w_gu = grad_w_gu.astype(BF)
    grad_w_gu, sum_down, grad_gu = lax.optimization_barrier((grad_w_gu, sum_down, grad_gu))
    sum_gu = reduce_z(grad_w_gu)
    if fs <= 4:
        grad_attended, grad_w_o, grad_hidden_one, gain_two_part = norm_turn(
            grad_gu, w_gu, hidden_one, branch, gain_two, w_o, attended, seqs, 5
        )
    else:
        grad_normed_two = plane_dot_scatter(grad_gu, w_gu, NT, seqs, 5)
        scale_two = rms_scale(hidden_one)
        gain_two_part = jnp.sum(grad_normed_two * hidden_one * scale_two, axis=0)
        grad_hidden_one = grad_rows + norm_back(grad_normed_two, hidden_one, scale_two, gain_two)
        grad_attn, grad_attended = plane_gather_dot(
            grad_hidden_one.astype(BF), w_o, NT, seqs, 6
        )
        grad_w_o = jnp.einsum("rk,rd->kd", attended, grad_attn, preferred_element_type=F32)
        grad_w_o = grad_w_o.astype(BF)
    dqkv, grad_offset, grad_w_qkv, output, sum_o, got_gu = attn_bwd(
        qkv, grad_attended, lse, offset_bias, lens, heads, head_dim, seqs, normed,
        result, head_cols.whole(grad_w_o), sum_gu, 11,
    )
    output = output.reshape(seqs, block_len, width)
    sum_qkv = reduce_z(grad_w_qkv)
    grad_normed = plane_dot_scatter(dqkv, w_qkv, NT, seqs, 8)
    gain_one_part = jnp.sum(grad_normed * x * scale_one, axis=0)
    grad_x = grad_hidden_one + norm_back(grad_normed, x, scale_one, gain_one)

    grad_table = jnp.dot(grad_offset, one_hot, precision=HIGHEST)
    bias_all = jnp.zeros((fs * cs, heads, buckets_n), F32)
    bias_all = lax.dynamic_update_index_in_dim(bias_all, grad_table, plane_index, 0)
    bias_all = jnp.repeat(bias_all.transpose(0, 2, 1), head_dim, axis=2)
    bias_all = head_cols.join(bias_all)[:, ::head_dim].T.reshape(fs * zs * cs, -1)
    small_grad = jnp.concatenate(
        [
            gain_one_part.reshape(fs * zs * cs, -1),
            gain_two_part.reshape(fs * zs * cs, -1),
            bias_all,
        ],
        axis=1,
    )
    columns = (w_gate.shape[1],) * 2 + (w_query.shape[1],) * 3
    small_sum, grad_tokens, grad_gate_w, grad_up_w, grad_q_w, grad_k_w, grad_v_w = finish(
        to_tiles(small_grad), grad_x.astype(BF), sum_qkv, got_gu, runs, columns, 10
    )
    grad_tokens = grad_tokens.reshape(seqs, block_len, width)
    small_grad = small_sum.reshape(-1)[: small_grad.shape[1]]
    return (
        output,
        grad_tokens,
        small_grad[:g],
        small_grad[2 * g :],
        grad_q_w,
        grad_k_w,
        grad_v_w,
        sum_o,
        small_grad[g : 2 * g],
        grad_gate_w,
        grad_up_w,
        sum_down.astype(F32),
    )


def solution(mesh):
    fs, ctx = mesh.shape["fsdp"], mesh.shape["ctx"]
    mesh3 = Mesh(mesh.devices.reshape(fs, ctx // 2, 2), ALL)
    act = P("fsdp", ("z", "core"), None)
    vec, mat = P(ALL), P(ALL, None)
    in_specs = (act, act, P("fsdp"), P(), vec, vec, mat, mat, mat, mat, vec, mat, mat, mat)
    out_specs = (act, act, vec, vec, mat, mat, mat, mat, vec, mat, mat, mat)
    return jax.shard_map(shards, mesh=mesh3, in_specs=in_specs, out_specs=out_specs, check_vma=False)
```
